128 devices in a mesh: section: 2 (over y_hi), dp: 4 (over x), seq: 16 (over z, y_lo, core).
Axes of the slice: x: 4, y: 4 (y_hi: 2, y_lo: 2; y = y_hi * 2 + y_lo), z: 4, core: 2. Of those that a mesh axis runs over, the one named last changes fastest.
Arguments:
- trajectory: bfloat16 [5, 4, 16, 128, 128], P(None, None, 'seq', 'dp'), may hold values from -12 to 12
- block_input: bfloat16 [4, 4096, 3072], P('dp', 'seq'), may hold values from -6 to 6
- chosen: int32 [4], replicated, may hold values from 0 to 3
- lengths: int32 [4], replicated, may hold values from 1024 to 4096, as said below
- rewards: int32 [64], replicated, may hold values from 0 to 9
- prompt_group_index: int32 [64], replicated, may hold values from 0 to 3, as said below
- rollout_log_probability: float32 [4], replicated, may hold values from -0.95 to -0.5
- timestep_norm_shift: float32 [4, 2, 3072], replicated, may hold values from -2.5 to 2.5
- patch_input_weight: bfloat16 [64, 3072], replicated, may hold values from -0.75 to 0.75
- frozen_query_matrix: bfloat16 [3072, 1536], P(None, 'section'), may hold values from -1 to 1
- frozen_key_matrix: bfloat16 [3072, 1536], P(None, 'section'), may hold values from -1 to 1
- frozen_value_matrix: bfloat16 [3072, 1536], P(None, 'section'), may hold values from -0.109375 to 0.109375
- velocity_output_weight: bfloat16 [1536, 64], P('section'), may hold values from -0.15625 to 0.15625
- adapter_down_factor: float32 [3072, 128], replicated, may hold values from -6 to 6
- adapter_up_factor: float32 [128, 1536], P(None, 'section'), may hold values from -6 to 6
Outputs:
- revised_down_factor: float32 [3072, 128], replicated
- revised_up_factor: float32 [128, 1536], P(None, 'section')
- ratios: float32 [4], P('dp')
The draws below stay inside these ranges and needn't reach their ends.
Inputs may be any that keep to these rules, and one draw needn't show every extreme that they name: `lengths`: the longest trained clip has all 4096 tokens live. `prompt_group_index`: each of the 4 prompts names exactly 16 clips.
All inputs are finite; a program needn't handle non-finite values.
Results may differ from the reference program's by a relative error of at most 0.015.
Values may be sent and summed in bfloat16 or wider, within the bound.
A program may use at most 192 MiB of HBM per device.

```python
import math
import jax
import jax.numpy as jnp
from jax import lax

MODEL_WIDTH = 3072
HEADS_W = 12
HD = 128
PROJECTION_WIDTH = 1536
ADAPTER_RANK = 128
PATCH = 64
STEPS = 4
GROUP = 16
GROUPS = 4
ALL_CLIPS = 64
PAIR_DEV = 128
SEQ_BLOCKS = 16
TOKENS = 4096
CLIPS = 4


noise_level = 0.8


def draw_frozen_query_matrix(key, part):
    key = jax.random.fold_in(key, 21)
    values_all = jax.random.normal(key, (MODEL_WIDTH, PROJECTION_WIDTH), jnp.float32) / math.sqrt(MODEL_WIDTH)
    return jnp.clip(values_all, -1.0, 1.0).astype(jnp.bfloat16)


def draw_frozen_key_matrix(key, part):
    key = jax.random.fold_in(key, 22)
    own_draw = jax.random.normal(key, (MODEL_WIDTH, PROJECTION_WIDTH), jnp.float32) / math.sqrt(MODEL_WIDTH)
    values_all = own_draw
    return jnp.clip(values_all, -1.0, 1.0).astype(jnp.bfloat16)


def draw_trajectory(key, part):
    key = jax.random.fold_in(key, 11)
    grid_shape = (CLIPS, SEQ_BLOCKS, PAIR_DEV, 2 * PATCH)
    subkeys = jax.random.split(key, 2 * STEPS + 1)
    latent = jax.random.normal(subkeys[0], grid_shape, jnp.float32)
    frames = [latent]
    step_size = 1.0 / (STEPS + 1)
    for level_index in range(STEPS):
        spread = noise_level * math.sqrt(step_size * (1.0 - level_index * step_size))
        rollout_drift = jax.random.normal(subkeys[1 + 2 * level_index], grid_shape, jnp.float32)
        fresh_noise = jax.random.normal(subkeys[2 + 2 * level_index], grid_shape, jnp.float32)
        latent = latent - step_size * rollout_drift + spread * fresh_noise
        frames.append(latent)
    return jnp.clip(jnp.stack(frames), -12.0, 12.0).astype(jnp.bfloat16)


def draw_lengths(key, part):
    key = jax.random.fold_in(key, 41)
    base_draw = jax.random.randint(jax.random.fold_in(key, 1), (CLIPS,), TOKENS // 4, TOKENS + 1)
    full_slot = jax.random.randint(jax.random.fold_in(key, 2), (), 0, CLIPS)
    return jnp.where(jnp.arange(CLIPS) == full_slot, TOKENS, base_draw).astype(jnp.int32)


def draw_prompt_group_index(key, part):
    key = jax.random.fold_in(key, 31)
    return (jax.random.permutation(key, ALL_CLIPS) // GROUP).astype(jnp.int32)


def set_ends(values, stream_key, smallest, top_value):
    index_at = [jax.random.randint(jax.random.fold_in(stream_key, axis), (), 0, length) for axis, length in enumerate(values.shape)]
    longest = values.shape.index(max(values.shape))
    neighbour = index_at[:longest] + [(index_at[longest] + 1) % values.shape[longest]] + index_at[longest + 1:]
    return values.at[tuple(index_at)].set(smallest).at[tuple(neighbour)].set(top_value)


def shard_levels(stream_key, shape, cuts, least, top_value):
    def one(dim, shards_of):
        steps = jax.random.uniform(jax.random.fold_in(jax.random.fold_in(stream_key, 6), dim), (shards_of,), jnp.float32, least / len(cuts), top_value / len(cuts))
        return jnp.repeat(jnp.exp(steps), shape[dim] // shards_of).reshape((-1,) + (1,) * (len(shape) - dim - 1))

    level = one(*cuts[0])
    for cut in cuts[1:]:
        level = level * one(*cut)
    return level


def noise(key, shape, deviation, bound, shards=(), kind=jnp.bfloat16):
    level = shard_levels(key, shape, shards, -0.22, 0.18) if shards else 1.0
    values = jax.random.normal(key, shape, jnp.float32) * deviation * level
    return jnp.minimum(jnp.maximum(values, -bound), bound).astype(kind)


def setup_inputs(seed: int = 0) -> dict:
    splits = jax.random.split(jax.random.key(seed), 16)
    trajectory = draw_trajectory(jax.random.fold_in(splits[15], 71), 0)
    block_input = noise(splits[1], (CLIPS, TOKENS, MODEL_WIDTH), 1.0, 6.0, ((0, 4), (1, 16)))
    chosen = set_ends(jax.random.randint(splits[2], (CLIPS,), 0, STEPS), jax.random.fold_in(splits[2], 1), 0, STEPS - 1).astype(jnp.int32)
    lengths = draw_lengths(jax.random.fold_in(splits[15], 71), 0)
    rewards = set_ends(jax.random.randint(splits[4], (ALL_CLIPS,), 0, 10), jax.random.fold_in(splits[4], 1), 0, 9).astype(jnp.int32)
    prompt_group_index = draw_prompt_group_index(jax.random.fold_in(splits[15], 71), 0)
    rollout_log_probability = jnp.clip(jax.random.uniform(splits[6], (CLIPS,), jnp.float32, -0.95, -0.5), -0.95, -0.5)
    timestep_norm_shift = noise(splits[7], (STEPS, 2, MODEL_WIDTH), 0.3, 2.5, (), jnp.float32)
    patch_input_weight = noise(splits[8], (PATCH, MODEL_WIDTH), PATCH ** -0.5, 0.75)
    frozen_query_matrix = draw_frozen_query_matrix(jax.random.fold_in(splits[15], 71), 0)
    frozen_key_matrix = draw_frozen_key_matrix(jax.random.fold_in(splits[15], 71), 0)
    frozen_value_matrix = noise(splits[11], (MODEL_WIDTH, PROJECTION_WIDTH), MODEL_WIDTH ** -0.5, 0.109375, ((1, 2),))
    velocity_output_weight = noise(splits[12], (PROJECTION_WIDTH, PATCH), PROJECTION_WIDTH ** -0.5, 0.15625, ((0, 2),))
    adapter_down_factor = noise(splits[13], (MODEL_WIDTH, ADAPTER_RANK), 1.0, 6.0, (), jnp.float32)
    adapter_up_factor = noise(splits[14], (ADAPTER_RANK, PROJECTION_WIDTH), 1.0, 6.0, ((1, 2),), jnp.float32)
    return dict(trajectory=trajectory, block_input=block_input, chosen=chosen, lengths=lengths, rewards=rewards, prompt_group_index=prompt_group_index, rollout_log_probability=rollout_log_probability, timestep_norm_shift=timestep_norm_shift, patch_input_weight=patch_input_weight, frozen_query_matrix=frozen_query_matrix, frozen_key_matrix=frozen_key_matrix, frozen_value_matrix=frozen_value_matrix, velocity_output_weight=velocity_output_weight, adapter_down_factor=adapter_down_factor, adapter_up_factor=adapter_up_factor)


noise_level = 0.8
clip_range = 0.2
step_length = 256.0
norm_eps = 1e-06
masked_score = -1e+30

def split_heads(tensor):
    return tensor.reshape(CLIPS, TOKENS, HEADS_W, HD).transpose(0, 2, 1, 3).reshape(CLIPS * HEADS_W, TOKENS, HD)

def merge_heads(tensor):
    return tensor.reshape(CLIPS, HEADS_W, TOKENS, HD).transpose(0, 2, 1, 3).reshape(CLIPS, TOKENS, HEADS_W * HD)

def head_scores(query_head, key_head, live_keys):
    scores = jnp.dot(query_head, key_head.T, preferred_element_type=jnp.float32) * (1.0 / math.sqrt(HD))
    return jnp.where(live_keys[None, :], scores, masked_score)

def forward_head(head_item):
    query_head, key_head, value_head, live_keys = head_item
    scores = head_scores(query_head, key_head, live_keys)
    row_peak = lax.optimization_barrier(jnp.max(scores, axis=1))
    exp_scores = jnp.where(live_keys[None, :], jnp.exp(scores - row_peak[:, None]), 0.0)
    totals = lax.optimization_barrier(jnp.sum(exp_scores, axis=1))
    weighted = jnp.dot(exp_scores.astype(jnp.bfloat16), value_head, preferred_element_type=jnp.float32)
    return (weighted / totals[:, None], row_peak, totals)

def backward_head(head_item):
    query_head, key_head, value_head, live_keys, grad_head, row_peak, totals, deltas = head_item
    scores = head_scores(query_head, key_head, live_keys)
    probabilities = jnp.where(live_keys[None, :], jnp.exp(scores - row_peak[:, None]) / totals[:, None], 0.0)
    grad_probs = jnp.dot(grad_head, value_head.T, preferred_element_type=jnp.float32)
    grad_scores = (probabilities * (grad_probs - deltas[:, None])).astype(jnp.bfloat16)
    return jnp.dot(grad_scores, key_head, preferred_element_type=jnp.float32) * (1.0 / math.sqrt(HD))

def advantages(rewards, prompt_group_index):
    member = (prompt_group_index[:, None] == jnp.arange(GROUPS)[None, :]).astype(jnp.float32)
    reward_values = rewards.astype(jnp.float32)
    group_mean = lax.optimization_barrier(jnp.sum(member * reward_values[:, None], axis=0)) / GROUP
    own_mean = lax.optimization_barrier(jnp.sum(member * group_mean[None, :], axis=1))
    centered = reward_values - own_mean
    group_var = lax.optimization_barrier(jnp.sum(member * (centered * centered)[:, None], axis=0)) / GROUP
    own_std = lax.optimization_barrier(jnp.sum(member * jnp.sqrt(group_var)[None, :], axis=1))
    return centered / (own_std + 1.0)

def clip_weight(advantage, ratios, clip_total):
    low_edge = 1.0 - clip_range
    high_edge = 1.0 + clip_range
    inside = (ratios >= low_edge) & (ratios <= high_edge)
    active = inside | (advantage > 0) & (ratios < low_edge) | (advantage < 0) & (ratios > high_edge)
    return jnp.where(active, -advantage * ratios / clip_total, 0.0)

def reference(trajectory, block_input, chosen, lengths, rewards, prompt_group_index, rollout_log_probability, timestep_norm_shift, patch_input_weight, frozen_query_matrix, frozen_key_matrix, frozen_value_matrix, velocity_output_weight, adapter_down_factor, adapter_up_factor):
    levels = jnp.arange(STEPS + 1)
    pick_now = (levels[:, None] == chosen[None, :])[:, :, None, None, None]
    pick_next = (levels[:, None] == chosen[None, :] + 1)[:, :, None, None, None]
    zero_frame = jnp.zeros((), trajectory.dtype)
    current = lax.optimization_barrier(jnp.sum(jnp.where(pick_now, trajectory, zero_frame), axis=0)).reshape(CLIPS, TOKENS, PATCH)
    following = lax.optimization_barrier(jnp.sum(jnp.where(pick_next, trajectory, zero_frame), axis=0)).reshape(CLIPS, TOKENS, PATCH)
    step_size = 1.0 / (STEPS + 1)
    noise_sigma = 1.0 - chosen.astype(jnp.float32) * step_size
    spread = noise_level * jnp.sqrt(step_size * noise_sigma)
    embedded = block_input.astype(jnp.float32) + jnp.dot(current, patch_input_weight, preferred_element_type=jnp.float32)
    modulation = timestep_norm_shift[chosen]
    normed = embedded / jnp.sqrt(lax.optimization_barrier(jnp.mean(embedded * embedded, axis=2, keepdims=True)) + norm_eps)
    normalized_input = (normed * (1.0 + modulation[:, 1][:, None, :]) + modulation[:, 0][:, None, :]).astype(jnp.bfloat16)
    input_scale = 1.0 / math.sqrt(MODEL_WIDTH)
    out_scale = 1.0 / math.sqrt(ADAPTER_RANK)
    narrow_query_part = (jnp.dot(normalized_input, adapter_down_factor.astype(jnp.bfloat16), preferred_element_type=jnp.float32) * input_scale).astype(jnp.bfloat16)
    upper_adapter_half = adapter_up_factor.astype(jnp.bfloat16)
    query_proj = (jnp.dot(normalized_input, frozen_query_matrix, preferred_element_type=jnp.float32) + jnp.dot(narrow_query_part, upper_adapter_half, preferred_element_type=jnp.float32) * out_scale).astype(jnp.bfloat16)
    key_proj = jnp.dot(normalized_input, frozen_key_matrix, preferred_element_type=jnp.float32).astype(jnp.bfloat16)
    value_proj = jnp.dot(normalized_input, frozen_value_matrix, preferred_element_type=jnp.float32).astype(jnp.bfloat16)
    live_tokens = jnp.arange(TOKENS)[None, :] < lengths[:, None]
    live_items = jnp.repeat(live_tokens, HEADS_W, axis=0)
    query_items = split_heads(query_proj)
    key_items = split_heads(key_proj)
    value_items = split_heads(value_proj)
    head_out, row_peak, totals = lax.map(forward_head, (query_items, key_items, value_items, live_items))
    attn_out = merge_heads(head_out).astype(jnp.bfloat16)
    velocity = jnp.dot(attn_out, velocity_output_weight, preferred_element_type=jnp.float32)
    zscore = (following.astype(jnp.float32) - current.astype(jnp.float32) + step_size * velocity) / spread[:, None, None]
    counts = (lengths * PATCH).astype(jnp.float32)
    squares = jnp.where(live_tokens[:, :, None], zscore * zscore, 0.0)
    logprob = -0.5 * lax.optimization_barrier(jnp.sum(squares, axis=(1, 2))) / counts
    ratios = jnp.exp(logprob - rollout_log_probability)
    advantage = advantages(rewards, prompt_group_index)[:CLIPS]
    weight = clip_weight(advantage, ratios, float(CLIPS))
    grad_vel = jnp.where(live_tokens[:, :, None], -weight[:, None, None] * zscore * step_size / (spread[:, None, None] * counts[:, None, None]), 0.0).astype(jnp.bfloat16)
    grad_out = jnp.dot(grad_vel, velocity_output_weight.T, preferred_element_type=jnp.float32).astype(jnp.bfloat16)
    grad_items = split_heads(grad_out)
    deltas = lax.optimization_barrier(jnp.sum(grad_items.astype(jnp.float32) * split_heads(attn_out).astype(jnp.float32), axis=2))
    grad_heads = lax.map(backward_head, (query_items, key_items, value_items, live_items, grad_items, row_peak, totals, deltas))
    grad_q = merge_heads(grad_heads).astype(jnp.bfloat16)
    up_gradient = jnp.dot(narrow_query_part.reshape(-1, ADAPTER_RANK).T, grad_q.reshape(-1, PROJECTION_WIDTH), preferred_element_type=jnp.float32) * out_scale
    grad_low = (jnp.dot(grad_q, upper_adapter_half.T, preferred_element_type=jnp.float32) * out_scale).astype(jnp.bfloat16)
    down_gradient = jnp.dot(normalized_input.reshape(-1, MODEL_WIDTH).T, grad_low.reshape(-1, ADAPTER_RANK), preferred_element_type=jnp.float32) * input_scale
    update_factor = step_length / jnp.sqrt(jnp.sum(down_gradient * down_gradient) + norm_eps)
    return (adapter_down_factor - update_factor * down_gradient, adapter_up_factor - update_factor * up_gradient, ratios)
```

```python
import functools
import math

import jax
import jax.numpy as jnp
from jax import lax
from jax.experimental import pallas as pl
from jax.experimental.pallas import tpu as pltpu
from jax.sharding import PartitionSpec as P

MESH = pl.DeviceIdType.MESH
F32 = jnp.float32
BF16 = jnp.bfloat16

MODEL_WIDTH = 3072
HD = 128
ADAPTER_RANK = 128
STEPS = 4
GROUP = 16
PATCH = 64
CLIPS = 4
ROWS = 256
PAIRS = 32
OWN = 384
PLANE = 1024
HALF = 1536

noise_level = 0.8
clip_range = 0.2
step_length = 256.0
norm_eps = 1e-06
masked_score = -1e30
step_size = 1.0 / (STEPS + 1)
input_scale = 1.0 / math.sqrt(MODEL_WIDTH)
out_scale = 1.0 / math.sqrt(ADAPTER_RANK)
head_scale = 1.0 / math.sqrt(HD)
query_scale = head_scale * math.log2(math.e)

NT = (((1,), (1,)), ((), ()))

R_X = 0
R_PAIR = 3
R_Z = 8
R_FAR = 16
R_CORE = 20
R_VEL = 36
R_SQ = 39
R_LOW = 46
R_RC = 49
R_RX = 50
R_RZ = 53
R_RY = 56
R_GZ = 59
R_GX = 62
R_GC = 65
N_RECV = 69
N_SEND = 96


def dot(a, b):
    return jnp.dot(a, b, preferred_element_type=F32)


def dot_nt(a, b):
    return lax.dot_general(a, b, NT, preferred_element_type=F32)


def iota(shape, dim):
    return lax.broadcasted_iota(jnp.int32, shape, dim)


def lanes(start, size):
    return pl.ds(pl.multiple_of(start, 128), size)


def rows_at(start, size, unit=256):
    return pl.ds(pl.multiple_of(start, unit), size)


def body(
    chosen_ref, lengths_ref, rollout_ref,
    traj_ref, rewards_ref, groups_ref, shift_ref, patch_ref, wout_ref, down_ref, up_ref,
    x_hbm, wq_hbm, wk_hbm, wv_hbm,
    out_down, out_up, out_ratio,
    xin, wq, wk, wv, downb, upb, emb, normed,
    sel, latents, stage_k, stage_v, stage_q, keys, values, queries, low,
    top, total, acc, attn, vel, squares, gout, gq, glow_send, glow,
    du, core_recv, xs, xr, zs, zr, yr, zg, full,
    send_sem, recv_sem, local_sem,
):
    sec = lax.axis_index("section")
    x = lax.axis_index("dp")
    seq = lax.axis_index("seq")
    z = seq // 4
    yl = (seq // 2) % 2
    core = seq % 2
    y = sec * 2 + yl

    def at(sec_, x_, z_, yl_, core_):
        return (sec_, x_, z_ * 4 + yl_ * 2 + core_)

    def y_peer(step):
        other = (y + step) % 4
        return other, at(other // 2, x, z, other % 2, core)

    other_core = at(sec, x, z, yl, 1 - core)
    partner = at(sec, x, z, 1 - yl, core)
    z_up = at(sec, x, (z + 1) % 4, yl, core)
    z_down = at(sec, x, (z + 3) % 4, yl, core)

    pending = []

    def descriptor(src, dst, send_index, recv_index, device):
        return pltpu.make_async_remote_copy(
            src_ref=src, dst_ref=dst, send_sem=send_sem.at[send_index], recv_sem=recv_sem.at[recv_index],
            device_id=device, device_id_type=MESH,
        )

    def send(src, dst, recv_index, device):
        copy = descriptor(src, dst, len(pending), recv_index, device)
        copy.start()
        pending.append(copy)

    def arrive(dst, recv_index):
        descriptor(dst, dst, 0, recv_index, other_core).wait_recv()

    loads = []

    def load(src, dst):
        copy = pltpu.make_async_copy(src, dst, local_sem.at[len(loads)])
        copy.start()
        loads.append(copy)
        return copy

    load_x = load(x_hbm, xin)
    own_cols, other_cols = lanes(yl * OWN, OWN), lanes((1 - yl) * OWN, OWN)
    load_w = []
    for src, dst in ((wk_hbm, wk), (wv_hbm, wv), (wq_hbm, wq)):
        load_w.append((load(src.at[:, own_cols], dst.at[:, 0:OWN]), load(src.at[:, other_cols], dst.at[:, OWN : 2 * OWN])))

    peers = [at(sec, (x + d) % 4, z, yl, core) for d in (1, 2, 3)]
    peers += [y_peer(d)[1] for d in (1, 2, 3)]
    peers += [at(sec, x, (z + d) % 4, yl, core) for d in (1, 2, 3)]
    peers += [at(sec, x, (z + d) % 4, yl, 1 - core) for d in (0, 1, 2, 3)]
    barrier = pltpu.get_barrier_semaphore()
    for peer in peers:
        pl.semaphore_signal(barrier, inc=1, device_id=peer, device_id_type=MESH)

    for c in range(CLIPS):
        sel[c, 0] = traj_ref[chosen_ref[c], c]
        sel[c, 1] = traj_ref[chosen_ref[c] + 1, c]
    pl.semaphore_wait(barrier, len(peers))
    x_rows = rows_at(x * PAIRS, PAIRS, PAIRS)
    for d in (1, 2, 3):
        to = (x + d) % 4
        send(sel.at[to], latents.at[yl, :, x_rows, :], R_X + d - 1, at(sec, to, z, yl, core))
    latents[yl, :, x_rows, :] = sel[x]

    downb[...] = down_ref[...].astype(BF16)
    upb[:, 0:OWN] = up_ref[:, own_cols].astype(BF16)
    upb[:, OWN : 2 * OWN] = up_ref[:, other_cols].astype(BF16)

    chosen = chosen_ref[x]
    length = lengths_ref[x]
    one = jnp.ones((1, 1), F32)
    spread = noise_level * jnp.sqrt(step_size * (1.0 - one * chosen.astype(F32) * step_size))
    count = one * (length * PATCH).astype(F32)

    expand = jnp.where((iota((ROWS, 128), 0) >> 1) == iota((ROWS, 128), 1), 1.0, 0.0).astype(BF16)
    own_half = (iota((ROWS, 128), 1) >> 6) == (iota((ROWS, 128), 0) & 1)

    def token_rows(pairs):
        return jnp.where(own_half, dot(expand, pairs), 0.0).astype(BF16)

    def fold(offset, width):
        source = (iota((128, width), 0) & 63) + offset
        return jnp.where(source == iota((128, width), 1), 1.0, 0.0).astype(BF16)

    for d in (1, 2, 3):
        src_rows = rows_at(((x + 4 - d) % 4) * PAIRS, PAIRS, PAIRS)
        arrive(latents.at[yl, :, src_rows, :], R_X + d - 1)
    send(latents.at[yl], latents.at[yl], R_PAIR + 4, partner)

    now_tokens = dot(token_rows(latents[yl, 0]), fold(0, 64)).astype(BF16)
    load_x.wait()
    squares_sum = jnp.zeros((ROWS, 1), F32)
    chunk = 512
    for j in range(MODEL_WIDTH // chunk):
        cols = slice(j * chunk, (j + 1) * chunk)
        part = xin[:, cols].astype(F32) + dot(now_tokens, patch_ref[:, cols])
        emb[:, cols] = part
        squares_sum += jnp.sum(part * part, axis=1, keepdims=True)
    inverse = lax.rsqrt(squares_sum * (1.0 / MODEL_WIDTH) + norm_eps)
    for j in range(MODEL_WIDTH // chunk):
        cols = slice(j * chunk, (j + 1) * chunk)
        shift = shift_ref[chosen, 0:1, cols]
        scale = shift_ref[chosen, 1:2, cols]
        normed[:, cols] = (emb[:, cols] * inverse * (1.0 + scale) + shift).astype(BF16)

    seq_own = seq * ROWS
    seq_pair = (seq + 2 - 4 * yl) * ROWS

    def block(ref, z_, yl_, core_):
        return ref.at[rows_at((z_ * 4 + yl_ * 2 + core_) * ROWS, ROWS), :]

    def project(weight, loaded, stage, extra=None, scale=None):
        for copy in loaded:
            copy.wait()

        def step(n, carry):
            cols = lanes(n * 256, 256)
            part = dot(normed[...], weight[:, cols])
            if extra is not None:
                part = (part + dot(extra, upb[:, cols]) * out_scale) * scale
            stage[:, cols] = part.astype(BF16)
            return carry

        lax.fori_loop(0, 3, step, 0)

    store = (keys, values)

    def core_index(plane, pair, kv):
        return R_CORE + plane * 4 + pair * 2 + kv

    def to_core(plane, pair, kv):
        z_ = (z + plane) % 4
        yl_ = yl if pair == 0 else 1 - yl
        send(block(store[kv], z_, yl_, core), block(store[kv], z_, yl_, core), core_index(plane, pair, kv), other_core)

    def from_core(plane):
        z_ = (z + plane) % 4
        for pair in (0, 1):
            yl_ = yl if pair == 0 else 1 - yl
            for kv in (0, 1):
                arrive(block(store[kv], z_, yl_, 1 - core), core_index(plane, pair, kv))

    def z_index(pair, kv, above):
        return R_Z + pair * 4 + kv * 2 + above

    def to_z(pair, kv):
        src = block(store[kv], z, yl if pair == 0 else 1 - yl, core)
        send(src, src, z_index(pair, kv, 0), z_up)
        send(src, src, z_index(pair, kv, 1), z_down)

    def from_z(pair, kv, above):
        z_ = (z + 1) % 4 if above else (z + 3) % 4
        src = block(store[kv], z_, yl if pair == 0 else 1 - yl, core)
        arrive(src, z_index(pair, kv, above))
        if kv == 0 and not above:
            send(src, src, R_FAR + pair * 2 + kv, z_up)
        if kv == 1 and above:
            send(src, src, R_FAR + pair * 2 + kv, z_down)
        to_core(1 if above else 3, pair, kv)

    def from_far(pair, kv):
        arrive(block(store[kv], (z + 2) % 4, yl if pair == 0 else 1 - yl, core), R_FAR + pair * 2 + kv)
        to_core(2, pair, kv)

    own_block = rows_at(seq_own, ROWS)
    for kv, (weight, stage) in enumerate(((wk, stage_k), (wv, stage_v))):
        project(weight, load_w[kv], stage)
        send(stage.at[:, OWN : 2 * OWN], block(store[kv], z, yl, core), R_PAIR + kv, partner)
        store[kv][own_block, :] = stage[:, 0:OWN]
        to_z(0, kv)
        to_core(0, 0, kv)
    own_rows = rows_at(yl * ROWS, ROWS)
    pair_rows = rows_at((1 - yl) * ROWS, ROWS)
    low_own = (dot(normed[...], downb[...]) * input_scale).astype(BF16)
    low[own_rows, :] = low_own
    project(wq, load_w[2], stage_q, low_own, query_scale)
    send(stage_q.at[:, OWN : 2 * OWN], queries.at[own_rows, :], R_PAIR + 2, partner)
    queries[own_rows, :] = stage_q[:, 0:OWN]
    send(low.at[own_rows, :], low.at[own_rows, :], R_PAIR + 3, partner)
    for kv in (0, 1):
        arrive(block(store[kv], z, 1 - yl, core), R_PAIR + kv)
        to_z(1, kv)
        to_core(0, 1, kv)

    def key_bias(start):
        return jnp.where(start + iota((1, PLANE), 1) < length, 0.0, masked_score)

    def forward_plane(plane):
        start = ((z + plane) % 4) * PLANE
        plane_rows = rows_at(start, PLANE, PLANE)
        bias = key_bias(start)
        first = plane == 0

        def step(i, carry):
            head = i // 2
            cols = lanes(head * HD, HD)
            rows = rows_at((i % 2) * ROWS, ROWS)
            scores = dot_nt(queries[rows, cols], keys[plane_rows, cols]) + bias
            peak = jnp.max(scores, axis=1, keepdims=True)
            if not first:
                before = top[head, rows, :][:, 0:1]
                peak = jnp.maximum(peak, before)
            exp_scores = jnp.exp2(scores - peak)
            sums = jnp.sum(exp_scores, axis=1, keepdims=True)
            weighted = dot(exp_scores.astype(BF16), values[plane_rows, cols])
            if not first:
                decay = jnp.exp2(before - peak)
                sums += decay * total[head, rows, :][:, 0:1]
                weighted += decay * acc[rows, cols]
            top[head, rows, :] = jnp.broadcast_to(peak, (ROWS, 128))
            total[head, rows, :] = jnp.broadcast_to(sums, (ROWS, 128))
            acc[rows, cols] = weighted
            return carry

        lax.fori_loop(0, 6, step, 0)

    for kv in (0, 1):
        for above in (0, 1):
            from_z(0, kv, above)
    arrive(queries.at[pair_rows, :], R_PAIR + 2)
    from_core(0)
    forward_plane(0)
    for kv in (0, 1):
        for above in (0, 1):
            from_z(1, kv, above)
    from_core(1)
    forward_plane(1)
    from_far(0, 0)
    from_far(0, 1)
    from_core(3)
    forward_plane(3)
    from_far(1, 0)
    from_far(1, 1)
    from_core(2)
    forward_plane(2)

    def finish_head(i, carry):
        head = i // 2
        cols = lanes(head * HD, HD)
        rows = rows_at((i % 2) * ROWS, ROWS)
        sums = total[head, rows, :]
        attn[rows, cols] = (acc[rows, cols] / sums).astype(BF16)
        top[head, rows, :] = top[head, rows, :] + jnp.log(sums) * math.log2(math.e)
        return carry

    lax.fori_loop(0, 6, finish_head, 0)

    wout = wout_ref[rows_at(yl * OWN, OWN, 128), :]
    spread_cols = [
        jnp.where(iota((PATCH, 128), 0) + PATCH * b == iota((PATCH, 128), 1), 1.0, 0.0).astype(BF16) for b in (0, 1)
    ]
    wide = [dot(wout, cols).astype(BF16) for cols in spread_cols]
    partial = dot(attn[0:ROWS, :], wide[0]) + dot(attn[ROWS : 2 * ROWS, :], wide[1])
    vel[y] = partial.astype(BF16)
    for d in (1, 2, 3):
        send(vel.at[y], vel.at[y], R_VEL + d - 1, y_peer(d)[1])
    arrive(latents.at[1 - yl], R_PAIR + 4)
    arrive(low.at[pair_rows, :], R_PAIR + 3)
    moved = jnp.zeros((ROWS, 128), F32)
    for b in (0, 1):
        moved += dot(token_rows(latents[b, 1]), fold(PATCH * b, 128))
        moved -= dot(token_rows(latents[b, 0]), fold(PATCH * b, 128))
    lane_block = iota((ROWS, 128), 1) >> 6
    position = (z * 4 + lane_block * 2 + core) * ROWS + iota((ROWS, 128), 0)
    live = position < length
    for d in (1, 2, 3):
        arrive(vel.at[(y + 4 - d) % 4], R_VEL + d - 1)
    velocity = jnp.zeros((ROWS, 128), F32)
    for b in range(4):
        velocity += vel[b].astype(F32)
    zscore = (moved + step_size * velocity) / spread
    own_squares = jnp.where(live, zscore * zscore, 0.0)
    slot = z * 2 + core
    squares[slot] = jnp.sum(own_squares.reshape(ROWS // 8, 8, 128), axis=0)
    sq_index = 0
    sq_waits = []
    for dz in range(4):
        for dc in (0, 1):
            if dz == 0 and dc == 0:
                continue
            to_core_id = (core + dc) % 2
            send(squares.at[slot], squares.at[slot], R_SQ + sq_index, at(sec, x, (z + dz) % 4, yl, to_core_id))
            sq_waits.append((((z + 4 - dz) % 4) * 2 + to_core_id, R_SQ + sq_index))
            sq_index += 1

    batch = rewards_ref.shape[1]
    reward = rewards_ref[...].astype(F32)
    group = groups_ref[...].astype(F32)
    mine = iota((1, batch), 1) == x
    own_group = jnp.sum(jnp.where(mine, group, 0.0), axis=1, keepdims=True)
    own_reward = jnp.sum(jnp.where(mine, reward, 0.0), axis=1, keepdims=True)
    member = jnp.where(group == own_group, 1.0, 0.0)
    mean = jnp.sum(member * reward, axis=1, keepdims=True) / GROUP
    centered = reward - mean
    variance = jnp.sum(member * centered * centered, axis=1, keepdims=True) / GROUP
    advantage = (own_reward - mean) / (jnp.sqrt(variance) + 1.0)

    for index, recv in sq_waits:
        arrive(squares.at[index], recv)
    clip_squares = jnp.zeros((8, 128), F32)
    for b in range(8):
        clip_squares += squares[b]
    clip_squares = jnp.sum(jnp.sum(clip_squares, axis=1, keepdims=True), axis=0, keepdims=True)
    ratio = jnp.exp(-0.5 * clip_squares / count - one * rollout_ref[x])
    out_ratio[...] = jnp.broadcast_to(ratio, (8, 128))
    low_edge, high_edge = 1.0 - clip_range, 1.0 + clip_range
    inside = (ratio >= low_edge) & (ratio <= high_edge)
    active = inside | ((advantage > 0) & (ratio < low_edge)) | ((advantage < 0) & (ratio > high_edge))
    weight = jnp.where(active, -advantage * ratio / float(CLIPS), 0.0)

    grad_vel = jnp.where(live, -weight * zscore * step_size / (spread * count), 0.0).astype(BF16)
    for b in (0, 1):
        gout[b * ROWS : (b + 1) * ROWS, :] = dot_nt(grad_vel, wide[b]).astype(BF16)

    def backward(i, carry):
        head = i // 2
        cols = lanes(head * HD, HD)
        rows = rows_at((i % 2) * ROWS, ROWS)
        query, grad = queries[rows, cols], gout[rows, cols]
        shift_row = top[head, rows, :][:, 0:1]
        delta = jnp.sum(grad.astype(F32) * attn[rows, cols].astype(F32), axis=1, keepdims=True)

        def plane_step(p, grad_sum):
            plane_rows = rows_at(p * PLANE, PLANE, PLANE)
            key = keys[plane_rows, cols]
            probabilities = jnp.exp2(dot_nt(query, key) + key_bias(p * PLANE) - shift_row)
            grad_probs = dot_nt(grad, values[plane_rows, cols])
            grad_scores = (probabilities * (grad_probs - delta)).astype(BF16)
            return grad_sum + dot(grad_scores, key)

        grad_sum = lax.fori_loop(0, 4, plane_step, jnp.zeros((ROWS, HD), F32))
        gq[rows, cols] = (grad_sum * head_scale).astype(BF16)
        return carry

    lax.fori_loop(0, 6, backward, 0)

    for b in (0, 1):
        part = dot_nt(gq[b * ROWS : (b + 1) * ROWS, :], upb[:, 0:OWN]) * out_scale
        glow_send[b] = part.astype(BF16)
    for d in (1, 2, 3):
        other, device = y_peer(d)
        send(glow_send.at[other % 2], glow.at[y], R_LOW + d - 1, device)
    glow[y] = glow_send[yl]
    up_part = dot(jnp.transpose(low[...].astype(F32)).astype(BF16), gq[...])
    du[0, :, 768:1024] = up_part[:, 0:256]
    du[1, :, 768:896] = up_part[:, 256:384]
    du[1, :, 896:1024] = jnp.zeros((128, 128), F32)
    for d in (1, 2, 3):
        arrive(glow.at[(y + 4 - d) % 4], R_LOW + d - 1)
    low_sum = jnp.zeros((ROWS, 128), F32)
    for b in range(4):
        low_sum += glow[b].astype(F32)
    low_turned = jnp.transpose(low_sum).astype(BF16)

    for half in (1, 0):
        where = (core + half) % 2
        for j in range(3):
            cols = lanes(sec * HALF + where * 768 + j * 256, 256)
            du[where, :, j * 256 : (j + 1) * 256] = dot(low_turned, normed[:, cols])
        if half == 1:
            send(du.at[where], core_recv, R_RC, other_core)
    arrive(core_recv, R_RC)
    xs[...] = (du[core] + core_recv[...]).astype(BF16)
    for d in (1, 2, 3):
        to = (x + d) % 4
        send(xs.at[rows_at(to * 32, 32, 32), :], xr.at[d - 1], R_RX + d - 1, at(sec, to, z, yl, core))
    slab = du[core, x_rows, :] + core_recv[x_rows, :]
    for d in (1, 2, 3):
        arrive(xr.at[d - 1], R_RX + d - 1)
        slab += xr[d - 1].astype(F32)
    zs[...] = slab
    for d in (1, 2, 3):
        to = (z + d) % 4
        send(zs.at[rows_at(to * 8, 8, 8), :], zr.at[d - 1], R_RZ + d - 1, at(sec, x, to, yl, core))
    z_rows = rows_at(z * 8, 8, 8)
    piece = zs[z_rows, :]
    for d in (1, 2, 3):
        arrive(zr.at[d - 1], R_RZ + d - 1)
        piece += zr[d - 1]
    yr[y] = piece
    for d in (1, 2, 3):
        send(yr.at[y], yr.at[y], R_RY + d - 1, y_peer(d)[1])
    for d in (1, 2, 3):
        arrive(yr.at[(y + 4 - d) % 4], R_RY + d - 1)
    for b in (0, 1):
        zg[z_rows, b * 768 : (b + 1) * 768] = yr[2 * b, :, 0:768] + yr[2 * b + 1, :, 0:768]
        zg[z_rows, HALF + b * 256 : HALF + (b + 1) * 256] = yr[sec * 2 + b, :, 768:1024]

    for d in (1, 2, 3):
        send(zg.at[z_rows, :], zg.at[z_rows, :], R_GZ + d - 1, at(sec, x, (z + d) % 4, yl, core))
    for d in (1, 2, 3):
        arrive(zg.at[rows_at(((z + 4 - d) % 4) * 8, 8, 8), :], R_GZ + d - 1)
    full[core, x_rows, :] = zg[...].astype(BF16)
    mine_full = full.at[core, x_rows, :]
    for d in (1, 2, 3):
        send(mine_full, mine_full, R_GX + d - 1, at(sec, (x + d) % 4, z, yl, core))
    send(mine_full, mine_full, R_GC, other_core)
    for d in (1, 2, 3):
        from_rows = rows_at(((x + 4 - d) % 4) * 32, 32, 32)
        arrive(full.at[core, from_rows, :], R_GX + d - 1)
        send(full.at[core, from_rows, :], full.at[core, from_rows, :], R_GC + d, other_core)
    for d in (0, 1, 2, 3):
        from_rows = rows_at(((x + 4 - d) % 4) * 32, 32, 32)
        arrive(full.at[1 - core, from_rows, :], R_GC + d)

    norm_sum = jnp.zeros((128, 256), F32)
    for b in (0, 1):
        for j in range(HALF // 256):
            part = full[b, :, j * 256 : (j + 1) * 256].astype(F32)
            norm_sum += part * part
    norm_sum = jnp.sum(jnp.sum(norm_sum, axis=1, keepdims=True), axis=0, keepdims=True)
    factor = step_length / jnp.sqrt(norm_sum * (input_scale * input_scale) + norm_eps)
    down_factor, up_factor = factor * input_scale, factor * out_scale
    for t in range(MODEL_WIDTH // 128):
        part = full[(t % 12) // 6, :, (t // 12) * 768 + (t % 6) * 128 : (t // 12) * 768 + (t % 6) * 128 + 128]
        rows = slice(t * 128, (t + 1) * 128)
        out_down[rows, :] = down_ref[rows, :] - down_factor * jnp.transpose(part.astype(F32))
    for b in (0, 1):
        for c, width in ((0, 256), (1, 128)):
            cols = slice(b * OWN + c * 256, b * OWN + c * 256 + width)
            part = full[c, :, HALF + b * 256 : HALF + b * 256 + width].astype(F32)
            out_up[:, cols] = up_ref[:, cols] - up_factor * part

    for copy in pending:
        copy.wait_send()


def shards(
    trajectory, block_input, chosen, lengths, rewards, prompt_group_index, rollout_log_probability,
    timestep_norm_shift, patch_input_weight, frozen_query_matrix, frozen_key_matrix, frozen_value_matrix,
    velocity_output_weight, adapter_down_factor, adapter_up_factor,
):
    vmem = pl.BlockSpec(memory_space=pltpu.VMEM)
    smem = pl.BlockSpec(memory_space=pltpu.SMEM)
    hbm = pl.BlockSpec(memory_space=pl.ANY)
    V = pltpu.VMEM
    scratch = [
        V((ROWS, MODEL_WIDTH), BF16),
        V((MODEL_WIDTH, 2 * OWN), BF16),
        V((MODEL_WIDTH, 2 * OWN), BF16),
        V((MODEL_WIDTH, 2 * OWN), BF16),
        V((MODEL_WIDTH, ADAPTER_RANK), BF16),
        V((ADAPTER_RANK, 2 * OWN), BF16),
        V((ROWS, MODEL_WIDTH), F32),
        V((ROWS, MODEL_WIDTH), BF16),
        V((CLIPS, 2, PAIRS, 128), BF16),
        V((2, 2, 128, 128), BF16),
        V((ROWS, 2 * OWN), BF16),
        V((ROWS, 2 * OWN), BF16),
        V((ROWS, 2 * OWN), BF16),
        V((4 * PLANE, OWN), BF16),
        V((4 * PLANE, OWN), BF16),
        V((2 * ROWS, OWN), BF16),
        V((2 * ROWS, ADAPTER_RANK), BF16),
        V((3, 2 * ROWS, 128), F32),
        V((3, 2 * ROWS, 128), F32),
        V((2 * ROWS, OWN), F32),
        V((2 * ROWS, OWN), BF16),
        V((4, ROWS, 128), BF16),
        V((8, 8, 128), F32),
        V((2 * ROWS, OWN), BF16),
        V((2 * ROWS, OWN), BF16),
        V((2, ROWS, 128), BF16),
        V((4, ROWS, 128), BF16),
        V((2, 128, 1024), F32),
        V((128, 1024), F32),
        V((128, 1024), BF16),
        V((3, 32, 1024), BF16),
        V((32, 1024), F32),
        V((3, 8, 1024), F32),
        V((4, 8, 1024), F32),
        V((32, 2048), F32),
        V((2, 128, 2048), BF16),
        pltpu.SemaphoreType.DMA((N_SEND,)),
        pltpu.SemaphoreType.DMA((N_RECV,)),
        pltpu.SemaphoreType.DMA((8,)),
    ]
    revised_down, revised_up, ratio = pl.pallas_call(
        body,
        out_shape=(
            jax.ShapeDtypeStruct((MODEL_WIDTH, ADAPTER_RANK), F32),
            jax.ShapeDtypeStruct((ADAPTER_RANK, 2 * OWN), F32),
            jax.ShapeDtypeStruct((8, 128), F32),
        ),
        in_specs=[smem] * 3 + [vmem] * 8 + [hbm] * 4,
        out_specs=(vmem, vmem, vmem),
        scratch_shapes=scratch,
        compiler_params=pltpu.CompilerParams(
            collective_id=0, has_side_effects=True, vmem_limit_bytes=60 * 1024 * 1024
        ),
        cost_estimate=pl.CostEstimate(flops=12_000_000_000, bytes_accessed=24_000_000, transcendentals=13_000_000),
        name="policy_step",
    )(
        chosen, lengths, rollout_log_probability,
        trajectory.reshape(STEPS + 1, CLIPS, PAIRS, 128),
        rewards.reshape(1, -1), prompt_group_index.reshape(1, -1), timestep_norm_shift, patch_input_weight,
        velocity_output_weight, adapter_down_factor, adapter_up_factor,
        block_input.reshape(ROWS, MODEL_WIDTH), frozen_query_matrix, frozen_key_matrix, frozen_value_matrix,
    )
    return revised_down, revised_up, ratio[0, :1]


def solution(mesh):
    return jax.shard_map(
        shards,
        mesh=mesh,
        in_specs=(
            P(None, None, "seq", "dp", None),
            P("dp", "seq", None),
            P(), P(), P(), P(), P(), P(), P(),
            P(None, "section"),
            P(None, "section"),
            P(None, "section"),
            P("section", None),
            P(),
            P(None, "section"),
        ),
        out_specs=(P(), P(None, "section"), P("dp")),
        check_vma=False,
    )
```

```python
import functools
import math

import jax
import jax.numpy as jnp
from jax import lax
from jax.experimental import pallas as pl
from jax.experimental.pallas import tpu as pltpu
from jax.sharding import PartitionSpec as P

MESH = pl.DeviceIdType.MESH
F32 = jnp.float32
BF16 = jnp.bfloat16

MODEL_WIDTH = 3072
HD = 128
ADAPTER_RANK = 128
STEPS = 4
GROUP = 16
PATCH = 64
CLIPS = 4
ROWS = 256
PAIRS = 32
OWN = 384
PLANE = 1024
HALF = 1536

noise_level = 0.8
clip_range = 0.2
step_length = 256.0
norm_eps = 1e-06
masked_score = -1e30
step_size = 1.0 / (STEPS + 1)
input_scale = 1.0 / math.sqrt(MODEL_WIDTH)
out_scale = 1.0 / math.sqrt(ADAPTER_RANK)
head_scale = 1.0 / math.sqrt(HD)
query_scale = head_scale * math.log2(math.e)

NT = (((1,), (1,)), ((), ()))

R_X = 0
R_PAIR = 3
R_Z = 8
R_FAR = 16
R_CORE = 20
R_VEL = 36
R_SQ = 39
R_LOW = 46
R_RC = 49
R_RX = 50
R_RZ = 53
R_RY = 56
R_GZ = 59
R_GX = 62
R_GC = 65
N_RECV = 69
N_SEND = 96


def dot(a, b):
    return jnp.dot(a, b, preferred_element_type=F32)


def dot_nt(a, b):
    return lax.dot_general(a, b, NT, preferred_element_type=F32)


def iota(shape, dim):
    return lax.broadcasted_iota(jnp.int32, shape, dim)


def lanes(start, size):
    return pl.ds(pl.multiple_of(start, 128), size)


def rows_at(start, size, unit=256):
    return pl.ds(pl.multiple_of(start, unit), size)


def body(
    chosen_ref, lengths_ref, rollout_ref,
    traj_ref, rewards_ref, groups_ref,
    shift_hbm, patch_hbm, wout_hbm, down_hbm, up_hbm, x_hbm, wq_hbm, wk_hbm, wv_hbm,
    out_grad, out_ratio,
    shift_ref, patch_ref, wout_ref, down_ref, up_ref, xin, wq, wk, wv, downb, upb, emb, normed,
    sel, latents, stage_k, stage_v, stage_q, keys, values, queries, low,
    top, total, acc, attn, vel, squares, gout, gq, glow_send, glow,
    du, core_recv, xs, xr, zs, zr, yr, zg, full,
    send_sem, recv_sem, local_sem,
):
    sec = lax.axis_index("section")
    x = lax.axis_index("dp")
    seq = lax.axis_index("seq")
    z = seq // 4
    yl = (seq // 2) % 2
    core = seq % 2
    y = sec * 2 + yl

    def at(sec_, x_, z_, yl_, core_):
        return (sec_, x_, z_ * 4 + yl_ * 2 + core_)

    def y_peer(step):
        other = (y + step) % 4
        return other, at(other // 2, x, z, other % 2, core)

    other_core = at(sec, x, z, yl, 1 - core)
    partner = at(sec, x, z, 1 - yl, core)
    z_up = at(sec, x, (z + 1) % 4, yl, core)
    z_down = at(sec, x, (z + 3) % 4, yl, core)

    pending = []

    def descriptor(src, dst, send_index, recv_index, device):
        return pltpu.make_async_remote_copy(
            src_ref=src, dst_ref=dst, send_sem=send_sem.at[send_index], recv_sem=recv_sem.at[recv_index],
            device_id=device, device_id_type=MESH,
        )

    def send(src, dst, recv_index, device):
        copy = descriptor(src, dst, len(pending), recv_index, device)
        copy.start()
        pending.append(copy)

    def arrive(dst, recv_index):
        descriptor(dst, dst, 0, recv_index, other_core).wait_recv()

    loads = []

    def load(src, dst):
        copy = pltpu.make_async_copy(src, dst, local_sem.at[len(loads)])
        copy.start()
        loads.append(copy)
        return copy


    peers = [at(sec, (x + d) % 4, z, yl, core) for d in (1, 2, 3)]
    peers += [y_peer(d)[1] for d in (1, 2, 3)]
    peers += [at(sec, x, (z + d) % 4, yl, core) for d in (1, 2, 3)]
    peers += [at(sec, x, (z + d) % 4, yl, 1 - core) for d in (0, 1, 2, 3)]
    barrier = pltpu.get_barrier_semaphore()
    for peer in peers:
        pl.semaphore_signal(barrier, inc=1, device_id=peer, device_id_type=MESH)

    load_x = [load(x_hbm, xin), load(patch_hbm, patch_ref), load(shift_hbm, shift_ref)]
    own_cols, other_cols = lanes(yl * OWN, OWN), lanes((1 - yl) * OWN, OWN)
    load_w = []
    for src, dst in ((wk_hbm, wk), (wv_hbm, wv), (wq_hbm, wq)):
        load_w.append((load(src.at[:, own_cols], dst.at[:, 0:OWN]), load(src.at[:, other_cols], dst.at[:, OWN : 2 * OWN])))
    load_adapter = [load(down_hbm, down_ref), load(up_hbm, up_ref), load(wout_hbm.at[:, own_cols], wout_ref)]

    for c in range(CLIPS):
        sel[c, 0] = traj_ref[chosen_ref[c], c]
        sel[c, 1] = traj_ref[chosen_ref[c] + 1, c]
    pl.semaphore_wait(barrier, len(peers))
    x_rows = rows_at(x * PAIRS, PAIRS, PAIRS)
    for d in (1, 2, 3):
        to = (x + d) % 4
        send(sel.at[to], latents.at[yl, :, x_rows, :], R_X + d - 1, at(sec, to, z, yl, core))
    latents[yl, :, x_rows, :] = sel[x]

    chosen = chosen_ref[x]
    length = lengths_ref[x]
    one = jnp.ones((1, 1), F32)
    spread = noise_level * jnp.sqrt(step_size * (1.0 - one * chosen.astype(F32) * step_size))
    count = one * (length * PATCH).astype(F32)

    expand = jnp.where((iota((ROWS, 128), 0) >> 1) == iota((ROWS, 128), 1), 1.0, 0.0).astype(BF16)
    own_half = (iota((ROWS, 128), 1) >> 6) == (iota((ROWS, 128), 0) & 1)

    def token_rows(pairs):
        return jnp.where(own_half, dot(expand, pairs), 0.0).astype(BF16)

    def fold(offset, width):
        source = (iota((128, width), 0) & 63) + offset
        return jnp.where(source == iota((128, width), 1), 1.0, 0.0).astype(BF16)

    for d in (1, 2, 3):
        src_rows = rows_at(((x + 4 - d) % 4) * PAIRS, PAIRS, PAIRS)
        arrive(latents.at[yl, :, src_rows, :], R_X + d - 1)
    send(latents.at[yl], latents.at[yl], R_PAIR + 4, partner)

    now_tokens = dot(token_rows(latents[yl, 0]), fold(0, 64)).astype(BF16)
    for copy in load_x:
        copy.wait()
    squares_sum = jnp.zeros((ROWS, 1), F32)
    chunk = 512
    for j in range(MODEL_WIDTH // chunk):
        cols = slice(j * chunk, (j + 1) * chunk)
        part = xin[:, cols].astype(F32) + dot(now_tokens, patch_ref[:, cols])
        emb[:, cols] = part
        squares_sum += jnp.sum(part * part, axis=1, keepdims=True)
    inverse = lax.rsqrt(squares_sum * (1.0 / MODEL_WIDTH) + norm_eps)
    for j in range(MODEL_WIDTH // chunk):
        cols = slice(j * chunk, (j + 1) * chunk)
        shift = shift_ref[chosen, 0:1, cols]
        scale = shift_ref[chosen, 1:2, cols]
        normed[:, cols] = (emb[:, cols] * inverse * (1.0 + scale) + shift).astype(BF16)

    seq_own = seq * ROWS
    seq_pair = (seq + 2 - 4 * yl) * ROWS

    def block(ref, z_, yl_, core_):
        return ref.at[rows_at((z_ * 4 + yl_ * 2 + core_) * ROWS, ROWS), :]

    def project(weight, loaded, stage, extra=None, scale=None):
        for copy in loaded:
            copy.wait()

        def step(n, carry):
            cols = lanes(n * 256, 256)
            part = dot(normed[...], weight[:, cols])
            if extra is not None:
                part = (part + dot(extra, upb[:, cols]) * out_scale) * scale
            stage[:, cols] = part.astype(BF16)
            return carry

        lax.fori_loop(0, 3, step, 0)

    store = (keys, values)

    def core_index(plane, pair, kv):
        return R_CORE + plane * 4 + pair * 2 + kv

    def to_core(plane, pair, kv):
        z_ = (z + plane) % 4
        yl_ = yl if pair == 0 else 1 - yl
        send(block(store[kv], z_, yl_, core), block(store[kv], z_, yl_, core), core_index(plane, pair, kv), other_core)

    def from_core(plane):
        z_ = (z + plane) % 4
        for pair in (0, 1):
            yl_ = yl if pair == 0 else 1 - yl
            for kv in (0, 1):
                arrive(block(store[kv], z_, yl_, 1 - core), core_index(plane, pair, kv))

    def z_index(pair, kv, above):
        return R_Z + pair * 4 + kv * 2 + above

    def to_z(pair, kv):
        src = block(store[kv], z, yl if pair == 0 else 1 - yl, core)
        send(src, src, z_index(pair, kv, 0), z_up)
        send(src, src, z_index(pair, kv, 1), z_down)

    def from_z(pair, kv, above):
        z_ = (z + 1) % 4 if above else (z + 3) % 4
        src = block(store[kv], z_, yl if pair == 0 else 1 - yl, core)
        arrive(src, z_index(pair, kv, above))
        if kv == 0 and not above:
            send(src, src, R_FAR + pair * 2 + kv, z_up)
        if kv == 1 and above:
            send(src, src, R_FAR + pair * 2 + kv, z_down)
        to_core(1 if above else 3, pair, kv)

    def from_far(pair, kv):
        arrive(block(store[kv], (z + 2) % 4, yl if pair == 0 else 1 - yl, core), R_FAR + pair * 2 + kv)
        to_core(2, pair, kv)

    own_block = rows_at(seq_own, ROWS)
    for kv, (weight, stage) in enumerate(((wk, stage_k), (wv, stage_v))):
        project(weight, load_w[kv], stage)
        send(stage.at[:, OWN : 2 * OWN], block(store[kv], z, yl, core), R_PAIR + kv, partner)
        store[kv][own_block, :] = stage[:, 0:OWN]
        to_z(0, kv)
        to_core(0, 0, kv)
    own_rows = rows_at(yl * ROWS, ROWS)
    pair_rows = rows_at((1 - yl) * ROWS, ROWS)
    for copy in load_adapter:
        copy.wait()
    downb[...] = down_ref[...].astype(BF16)
    upb[:, 0:OWN] = up_ref[:, own_cols].astype(BF16)
    upb[:, OWN : 2 * OWN] = up_ref[:, other_cols].astype(BF16)
    low_own = (dot(normed[...], downb[...]) * input_scale).astype(BF16)
    low[own_rows, :] = low_own
    project(wq, load_w[2], stage_q, low_own, query_scale)
    send(stage_q.at[:, OWN : 2 * OWN], queries.at[own_rows, :], R_PAIR + 2, partner)
    queries[own_rows, :] = stage_q[:, 0:OWN]
    send(low.at[own_rows, :], low.at[own_rows, :], R_PAIR + 3, partner)
    for kv in (0, 1):
        arrive(block(store[kv], z, 1 - yl, core), R_PAIR + kv)
        to_z(1, kv)
        to_core(0, 1, kv)

    def key_bias(start):
        return jnp.where(start + iota((1, PLANE), 1) < length, 0.0, masked_score)

    def repeat(stat, count):
        return jnp.concatenate([stat] * count, axis=1)

    def fold_lanes(op, tile):
        out = tile[:, 0:128]
        for j in range(1, tile.shape[1] // 128):
            out = op(out, tile[:, j * 128 : (j + 1) * 128])
        return out

    def forward_plane(plane):
        start = ((z + plane) % 4) * PLANE
        plane_rows = rows_at(start, PLANE, PLANE)
        bias = key_bias(start)
        first = plane == 0
        tiles = [(h, slice(h * HD, (h + 1) * HD), slice(b * ROWS, (b + 1) * ROWS)) for h in range(3) for b in (0, 1)]

        def score(tile):
            _, cols, rows = tile
            return dot_nt(queries[rows, cols], keys[plane_rows, cols]) + bias

        def softmax(tile, scores):
            head, cols, rows = tile
            peak = jnp.max(fold_lanes(jnp.maximum, scores), axis=1, keepdims=True)
            peak = jnp.broadcast_to(peak, (ROWS, 128))
            if not first:
                before = top[head, rows, :]
                peak = jnp.maximum(peak, before)
            exp_scores = jnp.exp2(scores - repeat(peak, PLANE // 128))
            sums = fold_lanes(jnp.add, exp_scores)
            weighted = dot(exp_scores.astype(BF16), values[plane_rows, cols])
            if not first:
                decay = jnp.exp2(before - peak)
                sums += decay * total[head, rows, :]
                weighted += decay * acc[rows, cols]
            top[head, rows, :] = peak
            total[head, rows, :] = sums
            acc[rows, cols] = weighted

        scores = score(tiles[0])
        for i, tile in enumerate(tiles):
            ahead = score(tiles[i + 1]) if i + 1 < len(tiles) else None
            softmax(tile, scores)
            scores = ahead

    for kv in (0, 1):
        for above in (0, 1):
            from_z(0, kv, above)
    arrive(queries.at[pair_rows, :], R_PAIR + 2)
    from_core(0)
    forward_plane(0)
    for kv in (0, 1):
        for above in (0, 1):
            from_z(1, kv, above)
    from_core(1)
    forward_plane(1)
    from_far(0, 0)
    from_far(0, 1)
    from_core(3)
    forward_plane(3)
    from_far(1, 0)
    from_far(1, 1)
    from_core(2)
    forward_plane(2)

    def finish_head(i, carry):
        head = i // 2
        cols = lanes(head * HD, HD)
        rows = rows_at((i % 2) * ROWS, ROWS)
        sums = jnp.broadcast_to(jnp.sum(total[head, rows, :], axis=1, keepdims=True), (ROWS, 128))
        attn[rows, cols] = (acc[rows, cols] / sums).astype(BF16)
        top[head, rows, :] = top[head, rows, :] + jnp.log(sums) * math.log2(math.e)
        return carry

    lax.fori_loop(0, 6, finish_head, 0)

    blank = jnp.zeros((PATCH, OWN), BF16)
    wide = [jnp.concatenate([wout_ref[...], blank], axis=0), jnp.concatenate([blank, wout_ref[...]], axis=0)]
    partial = dot_nt(attn[0:ROWS, :], wide[0]) + dot_nt(attn[ROWS : 2 * ROWS, :], wide[1])
    vel[y] = partial.astype(BF16)
    for d in (1, 2, 3):
        send(vel.at[y], vel.at[y], R_VEL + d - 1, y_peer(d)[1])
    arrive(latents.at[1 - yl], R_PAIR + 4)
    arrive(low.at[pair_rows, :], R_PAIR + 3)
    moved = jnp.zeros((ROWS, 128), F32)
    for b in (0, 1):
        moved += dot(token_rows(latents[b, 1]), fold(PATCH * b, 128))
        moved -= dot(token_rows(latents[b, 0]), fold(PATCH * b, 128))
    lane_block = iota((ROWS, 128), 1) >> 6
    position = (z * 4 + lane_block * 2 + core) * ROWS + iota((ROWS, 128), 0)
    live = position < length
    for d in (1, 2, 3):
        arrive(vel.at[(y + 4 - d) % 4], R_VEL + d - 1)
    velocity = jnp.zeros((ROWS, 128), F32)
    for b in range(4):
        velocity += vel[b].astype(F32)
    zscore = (moved + step_size * velocity) / spread
    own_squares = jnp.where(live, zscore * zscore, 0.0)
    slot = z * 2 + core
    squares[slot] = jnp.sum(own_squares.reshape(ROWS // 8, 8, 128), axis=0)
    sq_index = 0
    sq_waits = []
    for dz in range(4):
        for dc in (0, 1):
            if dz == 0 and dc == 0:
                continue
            to_core_id = (core + dc) % 2
            send(squares.at[slot], squares.at[slot], R_SQ + sq_index, at(sec, x, (z + dz) % 4, yl, to_core_id))
            sq_waits.append((((z + 4 - dz) % 4) * 2 + to_core_id, R_SQ + sq_index))
            sq_index += 1

    grad_vel = jnp.where(live, -zscore * step_size / (spread * count), 0.0).astype(BF16)
    for b in (0, 1):
        gout[b * ROWS : (b + 1) * ROWS, :] = dot(grad_vel, wide[b]).astype(BF16)

    for head in range(3):
        cols = slice(head * HD, (head + 1) * HD)
        delta = jnp.sum(gout[:, cols].astype(F32) * attn[:, cols].astype(F32), axis=1, keepdims=True)
        total[head] = jnp.broadcast_to(delta, (2 * ROWS, 128))
    acc[...] = jnp.zeros_like(acc)

    def backward_plane(p, carry):
        plane_rows = rows_at(p * PLANE, PLANE, PLANE)
        bias = key_bias(p * PLANE)

        def products(head):
            cols = slice(head * HD, (head + 1) * HD)
            scores = dot_nt(queries[:, cols], keys[plane_rows, cols]) + bias
            return scores, dot_nt(gout[:, cols], values[plane_rows, cols])

        def gradient(head, scores, grad_probs):
            cols = slice(head * HD, (head + 1) * HD)
            probabilities = jnp.exp2(scores - repeat(top[head], PLANE // 128))
            grad_scores = (probabilities * (grad_probs - repeat(total[head], PLANE // 128))).astype(BF16)
            acc[:, cols] += dot(grad_scores, keys[plane_rows, cols])

        made = products(0)
        for head in range(3):
            ahead = products(head + 1) if head < 2 else None
            gradient(head, *made)
            made = ahead
        return carry

    lax.fori_loop(0, 4, backward_plane, 0)

    batch = rewards_ref.shape[1]
    reward = rewards_ref[...].astype(F32)
    group = groups_ref[...].astype(F32)
    mine = iota((1, batch), 1) == x
    own_group = jnp.sum(jnp.where(mine, group, 0.0), axis=1, keepdims=True)
    own_reward = jnp.sum(jnp.where(mine, reward, 0.0), axis=1, keepdims=True)
    member = jnp.where(group == own_group, 1.0, 0.0)
    mean = jnp.sum(member * reward, axis=1, keepdims=True) / GROUP
    centered = reward - mean
    variance = jnp.sum(member * centered * centered, axis=1, keepdims=True) / GROUP
    advantage = (own_reward - mean) / (jnp.sqrt(variance) + 1.0)

    for index, recv in sq_waits:
        arrive(squares.at[index], recv)
    clip_squares = jnp.zeros((8, 128), F32)
    for b in range(8):
        clip_squares += squares[b]
    clip_squares = jnp.sum(jnp.sum(clip_squares, axis=1, keepdims=True), axis=0, keepdims=True)
    ratio = jnp.exp(-0.5 * clip_squares / count - one * rollout_ref[x])
    out_ratio[...] = jnp.broadcast_to(ratio, (8, 128))
    low_edge, high_edge = 1.0 - clip_range, 1.0 + clip_range
    inside = (ratio >= low_edge) & (ratio <= high_edge)
    active = inside | ((advantage > 0) & (ratio < low_edge)) | ((advantage < 0) & (ratio > high_edge))
    weight = jnp.where(active, -advantage * ratio / float(CLIPS), 0.0)

    gq[...] = (acc[...] * (head_scale * weight)).astype(BF16)

    for b in (0, 1):
        part = dot_nt(gq[b * ROWS : (b + 1) * ROWS, :], upb[:, 0:OWN]) * out_scale
        glow_send[b] = part.astype(BF16)
    for d in (1, 2, 3):
        other, device = y_peer(d)
        send(glow_send.at[other % 2], glow.at[y], R_LOW + d - 1, device)
    glow[y] = glow_send[yl]
    up_part = dot(jnp.transpose(low[...].astype(F32)).astype(BF16), gq[...])
    du[0, :, 768:1024] = up_part[:, 0:256]
    du[1, :, 768:896] = up_part[:, 256:384]
    du[1, :, 896:1024] = jnp.zeros((128, 128), F32)
    for d in (1, 2, 3):
        arrive(glow.at[(y + 4 - d) % 4], R_LOW + d - 1)
    low_sum = jnp.zeros((ROWS, 128), F32)
    for b in range(4):
        low_sum += glow[b].astype(F32)
    low_turned = jnp.transpose(low_sum).astype(BF16)

    for half in (1, 0):
        where = (core + half) % 2
        for j in range(3):
            cols = lanes(sec * HALF + where * 768 + j * 256, 256)
            du[where, :, j * 256 : (j + 1) * 256] = dot(low_turned, normed[:, cols])
        if half == 1:
            send(du.at[where], core_recv, R_RC, other_core)
    arrive(core_recv, R_RC)
    xs[...] = (du[core] + core_recv[...]).astype(BF16)
    for d in (1, 2, 3):
        to = (x + d) % 4
        send(xs.at[rows_at(to * 32, 32, 32), :], xr.at[d - 1], R_RX + d - 1, at(sec, to, z, yl, core))
    slab = du[core, x_rows, :] + core_recv[x_rows, :]
    for d in (1, 2, 3):
        arrive(xr.at[d - 1], R_RX + d - 1)
        slab += xr[d - 1].astype(F32)
    zs[...] = slab
    for d in (1, 2, 3):
        to = (z + d) % 4
        send(zs.at[rows_at(to * 8, 8, 8), :], zr.at[d - 1], R_RZ + d - 1, at(sec, x, to, yl, core))
    z_rows = rows_at(z * 8, 8, 8)
    piece = zs[z_rows, :]
    for d in (1, 2, 3):
        arrive(zr.at[d - 1], R_RZ + d - 1)
        piece += zr[d - 1]
    yr[y] = piece
    for d in (1, 2, 3):
        send(yr.at[y], yr.at[y], R_RY + d - 1, y_peer(d)[1])
    for d in (1, 2, 3):
        arrive(yr.at[(y + 4 - d) % 4], R_RY + d - 1)
    for b in (0, 1):
        zg[z_rows, b * 768 : (b + 1) * 768] = yr[2 * b, :, 0:768] + yr[2 * b + 1, :, 0:768]
        zg[z_rows, HALF + b * 256 : HALF + (b + 1) * 256] = yr[sec * 2 + b, :, 768:1024]

    for d in (1, 2, 3):
        send(zg.at[z_rows, :], zg.at[z_rows, :], R_GZ + d - 1, at(sec, x, (z + d) % 4, yl, core))
    for d in (1, 2, 3):
        arrive(zg.at[rows_at(((z + 4 - d) % 4) * 8, 8, 8), :], R_GZ + d - 1)
    full[core, x_rows, :] = zg[...].astype(BF16)
    mine_full = full.at[core, x_rows, :]
    for d in (1, 2, 3):
        send(mine_full, mine_full, R_GX + d - 1, at(sec, (x + d) % 4, z, yl, core))
    send(mine_full, mine_full, R_GC, other_core)
    for d in (1, 2, 3):
        from_rows = rows_at(((x + 4 - d) % 4) * 32, 32, 32)
        arrive(full.at[core, from_rows, :], R_GX + d - 1)
        send(full.at[core, from_rows, :], full.at[core, from_rows, :], R_GC + d, other_core)
    for d in (0, 1, 2, 3):
        from_rows = rows_at(((x + 4 - d) % 4) * 32, 32, 32)
        arrive(full.at[1 - core, from_rows, :], R_GC + d)

    out_grad[...] = full[...]
    for copy in pending:
        copy.wait_send()


def update(grad_ref, down_ref, up_ref, ratio_ref, out_down, out_up, out_ratio):
    norm_sum = jnp.zeros((128, 256), F32)
    for b in (0, 1):
        for j in range(HALF // 256):
            part = grad_ref[b, :, j * 256 : (j + 1) * 256].astype(F32)
            norm_sum += part * part
    norm_sum = jnp.sum(jnp.sum(norm_sum, axis=1, keepdims=True), axis=0, keepdims=True)
    factor = step_length / jnp.sqrt(norm_sum * (input_scale * input_scale) + norm_eps)
    down_factor, up_factor = factor * input_scale, factor * out_scale
    for t in range(MODEL_WIDTH // 128):
        part = grad_ref[(t % 12) // 6, :, (t // 12) * 768 + (t % 6) * 128 : (t // 12) * 768 + (t % 6) * 128 + 128]
        rows = slice(t * 128, (t + 1) * 128)
        out_down[rows, :] = down_ref[rows, :] - down_factor * jnp.transpose(part.astype(F32))
    for b in (0, 1):
        for c, width in ((0, 256), (1, 128)):
            cols = slice(b * OWN + c * 256, b * OWN + c * 256 + width)
            part = grad_ref[c, :, HALF + b * 256 : HALF + b * 256 + width].astype(F32)
            out_up[:, cols] = up_ref[:, cols] - up_factor * part
    out_ratio[0] = jnp.sum(ratio_ref[0:1, 0:1])


def shards(
    trajectory, block_input, chosen, lengths, rewards, prompt_group_index, rollout_log_probability,
    timestep_norm_shift, patch_input_weight, frozen_query_matrix, frozen_key_matrix, frozen_value_matrix,
    velocity_output_weight, adapter_down_factor, adapter_up_factor,
):
    vmem = pl.BlockSpec(memory_space=pltpu.VMEM)
    smem = pl.BlockSpec(memory_space=pltpu.SMEM)
    hbm = pl.BlockSpec(memory_space=pl.ANY)
    V = pltpu.VMEM
    scratch = [
        V((STEPS, 2, MODEL_WIDTH), F32),
        V((PATCH, MODEL_WIDTH), BF16),
        V((PATCH, OWN), BF16),
        V((MODEL_WIDTH, ADAPTER_RANK), F32),
        V((ADAPTER_RANK, 2 * OWN), F32),
        V((ROWS, MODEL_WIDTH), BF16),
        V((MODEL_WIDTH, 2 * OWN), BF16),
        V((MODEL_WIDTH, 2 * OWN), BF16),
        V((MODEL_WIDTH, 2 * OWN), BF16),
        V((MODEL_WIDTH, ADAPTER_RANK), BF16),
        V((ADAPTER_RANK, 2 * OWN), BF16),
        V((ROWS, MODEL_WIDTH), F32),
        V((ROWS, MODEL_WIDTH), BF16),
        V((CLIPS, 2, PAIRS, 128), BF16),
        V((2, 2, 128, 128), BF16),
        V((ROWS, 2 * OWN), BF16),
        V((ROWS, 2 * OWN), BF16),
        V((ROWS, 2 * OWN), BF16),
        V((4 * PLANE, OWN), BF16),
        V((4 * PLANE, OWN), BF16),
        V((2 * ROWS, OWN), BF16),
        V((2 * ROWS, ADAPTER_RANK), BF16),
        V((3, 2 * ROWS, 128), F32),
        V((3, 2 * ROWS, 128), F32),
        V((2 * ROWS, OWN), F32),
        V((2 * ROWS, OWN), BF16),
        V((4, ROWS, 128), BF16),
        V((8, 8, 128), F32),
        V((2 * ROWS, OWN), BF16),
        V((2 * ROWS, OWN), BF16),
        V((2, ROWS, 128), BF16),
        V((4, ROWS, 128), BF16),
        V((2, 128, 1024), F32),
        V((128, 1024), F32),
        V((128, 1024), BF16),
        V((3, 32, 1024), BF16),
        V((32, 1024), F32),
        V((3, 8, 1024), F32),
        V((4, 8, 1024), F32),
        V((32, 2048), F32),
        V((2, 128, 2048), BF16),
        pltpu.SemaphoreType.DMA((N_SEND,)),
        pltpu.SemaphoreType.DMA((N_RECV,)),
        pltpu.SemaphoreType.DMA((16,)),
    ]
    gradients, ratio = pl.pallas_call(
        body,
        out_shape=(
            jax.ShapeDtypeStruct((2, ADAPTER_RANK, 2048), BF16),
            jax.ShapeDtypeStruct((8, 128), F32),
        ),
        in_specs=[smem] * 3 + [vmem] * 3 + [hbm] * 9,
        out_specs=(vmem, vmem),
        scratch_shapes=scratch,
        compiler_params=pltpu.CompilerParams(
            collective_id=0, has_side_effects=True, vmem_limit_bytes=60 * 1024 * 1024
        ),
        cost_estimate=pl.CostEstimate(flops=12_000_000_000, bytes_accessed=24_000_000, transcendentals=13_000_000),
        name="policy_step",
    )(
        chosen, lengths, rollout_log_probability,
        trajectory.reshape(STEPS + 1, CLIPS, PAIRS, 128),
        rewards.reshape(1, -1), prompt_group_index.reshape(1, -1), timestep_norm_shift, patch_input_weight,
        velocity_output_weight.T, adapter_down_factor, adapter_up_factor,
        block_input.reshape(ROWS, MODEL_WIDTH), frozen_query_matrix, frozen_key_matrix, frozen_value_matrix,
    )
    return pl.pallas_call(
        update,
        out_shape=(
            jax.ShapeDtypeStruct((MODEL_WIDTH, ADAPTER_RANK), F32),
            jax.ShapeDtypeStruct((ADAPTER_RANK, 2 * OWN), F32),
            jax.ShapeDtypeStruct((1,), F32),
        ),
        in_specs=[vmem] * 4,
        out_specs=(vmem, vmem, smem),
        compiler_params=pltpu.CompilerParams(vmem_limit_bytes=32 * 1024 * 1024),
        name="update",
    )(gradients, adapter_down_factor, adapter_up_factor, ratio)


def solution(mesh):
    return jax.shard_map(
        shards,
        mesh=mesh,
        in_specs=(
            P(None, None, "seq", "dp", None),
            P("dp", "seq", None),
            P(), P(), P(), P(), P(), P(), P(),
            P(None, "section"),
            P(None, "section"),
            P(None, "section"),
            P("section", None),
            P(),
            P(None, "section"),
        ),
        out_specs=(P(), P(None, "section"), P("dp")),
        check_vma=False,
    )
```

```python
import functools
import math

import jax
import jax.numpy as jnp
from jax import lax
from jax.experimental import pallas as pl
from jax.experimental.pallas import tpu as pltpu
from jax.sharding import PartitionSpec as P

MESH = pl.DeviceIdType.MESH
F32 = jnp.float32
BF16 = jnp.bfloat16

MODEL_WIDTH = 3072
HD = 128
ADAPTER_RANK = 128
STEPS = 4
GROUP = 16
PATCH = 64
CLIPS = 4
ROWS = 256
PAIRS = 32
OWN = 384
PLANE = 1024
HALF = 1536

noise_level = 0.8
clip_range = 0.2
step_length = 256.0
norm_eps = 1e-06
masked_score = -1e30
step_size = 1.0 / (STEPS + 1)
input_scale = 1.0 / math.sqrt(MODEL_WIDTH)
out_scale = 1.0 / math.sqrt(ADAPTER_RANK)
head_scale = 1.0 / math.sqrt(HD)
query_scale = head_scale * math.log2(math.e)

NT = (((1,), (1,)), ((), ()))

R_X = 0
R_PAIR = 3
R_Z = 8
R_FAR = 16
R_CORE = 20
R_VEL = 36
R_SQ = 39
R_LOW = 43
R_RC = 46
R_RS = 47
R_RY = 62
R_AG = 65
R_GC = 80
N_RECV = 96
N_SEND = 112
AROUND = sorted(
    ((dx, dz) for dx in range(4) for dz in range(4) if dx or dz),
    key=lambda d: min(d[0], 4 - d[0]) + min(d[1], 4 - d[1]),
)


def dot(a, b):
    return jnp.dot(a, b, preferred_element_type=F32)


def dot_nt(a, b):
    return lax.dot_general(a, b, NT, preferred_element_type=F32)


def iota(shape, dim):
    return lax.broadcasted_iota(jnp.int32, shape, dim)


def lanes(start, size):
    return pl.ds(pl.multiple_of(start, 128), size)


def rows_at(start, size, unit=256):
    return pl.ds(pl.multiple_of(start, unit), size)


def body(
    chosen_ref, lengths_ref, rollout_ref,
    traj_ref, rewards_ref, groups_ref,
    shift_hbm, patch_hbm, wout_hbm, down_hbm, up_hbm, x_hbm, wq_hbm, wk_hbm, wv_hbm,
    out_grad, out_ratio,
    shift_ref, patch_ref, wout_ref, down_ref, up_ref, xin, wk, wv, downb, upb, emb, normed,
    sel, latents, stage_k, stage_v, stage_q, keys, values, queries, low,
    top, peaks, probs, total, acc, attn, vel, squares, both, gout, gq, glow_send, glow,
    du, core_recv, xs, xr, yr, full,
    send_sem, recv_sem, local_sem,
):
    sec = lax.axis_index("section")
    x = lax.axis_index("dp")
    seq = lax.axis_index("seq")
    z = seq // 4
    yl = (seq // 2) % 2
    core = seq % 2
    y = sec * 2 + yl

    def at(sec_, x_, z_, yl_, core_):
        return (sec_, x_, z_ * 4 + yl_ * 2 + core_)

    def y_peer(step):
        other = (y + step) % 4
        return other, at(other // 2, x, z, other % 2, core)

    other_core = at(sec, x, z, yl, 1 - core)
    partner = at(sec, x, z, 1 - yl, core)
    z_up = at(sec, x, (z + 1) % 4, yl, core)
    z_down = at(sec, x, (z + 3) % 4, yl, core)

    pending = []

    def descriptor(src, dst, send_index, recv_index, device):
        return pltpu.make_async_remote_copy(
            src_ref=src, dst_ref=dst, send_sem=send_sem.at[send_index], recv_sem=recv_sem.at[recv_index],
            device_id=device, device_id_type=MESH,
        )

    def send(src, dst, recv_index, device):
        copy = descriptor(src, dst, len(pending), recv_index, device)
        copy.start()
        pending.append(copy)

    def arrive(dst, recv_index):
        descriptor(dst, dst, 0, recv_index, other_core).wait_recv()

    loads = []

    def load(src, dst):
        copy = pltpu.make_async_copy(src, dst, local_sem.at[len(loads)])
        copy.start()
        loads.append(copy)
        return copy


    peers = [at(sec, (x + dx) % 4, (z + dz) % 4, yl, core) for dx, dz in AROUND]
    peers += [y_peer(d)[1] for d in (1, 2, 3)]
    peers += [other_core]
    barrier = pltpu.get_barrier_semaphore()
    for peer in peers:
        pl.semaphore_signal(barrier, inc=1, device_id=peer, device_id_type=MESH)

    load_x = [load(x_hbm, xin), load(patch_hbm, patch_ref), load(shift_hbm, shift_ref)]
    own_cols, other_cols = lanes(yl * OWN, OWN), lanes((1 - yl) * OWN, OWN)

    def load_weight(src, dst):
        return load(src.at[:, own_cols], dst.at[:, 0:OWN]), load(src.at[:, other_cols], dst.at[:, OWN : 2 * OWN])

    load_w = [load_weight(wk_hbm, wk), load_weight(wv_hbm, wv)]
    load_adapter = [load(down_hbm, down_ref), load(up_hbm, up_ref), load(wout_hbm.at[:, own_cols], wout_ref)]

    for c in range(CLIPS):
        sel[c, 0] = traj_ref[chosen_ref[c], c]
        sel[c, 1] = traj_ref[chosen_ref[c] + 1, c]
    pl.semaphore_wait(barrier, len(peers))
    x_rows = rows_at(x * PAIRS, PAIRS, PAIRS)
    for d in (1, 2, 3):
        to = (x + d) % 4
        send(sel.at[to], latents.at[yl, :, x_rows, :], R_X + d - 1, at(sec, to, z, yl, core))
    latents[yl, :, x_rows, :] = sel[x]

    chosen = chosen_ref[x]
    length = lengths_ref[x]
    one = jnp.ones((1, 1), F32)
    spread = noise_level * jnp.sqrt(step_size * (1.0 - one * chosen.astype(F32) * step_size))
    count = one * (length * PATCH).astype(F32)

    expand = jnp.where((iota((ROWS, 128), 0) >> 1) == iota((ROWS, 128), 1), 1.0, 0.0).astype(BF16)
    own_half = (iota((ROWS, 128), 1) >> 6) == (iota((ROWS, 128), 0) & 1)

    def token_rows(pairs):
        return jnp.where(own_half, dot(expand, pairs), 0.0).astype(BF16)

    def fold(offset, width):
        source = (iota((128, width), 0) & 63) + offset
        return jnp.where(source == iota((128, width), 1), 1.0, 0.0).astype(BF16)

    for d in (1, 2, 3):
        src_rows = rows_at(((x + 4 - d) % 4) * PAIRS, PAIRS, PAIRS)
        arrive(latents.at[yl, :, src_rows, :], R_X + d - 1)
    send(latents.at[yl], latents.at[yl], R_PAIR + 4, partner)

    now_tokens = dot(token_rows(latents[yl, 0]), fold(0, 64)).astype(BF16)
    for copy in load_x:
        copy.wait()
    squares_sum = jnp.zeros((ROWS, 1), F32)
    chunk = 512
    for j in range(MODEL_WIDTH // chunk):
        cols = slice(j * chunk, (j + 1) * chunk)
        part = xin[:, cols].astype(F32) + dot(now_tokens, patch_ref[:, cols])
        emb[:, cols] = part
        squares_sum += jnp.sum(part * part, axis=1, keepdims=True)
    inverse = lax.rsqrt(squares_sum * (1.0 / MODEL_WIDTH) + norm_eps)
    for j in range(MODEL_WIDTH // chunk):
        cols = slice(j * chunk, (j + 1) * chunk)
        shift = shift_ref[chosen, 0:1, cols]
        scale = shift_ref[chosen, 1:2, cols]
        normed[:, cols] = (emb[:, cols] * inverse * (1.0 + scale) + shift).astype(BF16)

    seq_own = seq * ROWS
    seq_pair = (seq + 2 - 4 * yl) * ROWS

    def block(ref, z_, yl_, core_):
        return ref.at[rows_at((z_ * 4 + yl_ * 2 + core_) * ROWS, ROWS), :]

    def project(weight, loaded, stage, extra=None, scale=None):
        for copy in loaded:
            copy.wait()

        def step(n, carry):
            cols = lanes(n * 256, 256)
            part = dot(normed[...], weight[:, cols])
            if extra is not None:
                part = (part + dot(extra, upb[:, cols]) * out_scale) * scale
            stage[:, cols] = part.astype(BF16)
            return carry

        lax.fori_loop(0, 3, step, 0)

    store = (keys, values)

    def core_index(plane, pair, kv):
        return R_CORE + plane * 4 + pair * 2 + kv

    def to_core(plane, pair, kv):
        z_ = (z + plane) % 4
        yl_ = yl if pair == 0 else 1 - yl
        send(block(store[kv], z_, yl_, core), block(store[kv], z_, yl_, core), core_index(plane, pair, kv), other_core)

    def from_core(plane):
        z_ = (z + plane) % 4
        for pair in (0, 1):
            yl_ = yl if pair == 0 else 1 - yl
            for kv in (0, 1):
                arrive(block(store[kv], z_, yl_, 1 - core), core_index(plane, pair, kv))

    def z_index(pair, kv, above):
        return R_Z + pair * 4 + kv * 2 + above

    def to_z(pair, kv):
        src = block(store[kv], z, yl if pair == 0 else 1 - yl, core)
        send(src, src, z_index(pair, kv, 0), z_up)
        send(src, src, z_index(pair, kv, 1), z_down)

    def from_z(pair, kv, above):
        z_ = (z + 1) % 4 if above else (z + 3) % 4
        src = block(store[kv], z_, yl if pair == 0 else 1 - yl, core)
        arrive(src, z_index(pair, kv, above))
        if kv == 0 and not above:
            send(src, src, R_FAR + pair * 2 + kv, z_up)
        if kv == 1 and above:
            send(src, src, R_FAR + pair * 2 + kv, z_down)
        to_core(1 if above else 3, pair, kv)

    def from_far(pair, kv):
        arrive(block(store[kv], (z + 2) % 4, yl if pair == 0 else 1 - yl, core), R_FAR + pair * 2 + kv)
        to_core(2, pair, kv)

    own_block = rows_at(seq_own, ROWS)
    for kv, (weight, stage) in enumerate(((wk, stage_k), (wv, stage_v))):
        project(weight, load_w[kv], stage)
        send(stage.at[:, OWN : 2 * OWN], block(store[kv], z, yl, core), R_PAIR + kv, partner)
        store[kv][own_block, :] = stage[:, 0:OWN]
        to_z(0, kv)
        to_core(0, 0, kv)
        if kv == 0:
            load_w.append(load_weight(wq_hbm, wk))
    own_rows = rows_at(yl * ROWS, ROWS)
    pair_rows = rows_at((1 - yl) * ROWS, ROWS)
    for copy in load_adapter:
        copy.wait()
    downb[...] = down_ref[...].astype(BF16)
    upb[:, 0:OWN] = up_ref[:, own_cols].astype(BF16)
    upb[:, OWN : 2 * OWN] = up_ref[:, other_cols].astype(BF16)
    low_own = (dot(normed[...], downb[...]) * input_scale).astype(BF16)
    low[own_rows, :] = low_own
    project(wk, load_w[2], stage_q, low_own, query_scale)
    send(stage_q.at[:, OWN : 2 * OWN], queries.at[own_rows, :], R_PAIR + 2, partner)
    queries[own_rows, :] = stage_q[:, 0:OWN]
    send(low.at[own_rows, :], low.at[own_rows, :], R_PAIR + 3, partner)
    for kv in (0, 1):
        arrive(block(store[kv], z, 1 - yl, core), R_PAIR + kv)
        to_z(1, kv)
        to_core(0, 1, kv)

    def key_bias(start):
        return jnp.where(start + iota((1, PLANE), 1) < length, 0.0, masked_score)

    def repeat(stat, count):
        return jnp.concatenate([stat] * count, axis=1)

    def fold_lanes(op, tile):
        out = tile[:, 0:128]
        for j in range(1, tile.shape[1] // 128):
            out = op(out, tile[:, j * 128 : (j + 1) * 128])
        return out

    def forward_plane(plane):
        start = ((z + plane) % 4) * PLANE
        plane_rows = rows_at(start, PLANE, PLANE)
        bias = key_bias(start)
        first = plane == 0
        tiles = [(h, slice(h * HD, (h + 1) * HD), slice(b * ROWS, (b + 1) * ROWS)) for h in range(3) for b in (0, 1)]

        def score(tile):
            _, cols, rows = tile
            return dot_nt(queries[rows, cols], keys[plane_rows, cols]) + bias

        def softmax(tile, scores):
            head, cols, rows = tile
            peak = jnp.max(fold_lanes(jnp.maximum, scores), axis=1, keepdims=True)
            peak = jnp.broadcast_to(peak, (ROWS, 128))
            if not first:
                before = top[head, rows, :]
                peak = jnp.maximum(peak, before)
            exp_scores = jnp.exp2(scores - repeat(peak, PLANE // 128))
            sums = fold_lanes(jnp.add, exp_scores)
            kept = exp_scores.astype(BF16)
            probs[plane, head, rows, :] = kept
            weighted = dot(kept, values[plane_rows, cols])
            if not first:
                decay = jnp.exp2(before - peak)
                sums += decay * total[head, rows, :]
                weighted += decay * acc[rows, cols]
            top[head, rows, :] = peak
            peaks[plane, head, rows, :] = peak
            total[head, rows, :] = sums
            acc[rows, cols] = weighted

        scores = score(tiles[0])
        for i, tile in enumerate(tiles):
            ahead = score(tiles[i + 1]) if i + 1 < len(tiles) else None
            softmax(tile, scores)
            scores = ahead

    for kv in (0, 1):
        for above in (0, 1):
            from_z(0, kv, above)
    arrive(queries.at[pair_rows, :], R_PAIR + 2)
    from_core(0)
    forward_plane(0)
    for kv in (0, 1):
        for above in (0, 1):
            from_z(1, kv, above)
    from_core(1)
    forward_plane(1)
    from_far(0, 0)
    from_far(0, 1)
    from_core(3)
    forward_plane(3)
    from_far(1, 0)
    from_far(1, 1)
    from_core(2)
    forward_plane(2)

    def finish_head(i, carry):
        head = i // 2
        cols = lanes(head * HD, HD)
        rows = rows_at((i % 2) * ROWS, ROWS)
        sums = jnp.broadcast_to(jnp.sum(total[head, rows, :], axis=1, keepdims=True), (ROWS, 128))
        attn[rows, cols] = (acc[rows, cols] / sums).astype(BF16)
        top[head, rows, :] = top[head, rows, :] + jnp.log(sums) * math.log2(math.e)
        return carry

    lax.fori_loop(0, 6, finish_head, 0)

    blank = jnp.zeros((PATCH, OWN), BF16)
    wide = [jnp.concatenate([wout_ref[...], blank], axis=0), jnp.concatenate([blank, wout_ref[...]], axis=0)]
    partial = dot_nt(attn[0:ROWS, :], wide[0]) + dot_nt(attn[ROWS : 2 * ROWS, :], wide[1])
    vel[y] = partial.astype(BF16)
    for d in (1, 2, 3):
        send(vel.at[y], vel.at[y], R_VEL + d - 1, y_peer(d)[1])
    arrive(latents.at[1 - yl], R_PAIR + 4)
    arrive(low.at[pair_rows, :], R_PAIR + 3)
    moved = jnp.zeros((ROWS, 128), F32)
    for b in (0, 1):
        moved += dot(token_rows(latents[b, 1]), fold(PATCH * b, 128))
        moved -= dot(token_rows(latents[b, 0]), fold(PATCH * b, 128))
    lane_block = iota((ROWS, 128), 1) >> 6
    position = (z * 4 + lane_block * 2 + core) * ROWS + iota((ROWS, 128), 0)
    live = position < length
    for d in (1, 2, 3):
        arrive(vel.at[(y + 4 - d) % 4], R_VEL + d - 1)
    velocity = jnp.zeros((ROWS, 128), F32)
    for b in range(4):
        velocity += vel[b].astype(F32)
    zscore = (moved + step_size * velocity) / spread
    own_squares = jnp.where(live, zscore * zscore, 0.0)
    squares[z] = jnp.sum(own_squares.reshape(ROWS // 8, 8, 128), axis=0)
    for d in (1, 2, 3):
        send(squares.at[z], squares.at[z], R_SQ + d - 1, at(sec, x, (z + d) % 4, yl, core))

    grad_vel = jnp.where(live, -zscore * step_size / (spread * count), 0.0).astype(BF16)
    for b in (0, 1):
        gout[b * ROWS : (b + 1) * ROWS, :] = dot(grad_vel, wide[b]).astype(BF16)

    for head in range(3):
        cols = slice(head * HD, (head + 1) * HD)
        delta = jnp.sum(gout[:, cols].astype(F32) * attn[:, cols].astype(F32), axis=1, keepdims=True)
        total[head] = jnp.broadcast_to(delta, (2 * ROWS, 128))
    acc[...] = jnp.zeros_like(acc)

    def backward_plane(plane, carry):
        plane_rows = rows_at(((z + plane) % 4) * PLANE, PLANE, PLANE)

        def product(head):
            cols = slice(head * HD, (head + 1) * HD)
            return dot_nt(gout[:, cols], values[plane_rows, cols])

        def gradient(head, grad_probs):
            cols = slice(head * HD, (head + 1) * HD)
            scale = jnp.exp2(peaks[plane, head] - top[head])
            grad_scores = (grad_probs - repeat(total[head], PLANE // 128)) * repeat(scale, PLANE // 128)
            grad_scores = (probs[plane, head].astype(F32) * grad_scores).astype(BF16)
            acc[:, cols] += dot(grad_scores, keys[plane_rows, cols])

        made = product(0)
        for head in range(3):
            ahead = product(head + 1) if head < 2 else None
            gradient(head, made)
            made = ahead
        return carry

    lax.fori_loop(0, 2, backward_plane, 0)
    for d in (1, 2, 3):
        arrive(squares.at[(z + 4 - d) % 4], R_SQ + d - 1)
    plane_squares = jnp.zeros((8, 128), F32)
    for b in range(4):
        plane_squares += squares[b]
    both[core] = plane_squares
    send(both.at[core], both.at[core], R_SQ + 3, other_core)
    lax.fori_loop(2, 4, backward_plane, 0)

    batch = rewards_ref.shape[1]
    reward = rewards_ref[...].astype(F32)
    group = groups_ref[...].astype(F32)
    mine = iota((1, batch), 1) == x
    own_group = jnp.sum(jnp.where(mine, group, 0.0), axis=1, keepdims=True)
    own_reward = jnp.sum(jnp.where(mine, reward, 0.0), axis=1, keepdims=True)
    member = jnp.where(group == own_group, 1.0, 0.0)
    mean = jnp.sum(member * reward, axis=1, keepdims=True) / GROUP
    centered = reward - mean
    variance = jnp.sum(member * centered * centered, axis=1, keepdims=True) / GROUP
    advantage = (own_reward - mean) / (jnp.sqrt(variance) + 1.0)

    arrive(both.at[1 - core], R_SQ + 3)
    clip_squares = both[0] + both[1]
    clip_squares = jnp.sum(jnp.sum(clip_squares, axis=1, keepdims=True), axis=0, keepdims=True)
    ratio = jnp.exp(-0.5 * clip_squares / count - one * rollout_ref[x])
    out_ratio[0] = jnp.sum(ratio)
    low_edge, high_edge = 1.0 - clip_range, 1.0 + clip_range
    inside = (ratio >= low_edge) & (ratio <= high_edge)
    active = inside | ((advantage > 0) & (ratio < low_edge)) | ((advantage < 0) & (ratio > high_edge))
    weight = jnp.where(active, -advantage * ratio / float(CLIPS), 0.0)

    gq[...] = (acc[...] * (head_scale * weight)).astype(BF16)

    for b in (0, 1):
        part = dot_nt(gq[b * ROWS : (b + 1) * ROWS, :], upb[:, 0:OWN]) * out_scale
        glow_send[b] = part.astype(BF16)
    for d in (1, 2, 3):
        other, device = y_peer(d)
        send(glow_send.at[other % 2], glow.at[y], R_LOW + d - 1, device)
    glow[y] = glow_send[yl]
    up_part = dot(jnp.transpose(low[...].astype(F32)).astype(BF16), gq[...])
    du[0, :, 768:1024] = up_part[:, 0:256]
    du[1, :, 768:896] = up_part[:, 256:384]
    du[1, :, 896:1024] = jnp.zeros((128, 128), F32)
    for d in (1, 2, 3):
        arrive(glow.at[(y + 4 - d) % 4], R_LOW + d - 1)
    low_sum = jnp.zeros((ROWS, 128), F32)
    for b in range(4):
        low_sum += glow[b].astype(F32)
    low_turned = jnp.transpose(low_sum).astype(BF16)

    for half in (1, 0):
        where = (core + half) % 2
        for j in range(3):
            cols = lanes(sec * HALF + where * 768 + j * 256, 256)
            du[where, :, j * 256 : (j + 1) * 256] = dot(low_turned, normed[:, cols])
        if half == 1:
            send(du.at[where], core_recv, R_RC, other_core)
    arrive(core_recv, R_RC)
    xs[...] = (du[core] + core_recv[...]).astype(BF16)

    def unit(x_, z_):
        index = x_ * 4 + z_
        return rows_at((index // 2) * 16, 16, 16), lanes((index % 2) * 512, 512)

    def unit_rows(x_, z_):
        index = x_ * 4 + z_
        return index % 2, rows_at((index // 2) * 16, 16, 16)

    for i, (dx, dz) in reversed(list(enumerate(AROUND))):
        x_, z_ = (x + dx) % 4, (z + dz) % 4
        rows, cols = unit(x_, z_)
        send(xs.at[rows, cols], xr.at[i], R_RS + i, at(sec, x_, z_, yl, core))
    rows, cols = unit(x, z)
    piece = du[core, rows, cols] + core_recv[rows, cols]
    for i in range(len(AROUND)):
        arrive(xr.at[i], R_RS + i)
        piece += xr[i].astype(F32)
    yr[y] = piece
    for d in (1, 2, 3):
        send(yr.at[y], yr.at[y], R_RY + d - 1, y_peer(d)[1])
    for d in (1, 2, 3):
        arrive(yr.at[(y + 4 - d) % 4], R_RY + d - 1)
    down_sums = [yr[2 * b] + yr[2 * b + 1] for b in (0, 1)]
    first_half = jnp.concatenate(down_sums, axis=1)
    second_half = jnp.concatenate(
        [part[:, 0:256] for part in down_sums] + [yr[sec * 2 + b, :, 256:512] for b in (0, 1)], axis=1
    )
    half, rows = unit_rows(x, z)
    full[core, half, rows, :] = jnp.where(half == 0, first_half, second_half).astype(BF16)

    own_unit = full.at[core, half, rows, :]
    for i, (dx, dz) in reversed(list(enumerate(AROUND))):
        send(own_unit, own_unit, R_AG + i, at(sec, (x + dx) % 4, (z + dz) % 4, yl, core))
    send(own_unit, own_unit, R_GC + 15, other_core)
    sources = [unit_rows((x + 4 - dx) % 4, (z + 4 - dz) % 4) for dx, dz in AROUND]
    for i, (half_, rows_) in enumerate(sources):
        arrived_unit = full.at[core, half_, rows_, :]
        arrive(arrived_unit, R_AG + i)
        send(arrived_unit, arrived_unit, R_GC + i, other_core)
    for i, (half_, rows_) in enumerate(sources + [(half, rows)]):
        arrive(full.at[1 - core, half_, rows_, :], R_GC + i)

    load(full, out_grad).wait()
    for copy in pending:
        copy.wait_send()


def update(grad_ref, down_ref, up_ref, ratio_ref, out_down, out_up, out_ratio):
    norm_sum = jnp.zeros((128, 256), F32)
    for core in (0, 1):
        for half, width in ((0, 1024), (1, 512)):
            for j in range(width // 256):
                part = grad_ref[core, half, :, j * 256 : (j + 1) * 256].astype(F32)
                norm_sum += part * part
    norm_sum = jnp.sum(jnp.sum(norm_sum, axis=1, keepdims=True), axis=0, keepdims=True)
    factor = step_length / jnp.sqrt(norm_sum * (input_scale * input_scale) + norm_eps)
    down_factor, up_factor = factor * input_scale, factor * out_scale
    for t in range(MODEL_WIDTH // 128):
        sec, core, j = t // 12, (t % 12) // 6, t % 6
        half, start = (0, sec * 512 + j * 128) if j < 4 else (1, sec * 256 + (j - 4) * 128)
        part = grad_ref[core, half, :, start : start + 128].astype(F32)
        rows = slice(t * 128, (t + 1) * 128)
        out_down[rows, :] = down_ref[rows, :] - down_factor * jnp.transpose(part)
    for b in (0, 1):
        for core, width in ((0, 256), (1, 128)):
            cols = slice(b * OWN + core * 256, b * OWN + core * 256 + width)
            part = grad_ref[core, 1, :, 512 + b * 256 : 512 + b * 256 + width].astype(F32)
            out_up[:, cols] = up_ref[:, cols] - up_factor * part
    out_ratio[0] = ratio_ref[0]


def shards(
    trajectory, block_input, chosen, lengths, rewards, prompt_group_index, rollout_log_probability,
    timestep_norm_shift, patch_input_weight, frozen_query_matrix, frozen_key_matrix, frozen_value_matrix,
    velocity_output_weight, adapter_down_factor, adapter_up_factor,
):
    vmem = pl.BlockSpec(memory_space=pltpu.VMEM)
    smem = pl.BlockSpec(memory_space=pltpu.SMEM)
    hbm = pl.BlockSpec(memory_space=pl.ANY)
    V = pltpu.VMEM
    scratch = [
        V((STEPS, 2, MODEL_WIDTH), F32),
        V((PATCH, MODEL_WIDTH), BF16),
        V((PATCH, OWN), BF16),
        V((MODEL_WIDTH, ADAPTER_RANK), F32),
        V((ADAPTER_RANK, 2 * OWN), F32),
        V((ROWS, MODEL_WIDTH), BF16),
        V((MODEL_WIDTH, 2 * OWN), BF16),
        V((MODEL_WIDTH, 2 * OWN), BF16),
        V((MODEL_WIDTH, ADAPTER_RANK), BF16),
        V((ADAPTER_RANK, 2 * OWN), BF16),
        V((ROWS, MODEL_WIDTH), F32),
        V((ROWS, MODEL_WIDTH), BF16),
        V((CLIPS, 2, PAIRS, 128), BF16),
        V((2, 2, 128, 128), BF16),
        V((ROWS, 2 * OWN), BF16),
        V((ROWS, 2 * OWN), BF16),
        V((ROWS, 2 * OWN), BF16),
        V((4 * PLANE, OWN), BF16),
        V((4 * PLANE, OWN), BF16),
        V((2 * ROWS, OWN), BF16),
        V((2 * ROWS, ADAPTER_RANK), BF16),
        V((3, 2 * ROWS, 128), F32),
        V((4, 3, 2 * ROWS, 128), F32),
        V((4, 3, 2 * ROWS, PLANE), BF16),
        V((3, 2 * ROWS, 128), F32),
        V((2 * ROWS, OWN), F32),
        V((2 * ROWS, OWN), BF16),
        V((4, ROWS, 128), BF16),
        V((4, 8, 128), F32),
        V((2, 8, 128), F32),
        V((2 * ROWS, OWN), BF16),
        V((2 * ROWS, OWN), BF16),
        V((2, ROWS, 128), BF16),
        V((4, ROWS, 128), BF16),
        V((2, 128, 1024), F32),
        V((128, 1024), F32),
        V((128, 1024), BF16),
        V((15, 16, 512), BF16),
        V((4, 16, 512), F32),
        V((2, 2, 128, 1024), BF16),
        pltpu.SemaphoreType.DMA((N_SEND,)),
        pltpu.SemaphoreType.DMA((N_RECV,)),
        pltpu.SemaphoreType.DMA((16,)),
    ]
    gradients, ratio = pl.pallas_call(
        body,
        out_shape=(
            jax.ShapeDtypeStruct((2, 2, ADAPTER_RANK, 1024), BF16),
            jax.ShapeDtypeStruct((1,), F32),
        ),
        in_specs=[smem] * 3 + [vmem] * 3 + [hbm] * 9,
        out_specs=(hbm, smem),
        scratch_shapes=scratch,
        compiler_params=pltpu.CompilerParams(
            collective_id=0, has_side_effects=True, vmem_limit_bytes=60 * 1024 * 1024
        ),
        cost_estimate=pl.CostEstimate(flops=12_000_000_000, bytes_accessed=24_000_000, transcendentals=13_000_000),
        name="policy_step",
    )(
        chosen, lengths, rollout_log_probability,
        trajectory.reshape(STEPS + 1, CLIPS, PAIRS, 128),
        rewards.reshape(1, -1), prompt_group_index.reshape(1, -1), timestep_norm_shift, patch_input_weight,
        velocity_output_weight.T, adapter_down_factor, adapter_up_factor,
        block_input.reshape(ROWS, MODEL_WIDTH), frozen_query_matrix, frozen_key_matrix, frozen_value_matrix,
    )
    return pl.pallas_call(
        update,
        out_shape=(
            jax.ShapeDtypeStruct((MODEL_WIDTH, ADAPTER_RANK), F32),
            jax.ShapeDtypeStruct((ADAPTER_RANK, 2 * OWN), F32),
            jax.ShapeDtypeStruct((1,), F32),
        ),
        in_specs=[vmem] * 3 + [smem],
        out_specs=(vmem, vmem, smem),
        compiler_params=pltpu.CompilerParams(vmem_limit_bytes=32 * 1024 * 1024),
        name="update",
    )(gradients, adapter_down_factor, adapter_up_factor, ratio)


def solution(mesh):
    return jax.shard_map(
        shards,
        mesh=mesh,
        in_specs=(
            P(None, None, "seq", "dp", None),
            P("dp", "seq", None),
            P(), P(), P(), P(), P(), P(), P(),
            P(None, "section"),
            P(None, "section"),
            P(None, "section"),
            P("section", None),
            P(),
            P(None, "section"),
        ),
        out_specs=(P(), P(None, "section"), P("dp")),
        check_vma=False,
    )
```

```python
import functools
import math

import jax
import jax.numpy as jnp
from jax import lax
from jax.experimental import pallas as pl
from jax.experimental.pallas import tpu as pltpu
from jax.sharding import PartitionSpec as P

MESH = pl.DeviceIdType.MESH
F32 = jnp.float32
BF16 = jnp.bfloat16

MODEL_WIDTH = 3072
HD = 128
ADAPTER_RANK = 128
STEPS = 4
GROUP = 16
PATCH = 64
CLIPS = 4
ROWS = 256
PAIRS = 32
OWN = 384
PLANE = 1024
HALF = 1536

noise_level = 0.8
clip_range = 0.2
step_length = 256.0
norm_eps = 1e-06
masked_score = -1e30
step_size = 1.0 / (STEPS + 1)
input_scale = 1.0 / math.sqrt(MODEL_WIDTH)
out_scale = 1.0 / math.sqrt(ADAPTER_RANK)
head_scale = 1.0 / math.sqrt(HD)
query_scale = head_scale * math.log2(math.e)

NT = (((1,), (1,)), ((), ()))

R_X = 0
R_PAIR = 3
R_Z = 8
R_FAR = 16
R_CORE = 20
R_VEL = 36
R_SQ = 39
R_LOW = 43
R_RC = 46
R_S1 = 47
R_S2 = 53
R_RY = 59
R_G1 = 62
R_G2 = 68
R_GC = 74
N_RECV = 82
N_SEND = 96


def dot(a, b):
    return jnp.dot(a, b, preferred_element_type=F32)


def dot_nt(a, b):
    return lax.dot_general(a, b, NT, preferred_element_type=F32)


def iota(shape, dim):
    return lax.broadcasted_iota(jnp.int32, shape, dim)


def lanes(start, size):
    return pl.ds(pl.multiple_of(start, 128), size)


def rows_at(start, size, unit=256):
    return pl.ds(pl.multiple_of(start, unit), size)


def body(
    chosen_ref, lengths_ref, rollout_ref,
    traj_ref, rewards_ref, groups_ref,
    shift_hbm, patch_hbm, wout_hbm, down_hbm, up_hbm, x_hbm, wq_hbm, wk_hbm, wv_hbm,
    out_grad, out_ratio,
    shift_ref, patch_ref, wout_ref, down_ref, up_ref, xin, wk, wv, downb, upb, emb, normed,
    sel, latents, stage_k, stage_v, stage_q, keys, values, queries, low,
    top, peaks, probs, total, acc, attn, vel, squares, both, gout, gq, glow_send, glow,
    du, core_send, core_recv, xs, xr, slabs, slabs_send, zr, yr, full,
    send_sem, recv_sem, local_sem,
):
    sec = lax.axis_index("section")
    x = lax.axis_index("dp")
    seq = lax.axis_index("seq")
    z = seq // 4
    yl = (seq // 2) % 2
    core = seq % 2
    y = sec * 2 + yl

    def at(sec_, x_, z_, yl_, core_):
        return (sec_, x_, z_ * 4 + yl_ * 2 + core_)

    def y_peer(step):
        other = (y + step) % 4
        return other, at(other // 2, x, z, other % 2, core)

    other_core = at(sec, x, z, yl, 1 - core)
    partner = at(sec, x, z, 1 - yl, core)
    z_up = at(sec, x, (z + 1) % 4, yl, core)
    z_down = at(sec, x, (z + 3) % 4, yl, core)

    pending = []

    def descriptor(src, dst, send_index, recv_index, device):
        return pltpu.make_async_remote_copy(
            src_ref=src, dst_ref=dst, send_sem=send_sem.at[send_index], recv_sem=recv_sem.at[recv_index],
            device_id=device, device_id_type=MESH,
        )

    def send(src, dst, recv_index, device):
        copy = descriptor(src, dst, len(pending), recv_index, device)
        copy.start()
        pending.append(copy)

    def arrive(dst, recv_index):
        descriptor(dst, dst, 0, recv_index, other_core).wait_recv()

    loads = []

    def load(src, dst):
        copy = pltpu.make_async_copy(src, dst, local_sem.at[len(loads)])
        copy.start()
        loads.append(copy)
        return copy


    peers = [at(sec, (x + d) % 4, z, yl, core) for d in (1, 2, 3)]
    peers += [at(sec, x, (z + d) % 4, yl, core) for d in (1, 2, 3)]
    peers += [y_peer(d)[1] for d in (1, 2, 3)]
    peers += [other_core]
    barrier = pltpu.get_barrier_semaphore()
    for peer in peers:
        pl.semaphore_signal(barrier, inc=1, device_id=peer, device_id_type=MESH)

    load_x = [load(x_hbm, xin), load(patch_hbm, patch_ref), load(shift_hbm, shift_ref)]
    own_cols, other_cols = lanes(yl * OWN, OWN), lanes((1 - yl) * OWN, OWN)

    def load_weight(src, dst):
        return load(src.at[:, own_cols], dst.at[:, 0:OWN]), load(src.at[:, other_cols], dst.at[:, OWN : 2 * OWN])

    load_w = [load_weight(wk_hbm, wk), load_weight(wv_hbm, wv)]
    load_adapter = [load(down_hbm, down_ref), load(up_hbm, up_ref), load(wout_hbm.at[:, own_cols], wout_ref)]

    for c in range(CLIPS):
        sel[c, 0] = traj_ref[chosen_ref[c], c]
        sel[c, 1] = traj_ref[chosen_ref[c] + 1, c]
    pl.semaphore_wait(barrier, len(peers))
    x_rows = rows_at(x * PAIRS, PAIRS, PAIRS)
    for d in (1, 2, 3):
        to = (x + d) % 4
        send(sel.at[to], latents.at[yl, :, x_rows, :], R_X + d - 1, at(sec, to, z, yl, core))
    latents[yl, :, x_rows, :] = sel[x]

    chosen = chosen_ref[x]
    length = lengths_ref[x]
    one = jnp.ones((1, 1), F32)
    spread = noise_level * jnp.sqrt(step_size * (1.0 - one * chosen.astype(F32) * step_size))
    count = one * (length * PATCH).astype(F32)

    def repeat(stat, count):
        return jnp.concatenate([stat] * count, axis=1)

    def fold_lanes(op, tile):
        out = tile[:, 0:128]
        for j in range(1, tile.shape[1] // 128):
            out = op(out, tile[:, j * 128 : (j + 1) * 128])
        return out

    expand = jnp.where((iota((ROWS, 128), 0) >> 1) == iota((ROWS, 128), 1), 1.0, 0.0).astype(BF16)
    own_half = (iota((ROWS, 128), 1) >> 6) == (iota((ROWS, 128), 0) & 1)

    def token_rows(pairs):
        return jnp.where(own_half, dot(expand, pairs), 0.0).astype(BF16)

    def fold(offset, width):
        source = (iota((128, width), 0) & 63) + offset
        return jnp.where(source == iota((128, width), 1), 1.0, 0.0).astype(BF16)

    for d in (1, 2, 3):
        src_rows = rows_at(((x + 4 - d) % 4) * PAIRS, PAIRS, PAIRS)
        arrive(latents.at[yl, :, src_rows, :], R_X + d - 1)
    send(latents.at[yl], latents.at[yl], R_PAIR + 4, partner)

    now_tokens = dot(token_rows(latents[yl, 0]), fold(0, 64)).astype(BF16)
    for copy in load_x:
        copy.wait()
    squares_sum = jnp.zeros((ROWS, 128), F32)
    chunk = 512
    for j in range(MODEL_WIDTH // chunk):
        cols = slice(j * chunk, (j + 1) * chunk)
        part = xin[:, cols].astype(F32) + dot(now_tokens, patch_ref[:, cols])
        emb[:, cols] = part
        squares_sum += fold_lanes(jnp.add, part * part)
    mean_square = jnp.sum(squares_sum, axis=1, keepdims=True) * (1.0 / MODEL_WIDTH)
    inverse = repeat(jnp.broadcast_to(lax.rsqrt(mean_square + norm_eps), (ROWS, 128)), chunk // 128)
    for j in range(MODEL_WIDTH // chunk):
        cols = slice(j * chunk, (j + 1) * chunk)
        shift = shift_ref[chosen, 0:1, cols]
        scale = 1.0 + shift_ref[chosen, 1:2, cols]
        normed[:, cols] = (emb[:, cols] * inverse * scale + shift).astype(BF16)

    seq_own = seq * ROWS
    seq_pair = (seq + 2 - 4 * yl) * ROWS

    def block(ref, z_, yl_, core_):
        return ref.at[rows_at((z_ * 4 + yl_ * 2 + core_) * ROWS, ROWS), :]

    def project(weight, loaded, stage, extra=None, scale=None):
        for copy in loaded:
            copy.wait()

        def step(n, carry):
            cols = lanes(n * 256, 256)
            part = dot(normed[...], weight[:, cols])
            if extra is not None:
                part = (part + dot(extra, upb[:, cols]) * out_scale) * scale
            stage[:, cols] = part.astype(BF16)
            return carry

        lax.fori_loop(0, 3, step, 0)

    store = (keys, values)

    def core_index(plane, pair, kv):
        return R_CORE + plane * 4 + pair * 2 + kv

    def to_core(plane, pair, kv):
        z_ = (z + plane) % 4
        yl_ = yl if pair == 0 else 1 - yl
        send(block(store[kv], z_, yl_, core), block(store[kv], z_, yl_, core), core_index(plane, pair, kv), other_core)

    def from_core(plane):
        z_ = (z + plane) % 4
        for pair in (0, 1):
            yl_ = yl if pair == 0 else 1 - yl
            for kv in (0, 1):
                arrive(block(store[kv], z_, yl_, 1 - core), core_index(plane, pair, kv))

    def z_index(pair, kv, above):
        return R_Z + pair * 4 + kv * 2 + above

    def to_z(pair, kv):
        src = block(store[kv], z, yl if pair == 0 else 1 - yl, core)
        send(src, src, z_index(pair, kv, 0), z_up)
        send(src, src, z_index(pair, kv, 1), z_down)

    def from_z(pair, kv, above):
        z_ = (z + 1) % 4 if above else (z + 3) % 4
        src = block(store[kv], z_, yl if pair == 0 else 1 - yl, core)
        arrive(src, z_index(pair, kv, above))
        if kv == 0 and not above:
            send(src, src, R_FAR + pair * 2 + kv, z_up)
        if kv == 1 and above:
            send(src, src, R_FAR + pair * 2 + kv, z_down)
        to_core(1 if above else 3, pair, kv)

    def from_far(pair, kv):
        arrive(block(store[kv], (z + 2) % 4, yl if pair == 0 else 1 - yl, core), R_FAR + pair * 2 + kv)
        to_core(2, pair, kv)

    own_block = rows_at(seq_own, ROWS)
    for kv, (weight, stage) in enumerate(((wk, stage_k), (wv, stage_v))):
        project(weight, load_w[kv], stage)
        send(stage.at[:, OWN : 2 * OWN], block(store[kv], z, yl, core), R_PAIR + kv, partner)
        store[kv][own_block, :] = stage[:, 0:OWN]
        to_z(0, kv)
        to_core(0, 0, kv)
        if kv == 0:
            load_w.append(load_weight(wq_hbm, wk))
    own_rows = rows_at(yl * ROWS, ROWS)
    pair_rows = rows_at((1 - yl) * ROWS, ROWS)
    for copy in load_adapter:
        copy.wait()
    downb[...] = down_ref[...].astype(BF16)
    upb[:, 0:OWN] = up_ref[:, own_cols].astype(BF16)
    upb[:, OWN : 2 * OWN] = up_ref[:, other_cols].astype(BF16)
    low_own = (dot(normed[...], downb[...]) * input_scale).astype(BF16)
    low[own_rows, :] = low_own
    project(wk, load_w[2], stage_q, low_own, query_scale)
    send(stage_q.at[:, OWN : 2 * OWN], queries.at[own_rows, :], R_PAIR + 2, partner)
    queries[own_rows, :] = stage_q[:, 0:OWN]
    send(low.at[own_rows, :], low.at[own_rows, :], R_PAIR + 3, partner)
    for kv in (0, 1):
        arrive(block(store[kv], z, 1 - yl, core), R_PAIR + kv)
        to_z(1, kv)
        to_core(0, 1, kv)

    def key_bias(start):
        return jnp.where(start + iota((1, PLANE), 1) < length, 0.0, masked_score)

    def forward_plane(plane):
        start = ((z + plane) % 4) * PLANE
        plane_rows = rows_at(start, PLANE, PLANE)
        bias = key_bias(start)
        first = plane == 0
        tiles = [(h, slice(h * HD, (h + 1) * HD), slice(b * ROWS, (b + 1) * ROWS)) for h in range(3) for b in (0, 1)]

        def score(tile):
            _, cols, rows = tile
            return dot_nt(queries[rows, cols], keys[plane_rows, cols]) + bias

        def softmax(tile, scores):
            head, cols, rows = tile
            peak = jnp.max(fold_lanes(jnp.maximum, scores), axis=1, keepdims=True)
            peak = jnp.broadcast_to(peak, (ROWS, 128))
            if not first:
                before = top[head, rows, :]
                peak = jnp.maximum(peak, before)
            exp_scores = jnp.exp2(scores - repeat(peak, PLANE // 128))
            sums = fold_lanes(jnp.add, exp_scores)
            kept = exp_scores.astype(BF16)
            probs[plane, head, rows, :] = kept
            weighted = dot(kept, values[plane_rows, cols])
            if not first:
                decay = jnp.exp2(before - peak)
                sums += decay * total[head, rows, :]
                weighted += decay * acc[rows, cols]
            top[head, rows, :] = peak
            peaks[plane, head, rows, :] = peak
            total[head, rows, :] = sums
            acc[rows, cols] = weighted

        scores = score(tiles[0])
        for i, tile in enumerate(tiles):
            ahead = score(tiles[i + 1]) if i + 1 < len(tiles) else None
            softmax(tile, scores)
            scores = ahead

    for kv in (0, 1):
        for above in (0, 1):
            from_z(0, kv, above)
    arrive(queries.at[pair_rows, :], R_PAIR + 2)
    from_core(0)
    forward_plane(0)
    for kv in (0, 1):
        for above in (0, 1):
            from_z(1, kv, above)
    from_core(1)
    forward_plane(1)
    from_far(0, 0)
    from_far(0, 1)
    from_core(3)
    forward_plane(3)
    from_far(1, 0)
    from_far(1, 1)
    from_core(2)
    forward_plane(2)

    def finish_head(i, carry):
        head = i // 2
        cols = lanes(head * HD, HD)
        rows = rows_at((i % 2) * ROWS, ROWS)
        sums = jnp.broadcast_to(jnp.sum(total[head, rows, :], axis=1, keepdims=True), (ROWS, 128))
        attn[rows, cols] = (acc[rows, cols] / sums).astype(BF16)
        top[head, rows, :] = top[head, rows, :] + jnp.log(sums) * math.log2(math.e)
        return carry

    lax.fori_loop(0, 6, finish_head, 0)

    blank = jnp.zeros((PATCH, OWN), BF16)
    wide = [jnp.concatenate([wout_ref[...], blank], axis=0), jnp.concatenate([blank, wout_ref[...]], axis=0)]
    partial = dot_nt(attn[0:ROWS, :], wide[0]) + dot_nt(attn[ROWS : 2 * ROWS, :], wide[1])
    vel[y] = partial.astype(BF16)
    for d in (1, 2, 3):
        send(vel.at[y], vel.at[y], R_VEL + d - 1, y_peer(d)[1])
    arrive(latents.at[1 - yl], R_PAIR + 4)
    arrive(low.at[pair_rows, :], R_PAIR + 3)
    moved = jnp.zeros((ROWS, 128), F32)
    for b in (0, 1):
        moved += dot(token_rows(latents[b, 1]), fold(PATCH * b, 128))
        moved -= dot(token_rows(latents[b, 0]), fold(PATCH * b, 128))
    lane_block = iota((ROWS, 128), 1) >> 6
    position = (z * 4 + lane_block * 2 + core) * ROWS + iota((ROWS, 128), 0)
    live = position < length
    for d in (1, 2, 3):
        arrive(vel.at[(y + 4 - d) % 4], R_VEL + d - 1)
    velocity = jnp.zeros((ROWS, 128), F32)
    for b in range(4):
        velocity += vel[b].astype(F32)
    zscore = (moved + step_size * velocity) / spread
    own_squares = jnp.where(live, zscore * zscore, 0.0)
    squares[z] = jnp.sum(own_squares.reshape(ROWS // 8, 8, 128), axis=0)
    for d in (1, 2, 3):
        send(squares.at[z], squares.at[z], R_SQ + d - 1, at(sec, x, (z + d) % 4, yl, core))

    grad_vel = jnp.where(live, -zscore * step_size / (spread * count), 0.0).astype(BF16)
    for b in (0, 1):
        gout[b * ROWS : (b + 1) * ROWS, :] = dot(grad_vel, wide[b]).astype(BF16)

    for head in range(3):
        cols = slice(head * HD, (head + 1) * HD)
        delta = jnp.sum(gout[:, cols].astype(F32) * attn[:, cols].astype(F32), axis=1, keepdims=True)
        total[head] = jnp.broadcast_to(delta, (2 * ROWS, 128))
    acc[...] = jnp.zeros_like(acc)

    def backward_plane(plane, carry):
        plane_rows = rows_at(((z + plane) % 4) * PLANE, PLANE, PLANE)

        def product(head):
            cols = slice(head * HD, (head + 1) * HD)
            return dot_nt(gout[:, cols], values[plane_rows, cols])

        def gradient(head, grad_probs):
            cols = slice(head * HD, (head + 1) * HD)
            scale = jnp.exp2(peaks[plane, head] - top[head])
            grad_scores = (grad_probs - repeat(total[head], PLANE // 128)) * repeat(scale, PLANE // 128)
            grad_scores = (probs[plane, head].astype(F32) * grad_scores).astype(BF16)
            acc[:, cols] += dot(grad_scores, keys[plane_rows, cols])

        made = product(0)
        for head in range(3):
            ahead = product(head + 1) if head < 2 else None
            gradient(head, made)
            made = ahead
        return carry

    lax.fori_loop(0, 2, backward_plane, 0)
    for d in (1, 2, 3):
        arrive(squares.at[(z + 4 - d) % 4], R_SQ + d - 1)
    plane_squares = jnp.zeros((8, 128), F32)
    for b in range(4):
        plane_squares += squares[b]
    both[core] = plane_squares
    send(both.at[core], both.at[core], R_SQ + 3, other_core)
    lax.fori_loop(2, 4, backward_plane, 0)

    batch = rewards_ref.shape[1]
    reward = rewards_ref[...].astype(F32)
    group = groups_ref[...].astype(F32)
    mine = iota((1, batch), 1) == x
    own_group = jnp.sum(jnp.where(mine, group, 0.0), axis=1, keepdims=True)
    own_reward = jnp.sum(jnp.where(mine, reward, 0.0), axis=1, keepdims=True)
    member = jnp.where(group == own_group, 1.0, 0.0)
    mean = jnp.sum(member * reward, axis=1, keepdims=True) / GROUP
    centered = reward - mean
    variance = jnp.sum(member * centered * centered, axis=1, keepdims=True) / GROUP
    advantage = (own_reward - mean) / (jnp.sqrt(variance) + 1.0)

    arrive(both.at[1 - core], R_SQ + 3)
    clip_squares = both[0] + both[1]
    clip_squares = jnp.sum(jnp.sum(clip_squares, axis=1, keepdims=True), axis=0, keepdims=True)
    ratio = jnp.exp(-0.5 * clip_squares / count - one * rollout_ref[x])
    out_ratio[0] = jnp.sum(ratio)
    low_edge, high_edge = 1.0 - clip_range, 1.0 + clip_range
    inside = (ratio >= low_edge) & (ratio <= high_edge)
    active = inside | ((advantage > 0) & (ratio < low_edge)) | ((advantage < 0) & (ratio > high_edge))
    weight = jnp.where(active, -advantage * ratio / float(CLIPS), 0.0)

    gq[...] = (acc[...] * (head_scale * weight)).astype(BF16)

    for b in (0, 1):
        part = dot_nt(gq[b * ROWS : (b + 1) * ROWS, :], upb[:, 0:OWN]) * out_scale
        glow_send[b] = part.astype(BF16)
    for d in (1, 2, 3):
        other, device = y_peer(d)
        send(glow_send.at[other % 2], glow.at[y], R_LOW + d - 1, device)
    glow[y] = glow_send[yl]
    up_part = dot(jnp.transpose(low[...].astype(F32)).astype(BF16), gq[...])
    du[0, :, 768:1024] = up_part[:, 0:256]
    du[1, :, 768:896] = up_part[:, 256:384]
    du[1, :, 896:1024] = jnp.zeros((128, 128), F32)
    for d in (1, 2, 3):
        arrive(glow.at[(y + 4 - d) % 4], R_LOW + d - 1)
    low_sum = jnp.zeros((ROWS, 128), F32)
    for b in range(4):
        low_sum += glow[b].astype(F32)
    low_turned = jnp.transpose(low_sum).astype(BF16)

    for half in (1, 0):
        where = (core + half) % 2
        for j in range(3):
            cols = lanes(sec * HALF + where * 768 + j * 256, 256)
            du[where, :, j * 256 : (j + 1) * 256] = dot(low_turned, normed[:, cols])
        if half == 1:
            core_send[...] = du[where].astype(BF16)
            send(core_send, core_recv, R_RC, other_core)
    arrive(core_recv, R_RC)
    summed = du[core] + core_recv[...].astype(F32)
    du[core] = summed
    xs[...] = summed.astype(BF16)

    spots = (x, z)

    def along(half, step):
        if half == 0:
            other = (x + step) % 4
            return other, at(sec, other, z, yl, core)
        other = (z + step) % 4
        return other, at(sec, x, other, yl, core)

    def slab(index):
        return rows_at(index * 32, 32, 32)

    def piece_cols(index):
        return lanes(index * 128, 128)

    for d in (2, 1, 3):
        for half in (0, 1):
            other, device = along(half, d)
            send(xs.at[slab(other), half * 512 : (half + 1) * 512], xr.at[half, d - 1], R_S1 + half * 3 + d - 1, device)
    for half in (0, 1):
        part = du[core, slab(spots[half]), half * 512 : (half + 1) * 512]
        for d in (1, 2, 3):
            arrive(xr.at[half, d - 1], R_S1 + half * 3 + d - 1)
            part += xr[half, d - 1].astype(F32)
        slabs[half] = part
        slabs_send[half] = part.astype(BF16)
        for d in (2, 1, 3):
            other, device = along(1 - half, d)
            send(slabs_send.at[half, :, piece_cols(other)], zr.at[half, d - 1], R_S2 + half * 3 + d - 1, device)
    for half in (0, 1):
        part = slabs[half, :, piece_cols(spots[1 - half])]
        for d in (1, 2, 3):
            arrive(zr.at[half, d - 1], R_S2 + half * 3 + d - 1)
            part += zr[half, d - 1].astype(F32)
        yr[y, half] = part.astype(BF16)
    for d in (1, 2, 3):
        send(yr.at[y], yr.at[y], R_RY + d - 1, y_peer(d)[1])
    for d in (1, 2, 3):
        arrive(yr.at[(y + 4 - d) % 4], R_RY + d - 1)
    for b in (0, 1):
        sums = yr[2 * b].astype(F32) + yr[2 * b + 1].astype(F32)
        full[core, 0, b, slab(x), piece_cols(z)] = sums[0].astype(BF16)
        full[core, 1, b, slab(z), piece_cols(x)] = jnp.where(x < 2, sums[1], yr[sec * 2 + b, 1].astype(F32)).astype(BF16)

    for d in (2, 1, 3):
        for half in (0, 1):
            mine_ = full.at[core, half, :, slab(spots[half]), piece_cols(spots[1 - half])]
            send(mine_, mine_, R_G1 + half * 3 + d - 1, along(1 - half, d)[1])
    for half in (0, 1):
        for d in (1, 2, 3):
            source = along(1 - half, 4 - d)[0]
            arrive(full.at[core, half, :, slab(spots[half]), piece_cols(source)], R_G1 + half * 3 + d - 1)
        mine_ = full.at[core, half, :, slab(spots[half]), :]
        for d in (2, 1, 3):
            send(mine_, mine_, R_G2 + half * 3 + d - 1, along(half, d)[1])
        send(mine_, mine_, R_GC + half * 4, other_core)
    for d in (1, 3, 2):
        for half in (0, 1):
            source = slab(along(half, 4 - d)[0])
            theirs = full.at[core, half, :, source, :]
            arrive(theirs, R_G2 + half * 3 + d - 1)
            send(theirs, theirs, R_GC + half * 4 + d, other_core)
    for d in (0, 1, 2, 3):
        for half in (0, 1):
            arrive(full.at[1 - core, half, :, slab(along(half, 4 - d)[0]), :], R_GC + half * 4 + d)

    load(full, out_grad).wait()
    for copy in pending:
        copy.wait_send()


def update(grad_ref, down_ref, up_ref, ratio_ref, out_down, out_up, out_ratio):
    norm_sum = jnp.zeros((128, 256), F32)
    for core in (0, 1):
        for sec in (0, 1):
            for half, width in ((0, 512), (1, 256)):
                for j in range(width // 256):
                    part = grad_ref[core, half, sec, :, j * 256 : (j + 1) * 256].astype(F32)
                    norm_sum += part * part
    norm_sum = jnp.sum(jnp.sum(norm_sum, axis=1, keepdims=True), axis=0, keepdims=True)
    factor = step_length / jnp.sqrt(norm_sum * (input_scale * input_scale) + norm_eps)
    down_factor, up_factor = factor * input_scale, factor * out_scale
    for t in range(MODEL_WIDTH // 128):
        sec, core, j = t // 12, (t % 12) // 6, t % 6
        half, start = j // 4, (j % 4) * 128
        part = grad_ref[core, half, sec, :, start : start + 128].astype(F32)
        rows = slice(t * 128, (t + 1) * 128)
        out_down[rows, :] = down_ref[rows, :] - down_factor * jnp.transpose(part)
    for b in (0, 1):
        for core, width in ((0, 256), (1, 128)):
            cols = slice(b * OWN + core * 256, b * OWN + core * 256 + width)
            part = grad_ref[core, 1, b, :, 256 : 256 + width].astype(F32)
            out_up[:, cols] = up_ref[:, cols] - up_factor * part
    out_ratio[0] = ratio_ref[0]


def shards(
    trajectory, block_input, chosen, lengths, rewards, prompt_group_index, rollout_log_probability,
    timestep_norm_shift, patch_input_weight, frozen_query_matrix, frozen_key_matrix, frozen_value_matrix,
    velocity_output_weight, adapter_down_factor, adapter_up_factor,
):
    vmem = pl.BlockSpec(memory_space=pltpu.VMEM)
    smem = pl.BlockSpec(memory_space=pltpu.SMEM)
    hbm = pl.BlockSpec(memory_space=pl.ANY)
    V = pltpu.VMEM
    scratch = [
        V((STEPS, 2, MODEL_WIDTH), F32),
        V((PATCH, MODEL_WIDTH), BF16),
        V((PATCH, OWN), BF16),
        V((MODEL_WIDTH, ADAPTER_RANK), F32),
        V((ADAPTER_RANK, 2 * OWN), F32),
        V((ROWS, MODEL_WIDTH), BF16),
        V((MODEL_WIDTH, 2 * OWN), BF16),
        V((MODEL_WIDTH, 2 * OWN), BF16),
        V((MODEL_WIDTH, ADAPTER_RANK), BF16),
        V((ADAPTER_RANK, 2 * OWN), BF16),
        V((ROWS, MODEL_WIDTH), F32),
        V((ROWS, MODEL_WIDTH), BF16),
        V((CLIPS, 2, PAIRS, 128), BF16),
        V((2, 2, 128, 128), BF16),
        V((ROWS, 2 * OWN), BF16),
        V((ROWS, 2 * OWN), BF16),
        V((ROWS, 2 * OWN), BF16),
        V((4 * PLANE, OWN), BF16),
        V((4 * PLANE, OWN), BF16),
        V((2 * ROWS, OWN), BF16),
        V((2 * ROWS, ADAPTER_RANK), BF16),
        V((3, 2 * ROWS, 128), F32),
        V((4, 3, 2 * ROWS, 128), F32),
        V((4, 3, 2 * ROWS, PLANE), BF16),
        V((3, 2 * ROWS, 128), F32),
        V((2 * ROWS, OWN), F32),
        V((2 * ROWS, OWN), BF16),
        V((4, ROWS, 128), BF16),
        V((4, 8, 128), F32),
        V((2, 8, 128), F32),
        V((2 * ROWS, OWN), BF16),
        V((2 * ROWS, OWN), BF16),
        V((2, ROWS, 128), BF16),
        V((4, ROWS, 128), BF16),
        V((2, 128, 1024), F32),
        V((128, 1024), BF16),
        V((128, 1024), BF16),
        V((128, 1024), BF16),
        V((2, 3, 32, 512), BF16),
        V((2, 32, 512), F32),
        V((2, 32, 512), BF16),
        V((2, 3, 32, 128), BF16),
        V((4, 2, 32, 128), BF16),
        V((2, 2, 2, 128, 512), BF16),
        pltpu.SemaphoreType.DMA((N_SEND,)),
        pltpu.SemaphoreType.DMA((N_RECV,)),
        pltpu.SemaphoreType.DMA((16,)),
    ]
    gradients, ratio = pl.pallas_call(
        body,
        out_shape=(
            jax.ShapeDtypeStruct((2, 2, 2, ADAPTER_RANK, 512), BF16),
            jax.ShapeDtypeStruct((1,), F32),
        ),
        in_specs=[smem] * 3 + [vmem] * 3 + [hbm] * 9,
        out_specs=(hbm, smem),
        scratch_shapes=scratch,
        compiler_params=pltpu.CompilerParams(
            collective_id=0, has_side_effects=True, vmem_limit_bytes=60 * 1024 * 1024
        ),
        cost_estimate=pl.CostEstimate(flops=12_000_000_000, bytes_accessed=24_000_000, transcendentals=13_000_000),
        name="policy_step",
    )(
        chosen, lengths, rollout_log_probability,
        trajectory.reshape(STEPS + 1, CLIPS, PAIRS, 128),
        rewards.reshape(1, -1), prompt_group_index.reshape(1, -1), timestep_norm_shift, patch_input_weight,
        velocity_output_weight.T, adapter_down_factor, adapter_up_factor,
        block_input.reshape(ROWS, MODEL_WIDTH), frozen_query_matrix, frozen_key_matrix, frozen_value_matrix,
    )
    return pl.pallas_call(
        update,
        out_shape=(
            jax.ShapeDtypeStruct((MODEL_WIDTH, ADAPTER_RANK), F32),
            jax.ShapeDtypeStruct((ADAPTER_RANK, 2 * OWN), F32),
            jax.ShapeDtypeStruct((1,), F32),
        ),
        in_specs=[vmem] * 3 + [smem],
        out_specs=(vmem, vmem, smem),
        compiler_params=pltpu.CompilerParams(vmem_limit_bytes=32 * 1024 * 1024),
        name="update",
    )(gradients, adapter_down_factor, adapter_up_factor, ratio)


def solution(mesh):
    return jax.shard_map(
        shards,
        mesh=mesh,
        in_specs=(
            P(None, None, "seq", "dp", None),
            P("dp", "seq", None),
            P(), P(), P(), P(), P(), P(), P(),
            P(None, "section"),
            P(None, "section"),
            P(None, "section"),
            P("section", None),
            P(),
            P(None, "section"),
        ),
        out_specs=(P(), P(None, "section"), P("dp")),
        check_vma=False,
    )
```

```python
import functools
import math

import jax
import jax.numpy as jnp
from jax import lax
from jax.experimental import pallas as pl
from jax.experimental.pallas import tpu as pltpu
from jax.sharding import PartitionSpec as P

MESH = pl.DeviceIdType.MESH
F32 = jnp.float32
BF16 = jnp.bfloat16

MODEL_WIDTH = 3072
HD = 128
ADAPTER_RANK = 128
STEPS = 4
GROUP = 16
PATCH = 64
CLIPS = 4
ROWS = 256
PAIRS = 32
OWN = 384
PLANE = 1024
HALF = 1536

noise_level = 0.8
clip_range = 0.2
step_length = 256.0
norm_eps = 1e-06
masked_score = -1e30
step_size = 1.0 / (STEPS + 1)
input_scale = 1.0 / math.sqrt(MODEL_WIDTH)
out_scale = 1.0 / math.sqrt(ADAPTER_RANK)
head_scale = 1.0 / math.sqrt(HD)
query_scale = head_scale * math.log2(math.e)

NT = (((1,), (1,)), ((), ()))

R_X = 0
R_PAIR = 3
R_Z = 8
R_FAR = 16
R_CORE = 20
R_VEL = 36
R_SQ = 39
R_LOW = 43
R_RC = 46
R_S1 = 47
R_S2 = 53
R_RY = 59
R_G1 = 62
R_G2 = 68
R_GC = 74
N_RECV = 82
N_SEND = 96


def dot(a, b):
    return jnp.dot(a, b, preferred_element_type=F32)


def dot_nt(a, b):
    return lax.dot_general(a, b, NT, preferred_element_type=F32)


def iota(shape, dim):
    return lax.broadcasted_iota(jnp.int32, shape, dim)


def lanes(start, size):
    return pl.ds(pl.multiple_of(start, 128), size)


def rows_at(start, size, unit=256):
    return pl.ds(pl.multiple_of(start, unit), size)


def body(
    chosen_ref, lengths_ref, rollout_ref,
    traj_ref, rewards_ref, groups_ref,
    shift_hbm, patch_hbm, wout_hbm, down_hbm, up_hbm, x_hbm, wq_hbm, wk_hbm, wv_hbm,
    out_grad, out_ratio,
    shift_ref, patch_ref, wout_ref, down_ref, up_ref, xin, wk, wv, downb, upb, emb, normed,
    sel, latents, stage_k, stage_v, stage_q, keys, values, queries, low,
    top, peaks, probs, total, acc, attn, vel, squares, both, gout, gq, glow_send, glow,
    du, core_send, core_recv, xs, xr, slabs, slabs_send, zr, yr, full,
    send_sem, recv_sem, local_sem,
):
    sec = lax.axis_index("section")
    x = lax.axis_index("dp")
    seq = lax.axis_index("seq")
    z = seq // 4
    yl = (seq // 2) % 2
    core = seq % 2
    y = sec * 2 + yl

    def at(sec_, x_, z_, yl_, core_):
        return (sec_, x_, z_ * 4 + yl_ * 2 + core_)

    def y_peer(step):
        other = (y + step) % 4
        return other, at(other // 2, x, z, other % 2, core)

    other_core = at(sec, x, z, yl, 1 - core)
    partner = at(sec, x, z, 1 - yl, core)
    z_up = at(sec, x, (z + 1) % 4, yl, core)
    z_down = at(sec, x, (z + 3) % 4, yl, core)

    pending = []

    def descriptor(src, dst, send_index, recv_index, device):
        return pltpu.make_async_remote_copy(
            src_ref=src, dst_ref=dst, send_sem=send_sem.at[send_index], recv_sem=recv_sem.at[recv_index],
            device_id=device, device_id_type=MESH,
        )

    def send(src, dst, recv_index, device):
        copy = descriptor(src, dst, len(pending), recv_index, device)
        copy.start()
        pending.append(copy)

    def arrive(dst, recv_index):
        descriptor(dst, dst, 0, recv_index, other_core).wait_recv()

    loads = []

    def load(src, dst):
        copy = pltpu.make_async_copy(src, dst, local_sem.at[len(loads)])
        copy.start()
        loads.append(copy)
        return copy


    peers = [at(sec, (x + d) % 4, z, yl, core) for d in (1, 2, 3)]
    peers += [at(sec, x, (z + d) % 4, yl, core) for d in (1, 2, 3)]
    peers += [y_peer(d)[1] for d in (1, 2, 3)]
    peers += [other_core]
    barrier = pltpu.get_barrier_semaphore()
    for peer in peers:
        pl.semaphore_signal(barrier, inc=1, device_id=peer, device_id_type=MESH)

    load_x = [load(x_hbm, xin), load(patch_hbm, patch_ref), load(shift_hbm, shift_ref)]
    own_cols, other_cols = lanes(yl * OWN, OWN), lanes((1 - yl) * OWN, OWN)

    def load_weight(src, dst):
        return load(src.at[:, own_cols], dst.at[:, 0:OWN]), load(src.at[:, other_cols], dst.at[:, OWN : 2 * OWN])

    load_w = [load_weight(wk_hbm, wk), load_weight(wv_hbm, wv)]
    load_adapter = [load(down_hbm, down_ref), load(up_hbm, up_ref), load(wout_hbm.at[:, own_cols], wout_ref)]

    for c in range(CLIPS):
        sel[c, 0] = traj_ref[chosen_ref[c], c]
        sel[c, 1] = traj_ref[chosen_ref[c] + 1, c]
    pl.semaphore_wait(barrier, len(peers))
    x_rows = rows_at(x * PAIRS, PAIRS, PAIRS)
    for d in (1, 2, 3):
        to = (x + d) % 4
        send(sel.at[to], latents.at[yl, :, x_rows, :], R_X + d - 1, at(sec, to, z, yl, core))
    latents[yl, :, x_rows, :] = sel[x]

    chosen = chosen_ref[x]
    length = lengths_ref[x]
    one = jnp.ones((1, 1), F32)
    spread = noise_level * jnp.sqrt(step_size * (1.0 - one * chosen.astype(F32) * step_size))
    count = one * (length * PATCH).astype(F32)

    def repeat(stat, count):
        return jnp.concatenate([stat] * count, axis=1)

    def fold_lanes(op, tile):
        out = tile[:, 0:128]
        for j in range(1, tile.shape[1] // 128):
            out = op(out, tile[:, j * 128 : (j + 1) * 128])
        return out

    expand = jnp.where((iota((ROWS, 128), 0) >> 1) == iota((ROWS, 128), 1), 1.0, 0.0).astype(BF16)
    own_half = (iota((ROWS, 128), 1) >> 6) == (iota((ROWS, 128), 0) & 1)

    def token_rows(pairs):
        return jnp.where(own_half, dot(expand, pairs), 0.0).astype(BF16)

    def fold(offset, width):
        source = (iota((128, width), 0) & 63) + offset
        return jnp.where(source == iota((128, width), 1), 1.0, 0.0).astype(BF16)

    for d in (1, 2, 3):
        src_rows = rows_at(((x + 4 - d) % 4) * PAIRS, PAIRS, PAIRS)
        arrive(latents.at[yl, :, src_rows, :], R_X + d - 1)
    send(latents.at[yl], latents.at[yl], R_PAIR + 4, partner)

    now_tokens = dot(token_rows(latents[yl, 0]), fold(0, 64)).astype(BF16)
    for copy in load_x:
        copy.wait()
    squares_sum = jnp.zeros((ROWS, 128), F32)
    chunk = 512
    for j in range(MODEL_WIDTH // chunk):
        cols = slice(j * chunk, (j + 1) * chunk)
        part = xin[:, cols].astype(F32) + dot(now_tokens, patch_ref[:, cols])
        emb[:, cols] = part
        squares_sum += fold_lanes(jnp.add, part * part)
    mean_square = jnp.sum(squares_sum, axis=1, keepdims=True) * (1.0 / MODEL_WIDTH)
    inverse = repeat(jnp.broadcast_to(lax.rsqrt(mean_square + norm_eps), (ROWS, 128)), chunk // 128)
    for j in range(MODEL_WIDTH // chunk):
        cols = slice(j * chunk, (j + 1) * chunk)
        shift = shift_ref[chosen, 0:1, cols]
        scale = 1.0 + shift_ref[chosen, 1:2, cols]
        normed[:, cols] = (emb[:, cols] * inverse * scale + shift).astype(BF16)

    seq_own = seq * ROWS
    seq_pair = (seq + 2 - 4 * yl) * ROWS

    def block(ref, z_, yl_, core_):
        return ref.at[rows_at((z_ * 4 + yl_ * 2 + core_) * ROWS, ROWS), :]

    def project(weight, loaded, stage, extra=None, scale=None):
        for copy in loaded:
            copy.wait()

        def step(n, carry):
            cols = lanes(n * 256, 256)
            part = dot(normed[...], weight[:, cols])
            if extra is not None:
                part = (part + dot(extra, upb[:, cols]) * out_scale) * scale
            stage[:, cols] = part.astype(BF16)
            return carry

        lax.fori_loop(0, 3, step, 0)

    store = (keys, values)

    def core_index(plane, pair, kv):
        return R_CORE + plane * 4 + pair * 2 + kv

    def to_core(plane, pair, kv):
        z_ = (z + plane) % 4
        yl_ = yl if pair == 0 else 1 - yl
        send(block(store[kv], z_, yl_, core), block(store[kv], z_, yl_, core), core_index(plane, pair, kv), other_core)

    def from_core(plane, pairs=(0, 1)):
        z_ = (z + plane) % 4
        for pair in pairs:
            yl_ = yl if pair == 0 else 1 - yl
            for kv in (0, 1):
                arrive(block(store[kv], z_, yl_, 1 - core), core_index(plane, pair, kv))

    def z_index(pair, kv, above):
        return R_Z + pair * 4 + kv * 2 + above

    def to_z(pair, kv):
        src = block(store[kv], z, yl if pair == 0 else 1 - yl, core)
        send(src, src, z_index(pair, kv, 0), z_up)
        send(src, src, z_index(pair, kv, 1), z_down)

    def from_z(pair, kv, above):
        z_ = (z + 1) % 4 if above else (z + 3) % 4
        src = block(store[kv], z_, yl if pair == 0 else 1 - yl, core)
        arrive(src, z_index(pair, kv, above))
        if kv == 0 and not above:
            send(src, src, R_FAR + pair * 2 + kv, z_up)
        if kv == 1 and above:
            send(src, src, R_FAR + pair * 2 + kv, z_down)
        to_core(1 if above else 3, pair, kv)

    def from_far(pair, kv):
        arrive(block(store[kv], (z + 2) % 4, yl if pair == 0 else 1 - yl, core), R_FAR + pair * 2 + kv)
        to_core(2, pair, kv)

    own_block = rows_at(seq_own, ROWS)
    for kv, (weight, stage) in enumerate(((wk, stage_k), (wv, stage_v))):
        project(weight, load_w[kv], stage)
        send(stage.at[:, OWN : 2 * OWN], block(store[kv], z, yl, core), R_PAIR + kv, partner)
        store[kv][own_block, :] = stage[:, 0:OWN]
        to_z(0, kv)
        to_core(0, 0, kv)
        if kv == 0:
            load_w.append(load_weight(wq_hbm, wk))
    own_rows = rows_at(yl * ROWS, ROWS)
    pair_rows = rows_at((1 - yl) * ROWS, ROWS)
    for copy in load_adapter:
        copy.wait()
    downb[...] = down_ref[...].astype(BF16)
    upb[:, 0:OWN] = up_ref[:, own_cols].astype(BF16)
    upb[:, OWN : 2 * OWN] = up_ref[:, other_cols].astype(BF16)
    low_own = (dot(normed[...], downb[...]) * input_scale).astype(BF16)
    low[own_rows, :] = low_own
    project(wk, load_w[2], stage_q, low_own, query_scale)
    send(stage_q.at[:, OWN : 2 * OWN], queries.at[own_rows, :], R_PAIR + 2, partner)
    queries[own_rows, :] = stage_q[:, 0:OWN]
    send(low.at[own_rows, :], low.at[own_rows, :], R_PAIR + 3, partner)
    for kv in (0, 1):
        arrive(block(store[kv], z, 1 - yl, core), R_PAIR + kv)
        to_z(1, kv)
        to_core(0, 1, kv)

    def key_bias(start, width):
        return jnp.where(start + iota((1, width), 1) < length, 0.0, masked_score)

    def forward_part(plane, slot, offset, width):
        start = ((z + plane) % 4) * PLANE + offset
        plane_rows = rows_at(start, width, width)
        bias = key_bias(start, width)
        first = plane == 0
        tiles = [(h, slice(h * HD, (h + 1) * HD), slice(b * ROWS, (b + 1) * ROWS)) for h in range(3) for b in (0, 1)]

        def score(tile):
            _, cols, rows = tile
            return dot_nt(queries[rows, cols], keys[plane_rows, cols]) + bias

        def softmax(tile, scores):
            head, cols, rows = tile
            peak = jnp.max(fold_lanes(jnp.maximum, scores), axis=1, keepdims=True)
            peak = jnp.broadcast_to(peak, (ROWS, 128))
            if not first:
                before = top[head, rows, :]
                peak = jnp.maximum(peak, before)
            exp_scores = jnp.exp2(scores - repeat(peak, width // 128))
            sums = fold_lanes(jnp.add, exp_scores)
            kept = exp_scores.astype(BF16)
            probs[plane, head, rows, lanes(offset, width)] = kept
            weighted = dot(kept, values[plane_rows, cols])
            if not first:
                decay = jnp.exp2(before - peak)
                sums += decay * total[head, rows, :]
                weighted += decay * acc[rows, cols]
            top[head, rows, :] = peak
            peaks[slot, head, rows, :] = peak
            total[head, rows, :] = sums
            acc[rows, cols] = weighted

        scores = score(tiles[0])
        for i, tile in enumerate(tiles):
            ahead = score(tiles[i + 1]) if i + 1 < len(tiles) else None
            softmax(tile, scores)
            scores = ahead

    for kv in (0, 1):
        for above in (0, 1):
            from_z(0, kv, above)
    arrive(queries.at[pair_rows, :], R_PAIR + 2)
    from_core(0)
    forward_part(0, 0, 0, PLANE)
    for kv in (0, 1):
        for above in (0, 1):
            from_z(1, kv, above)
    from_core(1)
    forward_part(1, 1, 0, PLANE)
    from_far(0, 0)
    from_far(0, 1)
    from_core(3)
    forward_part(3, 3, 0, PLANE)
    from_core(2, (0,))
    forward_part(2, 2, yl * 512, 512)
    from_far(1, 0)
    from_far(1, 1)
    from_core(2, (1,))
    forward_part(2, 4, (1 - yl) * 512, 512)

    for head in range(3):
        cols = slice(head * HD, (head + 1) * HD)
        sums = jnp.broadcast_to(jnp.sum(total[head], axis=1, keepdims=True), (2 * ROWS, 128))
        attn[:, cols] = (acc[:, cols] / sums).astype(BF16)
        top[head] = top[head] + jnp.log(sums) * math.log2(math.e)

    blank = jnp.zeros((PATCH, OWN), BF16)
    wide = [jnp.concatenate([wout_ref[...], blank], axis=0), jnp.concatenate([blank, wout_ref[...]], axis=0)]
    partial = dot_nt(attn[0:ROWS, :], wide[0]) + dot_nt(attn[ROWS : 2 * ROWS, :], wide[1])
    vel[y] = partial.astype(BF16)
    for d in (2, 1, 3):
        send(vel.at[y], vel.at[y], R_VEL + d - 1, y_peer(d)[1])
    arrive(latents.at[1 - yl], R_PAIR + 4)
    arrive(low.at[pair_rows, :], R_PAIR + 3)
    moved = jnp.zeros((ROWS, 128), F32)
    for b in (0, 1):
        moved += dot(token_rows(latents[b, 1]), fold(PATCH * b, 128))
        moved -= dot(token_rows(latents[b, 0]), fold(PATCH * b, 128))
    lane_block = iota((ROWS, 128), 1) >> 6
    position = (z * 4 + lane_block * 2 + core) * ROWS + iota((ROWS, 128), 0)
    live = position < length
    for d in (1, 2, 3):
        arrive(vel.at[(y + 4 - d) % 4], R_VEL + d - 1)
    velocity = jnp.zeros((ROWS, 128), F32)
    for b in range(4):
        velocity += vel[b].astype(F32)
    zscore = (moved + step_size * velocity) / spread
    own_squares = jnp.where(live, zscore * zscore, 0.0)
    squares[z] = jnp.sum(own_squares.reshape(ROWS // 8, 8, 128), axis=0)
    for d in (1, 2, 3):
        send(squares.at[z], squares.at[z], R_SQ + d - 1, at(sec, x, (z + d) % 4, yl, core))

    grad_vel = jnp.where(live, -zscore * step_size / (spread * count), 0.0).astype(BF16)
    for b in (0, 1):
        gout[b * ROWS : (b + 1) * ROWS, :] = dot(grad_vel, wide[b]).astype(BF16)

    for head in range(3):
        cols = slice(head * HD, (head + 1) * HD)
        delta = jnp.sum(gout[:, cols].astype(F32) * attn[:, cols].astype(F32), axis=1, keepdims=True)
        total[head] = jnp.broadcast_to(delta, (2 * ROWS, 128))
    acc[...] = jnp.zeros_like(acc)

    def backward_plane(plane, carry):
        plane_rows = rows_at(((z + plane) % 4) * PLANE, PLANE, PLANE)
        slots = [jnp.where((plane == 2) & (yl == 1 - b), 4, plane) for b in (0, 1)]

        def product(head):
            cols = slice(head * HD, (head + 1) * HD)
            return dot_nt(gout[:, cols], values[plane_rows, cols])

        def gradient(head, grad_probs):
            cols = slice(head * HD, (head + 1) * HD)
            scale = jnp.concatenate(
                [repeat(jnp.exp2(peaks[slot, head] - top[head]), 4) for slot in slots], axis=1
            )
            grad_scores = (grad_probs - repeat(total[head], PLANE // 128)) * scale
            grad_scores = (probs[plane, head].astype(F32) * grad_scores).astype(BF16)
            acc[:, cols] += dot(grad_scores, keys[plane_rows, cols])

        made = product(0)
        for head in range(3):
            ahead = product(head + 1) if head < 2 else None
            gradient(head, made)
            made = ahead
        return carry

    lax.fori_loop(0, 2, backward_plane, 0)
    for d in (1, 2, 3):
        arrive(squares.at[(z + 4 - d) % 4], R_SQ + d - 1)
    plane_squares = jnp.zeros((8, 128), F32)
    for b in range(4):
        plane_squares += squares[b]
    both[core] = plane_squares
    send(both.at[core], both.at[core], R_SQ + 3, other_core)
    lax.fori_loop(2, 4, backward_plane, 0)

    batch = rewards_ref.shape[1]
    reward = rewards_ref[...].astype(F32)
    group = groups_ref[...].astype(F32)
    mine = iota((1, batch), 1) == x
    own_group = jnp.sum(jnp.where(mine, group, 0.0), axis=1, keepdims=True)
    own_reward = jnp.sum(jnp.where(mine, reward, 0.0), axis=1, keepdims=True)
    member = jnp.where(group == own_group, 1.0, 0.0)
    mean = jnp.sum(member * reward, axis=1, keepdims=True) / GROUP
    centered = reward - mean
    variance = jnp.sum(member * centered * centered, axis=1, keepdims=True) / GROUP
    advantage = (own_reward - mean) / (jnp.sqrt(variance) + 1.0)

    arrive(both.at[1 - core], R_SQ + 3)
    clip_squares = both[0] + both[1]
    clip_squares = jnp.sum(jnp.sum(clip_squares, axis=1, keepdims=True), axis=0, keepdims=True)
    ratio = jnp.exp(-0.5 * clip_squares / count - one * rollout_ref[x])
    out_ratio[0] = jnp.sum(ratio)
    low_edge, high_edge = 1.0 - clip_range, 1.0 + clip_range
    inside = (ratio >= low_edge) & (ratio <= high_edge)
    active = inside | ((advantage > 0) & (ratio < low_edge)) | ((advantage < 0) & (ratio > high_edge))
    weight = jnp.where(active, -advantage * ratio / float(CLIPS), 0.0)

    gq[...] = (acc[...] * (head_scale * weight)).astype(BF16)

    for b in (0, 1):
        part = dot_nt(gq[b * ROWS : (b + 1) * ROWS, :], upb[:, 0:OWN]) * out_scale
        glow_send[b] = part.astype(BF16)
    for d in (2, 1, 3):
        other, device = y_peer(d)
        send(glow_send.at[other % 2], glow.at[y], R_LOW + d - 1, device)
    glow[y] = glow_send[yl]
    up_part = dot(jnp.transpose(low[...].astype(F32)).astype(BF16), gq[...])
    du[0, :, 768:1024] = up_part[:, 0:256]
    du[1, :, 768:896] = up_part[:, 256:384]
    du[1, :, 896:1024] = jnp.zeros((128, 128), F32)
    for d in (1, 2, 3):
        arrive(glow.at[(y + 4 - d) % 4], R_LOW + d - 1)
    low_sum = jnp.zeros((ROWS, 128), F32)
    for b in range(4):
        low_sum += glow[b].astype(F32)
    low_turned = jnp.transpose(low_sum).astype(BF16)

    for half in (1, 0):
        where = (core + half) % 2
        for j in range(3):
            cols = lanes(sec * HALF + where * 768 + j * 256, 256)
            du[where, :, j * 256 : (j + 1) * 256] = dot(low_turned, normed[:, cols])
        if half == 1:
            core_send[...] = du[where].astype(BF16)
            send(core_send, core_recv, R_RC, other_core)
    arrive(core_recv, R_RC)
    summed = du[core] + core_recv[...].astype(F32)
    du[core] = summed
    xs[...] = summed.astype(BF16)

    spots = (x, z)

    def along(half, step):
        if half == 0:
            other = (x + step) % 4
            return other, at(sec, other, z, yl, core)
        other = (z + step) % 4
        return other, at(sec, x, other, yl, core)

    def slab(index):
        return rows_at(index * 32, 32, 32)

    def piece_cols(index):
        return lanes(index * 128, 128)

    for d in (2, 1, 3):
        for half in (0, 1):
            other, device = along(half, d)
            send(xs.at[slab(other), half * 512 : (half + 1) * 512], xr.at[half, d - 1], R_S1 + half * 3 + d - 1, device)
    for half in (0, 1):
        part = du[core, slab(spots[half]), half * 512 : (half + 1) * 512]
        for d in (1, 2, 3):
            arrive(xr.at[half, d - 1], R_S1 + half * 3 + d - 1)
            part += xr[half, d - 1].astype(F32)
        slabs[half] = part
        slabs_send[half] = part.astype(BF16)
        for d in (2, 1, 3):
            other, device = along(1 - half, d)
            send(slabs_send.at[half, :, piece_cols(other)], zr.at[half, d - 1], R_S2 + half * 3 + d - 1, device)
    for half in (0, 1):
        part = slabs[half, :, piece_cols(spots[1 - half])]
        for d in (1, 2, 3):
            arrive(zr.at[half, d - 1], R_S2 + half * 3 + d - 1)
            part += zr[half, d - 1].astype(F32)
        yr[y, half] = part.astype(BF16)
    for d in (2, 1, 3):
        send(yr.at[y], yr.at[y], R_RY + d - 1, y_peer(d)[1])
    for d in (1, 2, 3):
        arrive(yr.at[(y + 4 - d) % 4], R_RY + d - 1)
    for b in (0, 1):
        sums = yr[2 * b].astype(F32) + yr[2 * b + 1].astype(F32)
        full[core, 0, b, slab(x), piece_cols(z)] = sums[0].astype(BF16)
        full[core, 1, b, slab(z), piece_cols(x)] = jnp.where(x < 2, sums[1], yr[sec * 2 + b, 1].astype(F32)).astype(BF16)

    for d in (2, 1, 3):
        for half in (0, 1):
            mine_ = full.at[core, half, :, slab(spots[half]), piece_cols(spots[1 - half])]
            send(mine_, mine_, R_G1 + half * 3 + d - 1, along(1 - half, d)[1])
    for half in (0, 1):
        for d in (1, 2, 3):
            source = along(1 - half, 4 - d)[0]
            arrive(full.at[core, half, :, slab(spots[half]), piece_cols(source)], R_G1 + half * 3 + d - 1)
        mine_ = full.at[core, half, :, slab(spots[half]), :]
        for d in (2, 1, 3):
            send(mine_, mine_, R_G2 + half * 3 + d - 1, along(half, d)[1])
        send(mine_, mine_, R_GC + half * 4, other_core)
    for d in (1, 3, 2):
        for half in (0, 1):
            source = slab(along(half, 4 - d)[0])
            theirs = full.at[core, half, :, source, :]
            arrive(theirs, R_G2 + half * 3 + d - 1)
            send(theirs, theirs, R_GC + half * 4 + d, other_core)
    for d in (0, 1, 2, 3):
        for half in (0, 1):
            arrive(full.at[1 - core, half, :, slab(along(half, 4 - d)[0]), :], R_GC + half * 4 + d)

    load(full, out_grad).wait()
    for copy in pending:
        copy.wait_send()


def update(grad_hbm, down_hbm, up_hbm, ratio_ref, out_down, out_up, out_ratio, grad_ref, down_ref, up_ref, sem):
    copies = {}
    for core in (0, 1):
        for half in (0, 1):
            here = (core, half)
            copies[here] = pltpu.make_async_copy(grad_hbm.at[here], grad_ref.at[here], sem.at[2 * core + half])
            copies[here].start()
    adapters = [
        pltpu.make_async_copy(down_hbm, down_ref, sem.at[4]),
        pltpu.make_async_copy(up_hbm, up_ref, sem.at[5]),
    ]
    for copy in adapters:
        copy.start()
    norm_sum = jnp.zeros((128, 256), F32)
    for core in (0, 1):
        for half, width in ((0, 512), (1, 256)):
            copies[core, half].wait()
            for sec in (0, 1):
                for j in range(width // 256):
                    part = grad_ref[core, half, sec, :, j * 256 : (j + 1) * 256].astype(F32)
                    norm_sum += part * part
    norm_sum = jnp.sum(jnp.sum(norm_sum, axis=1, keepdims=True), axis=0, keepdims=True)
    factor = step_length / jnp.sqrt(norm_sum * (input_scale * input_scale) + norm_eps)
    down_factor, up_factor = factor * input_scale, factor * out_scale
    for copy in adapters:
        copy.wait()
    for t in range(MODEL_WIDTH // 128):
        sec, core, j = t // 12, (t % 12) // 6, t % 6
        half, start = j // 4, (j % 4) * 128
        part = grad_ref[core, half, sec, :, start : start + 128].astype(F32)
        rows = slice(t * 128, (t + 1) * 128)
        out_down[rows, :] = down_ref[rows, :] - down_factor * jnp.transpose(part)
    for b in (0, 1):
        for core, width in ((0, 256), (1, 128)):
            cols = slice(b * OWN + core * 256, b * OWN + core * 256 + width)
            part = grad_ref[core, 1, b, :, 256 : 256 + width].astype(F32)
            out_up[:, cols] = up_ref[:, cols] - up_factor * part
    out_ratio[0] = ratio_ref[0]


def shards(
    trajectory, block_input, chosen, lengths, rewards, prompt_group_index, rollout_log_probability,
    timestep_norm_shift, patch_input_weight, frozen_query_matrix, frozen_key_matrix, frozen_value_matrix,
    velocity_output_weight, adapter_down_factor, adapter_up_factor,
):
    vmem = pl.BlockSpec(memory_space=pltpu.VMEM)
    smem = pl.BlockSpec(memory_space=pltpu.SMEM)
    hbm = pl.BlockSpec(memory_space=pl.ANY)
    V = pltpu.VMEM
    scratch = [
        V((STEPS, 2, MODEL_WIDTH), F32),
        V((PATCH, MODEL_WIDTH), BF16),
        V((PATCH, OWN), BF16),
        V((MODEL_WIDTH, ADAPTER_RANK), F32),
        V((ADAPTER_RANK, 2 * OWN), F32),
        V((ROWS, MODEL_WIDTH), BF16),
        V((MODEL_WIDTH, 2 * OWN), BF16),
        V((MODEL_WIDTH, 2 * OWN), BF16),
        V((MODEL_WIDTH, ADAPTER_RANK), BF16),
        V((ADAPTER_RANK, 2 * OWN), BF16),
        V((ROWS, MODEL_WIDTH), F32),
        V((ROWS, MODEL_WIDTH), BF16),
        V((CLIPS, 2, PAIRS, 128), BF16),
        V((2, 2, 128, 128), BF16),
        V((ROWS, 2 * OWN), BF16),
        V((ROWS, 2 * OWN), BF16),
        V((ROWS, 2 * OWN), BF16),
        V((4 * PLANE, OWN), BF16),
        V((4 * PLANE, OWN), BF16),
        V((2 * ROWS, OWN), BF16),
        V((2 * ROWS, ADAPTER_RANK), BF16),
        V((3, 2 * ROWS, 128), F32),
        V((5, 3, 2 * ROWS, 128), F32),
        V((4, 3, 2 * ROWS, PLANE), BF16),
        V((3, 2 * ROWS, 128), F32),
        V((2 * ROWS, OWN), F32),
        V((2 * ROWS, OWN), BF16),
        V((4, ROWS, 128), BF16),
        V((4, 8, 128), F32),
        V((2, 8, 128), F32),
        V((2 * ROWS, OWN), BF16),
        V((2 * ROWS, OWN), BF16),
        V((2, ROWS, 128), BF16),
        V((4, ROWS, 128), BF16),
        V((2, 128, 1024), F32),
        V((128, 1024), BF16),
        V((128, 1024), BF16),
        V((128, 1024), BF16),
        V((2, 3, 32, 512), BF16),
        V((2, 32, 512), F32),
        V((2, 32, 512), BF16),
        V((2, 3, 32, 128), BF16),
        V((4, 2, 32, 128), BF16),
        V((2, 2, 2, 128, 512), BF16),
        pltpu.SemaphoreType.DMA((N_SEND,)),
        pltpu.SemaphoreType.DMA((N_RECV,)),
        pltpu.SemaphoreType.DMA((16,)),
    ]
    gradients, ratio = pl.pallas_call(
        body,
        out_shape=(
            jax.ShapeDtypeStruct((2, 2, 2, ADAPTER_RANK, 512), BF16),
            jax.ShapeDtypeStruct((1,), F32),
        ),
        in_specs=[smem] * 3 + [vmem] * 3 + [hbm] * 9,
        out_specs=(hbm, smem),
        scratch_shapes=scratch,
        compiler_params=pltpu.CompilerParams(
            collective_id=0, has_side_effects=True, vmem_limit_bytes=60 * 1024 * 1024
        ),
        cost_estimate=pl.CostEstimate(flops=12_000_000_000, bytes_accessed=24_000_000, transcendentals=13_000_000),
        name="policy_step",
    )(
        chosen, lengths, rollout_log_probability,
        trajectory.reshape(STEPS + 1, CLIPS, PAIRS, 128),
        rewards.reshape(1, -1), prompt_group_index.reshape(1, -1), timestep_norm_shift, patch_input_weight,
        velocity_output_weight.T, adapter_down_factor, adapter_up_factor,
        block_input.reshape(ROWS, MODEL_WIDTH), frozen_query_matrix, frozen_key_matrix, frozen_value_matrix,
    )
    return pl.pallas_call(
        update,
        out_shape=(
            jax.ShapeDtypeStruct((MODEL_WIDTH, ADAPTER_RANK), F32),
            jax.ShapeDtypeStruct((ADAPTER_RANK, 2 * OWN), F32),
            jax.ShapeDtypeStruct((1,), F32),
        ),
        in_specs=[hbm] * 3 + [smem],
        out_specs=(vmem, vmem, smem),
        scratch_shapes=[
            V((2, 2, 2, ADAPTER_RANK, 512), BF16),
            V((MODEL_WIDTH, ADAPTER_RANK), F32),
            V((ADAPTER_RANK, 2 * OWN), F32),
            pltpu.SemaphoreType.DMA((6,)),
        ],
        compiler_params=pltpu.CompilerParams(vmem_limit_bytes=61 * 1024 * 1024),
        name="update",
    )(gradients, adapter_down_factor, adapter_up_factor, ratio)


def solution(mesh):
    return jax.shard_map(
        shards,
        mesh=mesh,
        in_specs=(
            P(None, None, "seq", "dp", None),
            P("dp", "seq", None),
            P(), P(), P(), P(), P(), P(), P(),
            P(None, "section"),
            P(None, "section"),
            P(None, "section"),
            P("section", None),
            P(),
            P(None, "section"),
        ),
        out_specs=(P(), P(None, "section"), P("dp")),
        check_vma=False,
    )
```

```python
import functools
import math

import jax
import jax.numpy as jnp
from jax import lax
from jax.experimental import pallas as pl
from jax.experimental.pallas import tpu as pltpu
from jax.sharding import PartitionSpec as P

MESH = pl.DeviceIdType.MESH
F32 = jnp.float32
BF16 = jnp.bfloat16

MODEL_WIDTH = 3072
HD = 128
ADAPTER_RANK = 128
STEPS = 4
GROUP = 16
PATCH = 64
CLIPS = 4
ROWS = 256
PAIRS = 32
OWN = 384
PLANE = 1024
HALF = 1536

noise_level = 0.8
clip_range = 0.2
step_length = 256.0
norm_eps = 1e-06
masked_score = -1e30
step_size = 1.0 / (STEPS + 1)
input_scale = 1.0 / math.sqrt(MODEL_WIDTH)
out_scale = 1.0 / math.sqrt(ADAPTER_RANK)
head_scale = 1.0 / math.sqrt(HD)
query_scale = head_scale * math.log2(math.e)

NT = (((1,), (1,)), ((), ()))

R_X = 0
R_PAIR = 3
R_Z = 8
R_FAR = 16
R_CORE = 20
R_VEL = 36
R_SQ = 39
R_LOW = 43
R_RC = 46
R_S1 = 47
R_S2 = 53
R_RY = 59
R_G1 = 62
R_G2 = 68
R_GC = 74
N_RECV = 82
N_SEND = 96


def dot(a, b):
    return jnp.dot(a, b, preferred_element_type=F32)


def dot_nt(a, b):
    return lax.dot_general(a, b, NT, preferred_element_type=F32)


def iota(shape, dim):
    return lax.broadcasted_iota(jnp.int32, shape, dim)


def lanes(start, size):
    return pl.ds(pl.multiple_of(start, 128), size)


def rows_at(start, size, unit=256):
    return pl.ds(pl.multiple_of(start, unit), size)


def body(
    chosen_ref, lengths_ref, rollout_ref,
    traj_ref, rewards_ref, groups_ref,
    shift_hbm, patch_hbm, wout_hbm, down_hbm, up_hbm, x_hbm, wq_hbm, wk_hbm, wv_hbm,
    out_grad, out_ratio,
    shift_ref, patch_ref, wout_ref, down_ref, up_ref, xin, wk, wv, downb, upb, emb, normed,
    sel, latents, stage_k, stage_v, stage_q, keys, values, queries, low,
    top, peaks, probs, total, acc, attn, vel, squares, both, gout, gq, glow_send, glow,
    du, core_send, core_recv, xs, xr, slabs, slabs_send, zr, yr, full,
    send_sem, recv_sem, local_sem,
):
    sec = lax.axis_index("section")
    x = lax.axis_index("dp")
    seq = lax.axis_index("seq")
    z = seq // 4
    yl = (seq // 2) % 2
    core = seq % 2
    y = sec * 2 + yl

    def at(sec_, x_, z_, yl_, core_):
        return (sec_, x_, z_ * 4 + yl_ * 2 + core_)

    def y_peer(step):
        other = (y + step) % 4
        return other, at(other // 2, x, z, other % 2, core)

    other_core = at(sec, x, z, yl, 1 - core)
    partner = at(sec, x, z, 1 - yl, core)
    z_up = at(sec, x, (z + 1) % 4, yl, core)
    z_down = at(sec, x, (z + 3) % 4, yl, core)

    pending = []

    def descriptor(src, dst, send_index, recv_index, device):
        return pltpu.make_async_remote_copy(
            src_ref=src, dst_ref=dst, send_sem=send_sem.at[send_index], recv_sem=recv_sem.at[recv_index],
            device_id=device, device_id_type=MESH,
        )

    def send(src, dst, recv_index, device):
        copy = descriptor(src, dst, len(pending), recv_index, device)
        copy.start()
        pending.append(copy)

    def arrive(dst, recv_index):
        descriptor(dst, dst, 0, recv_index, other_core).wait_recv()

    loads = []

    def load(src, dst):
        copy = pltpu.make_async_copy(src, dst, local_sem.at[len(loads)])
        copy.start()
        loads.append(copy)
        return copy


    peers = [at(sec, (x + d) % 4, z, yl, core) for d in (1, 2, 3)]
    peers += [at(sec, x, (z + d) % 4, yl, core) for d in (1, 2, 3)]
    peers += [y_peer(d)[1] for d in (1, 2, 3)]
    peers += [other_core]
    barrier = pltpu.get_barrier_semaphore()
    for peer in peers:
        pl.semaphore_signal(barrier, inc=1, device_id=peer, device_id_type=MESH)

    load_x = [load(x_hbm, xin), load(patch_hbm, patch_ref), load(shift_hbm, shift_ref)]
    own_cols, other_cols = lanes(yl * OWN, OWN), lanes((1 - yl) * OWN, OWN)

    def load_weight(src, dst):
        return load(src.at[:, own_cols], dst.at[:, 0:OWN]), load(src.at[:, other_cols], dst.at[:, OWN : 2 * OWN])

    load_w = [load_weight(wk_hbm, wk), load_weight(wv_hbm, wv)]
    load_adapter = [load(down_hbm, down_ref), load(up_hbm, up_ref), load(wout_hbm.at[:, own_cols], wout_ref)]

    for c in range(CLIPS):
        sel[c, 0] = traj_ref[chosen_ref[c], c]
        sel[c, 1] = traj_ref[chosen_ref[c] + 1, c]
    pl.semaphore_wait(barrier, len(peers))
    x_rows = rows_at(x * PAIRS, PAIRS, PAIRS)
    for d in (1, 2, 3):
        to = (x + d) % 4
        send(sel.at[to], latents.at[yl, :, x_rows, :], R_X + d - 1, at(sec, to, z, yl, core))
    latents[yl, :, x_rows, :] = sel[x]

    chosen = chosen_ref[x]
    length = lengths_ref[x]
    one = jnp.ones((1, 1), F32)
    spread = noise_level * jnp.sqrt(step_size * (1.0 - one * chosen.astype(F32) * step_size))
    count = one * (length * PATCH).astype(F32)

    def repeat(stat, count):
        return jnp.concatenate([stat] * count, axis=1)

    def fold_lanes(op, tile):
        out = tile[:, 0:128]
        for j in range(1, tile.shape[1] // 128):
            out = op(out, tile[:, j * 128 : (j + 1) * 128])
        return out

    expand = jnp.where((iota((ROWS, 128), 0) >> 1) == iota((ROWS, 128), 1), 1.0, 0.0).astype(BF16)
    own_half = (iota((ROWS, 128), 1) >> 6) == (iota((ROWS, 128), 0) & 1)

    def token_rows(pairs):
        return jnp.where(own_half, dot(expand, pairs), 0.0).astype(BF16)

    def fold(offset, width):
        source = (iota((128, width), 0) & 63) + offset
        return jnp.where(source == iota((128, width), 1), 1.0, 0.0).astype(BF16)

    for d in (1, 2, 3):
        src_rows = rows_at(((x + 4 - d) % 4) * PAIRS, PAIRS, PAIRS)
        arrive(latents.at[yl, :, src_rows, :], R_X + d - 1)
    send(latents.at[yl], latents.at[yl], R_PAIR + 4, partner)

    now_tokens = dot(token_rows(latents[yl, 0]), fold(0, 64)).astype(BF16)
    for copy in load_x:
        copy.wait()
    squares_sum = jnp.zeros((ROWS, 128), F32)
    chunk = 512
    for j in range(MODEL_WIDTH // chunk):
        cols = slice(j * chunk, (j + 1) * chunk)
        part = xin[:, cols].astype(F32) + dot(now_tokens, patch_ref[:, cols])
        emb[:, cols] = part
        squares_sum += fold_lanes(jnp.add, part * part)
    mean_square = jnp.sum(squares_sum, axis=1, keepdims=True) * (1.0 / MODEL_WIDTH)
    inverse = repeat(jnp.broadcast_to(lax.rsqrt(mean_square + norm_eps), (ROWS, 128)), chunk // 128)
    for j in range(MODEL_WIDTH // chunk):
        cols = slice(j * chunk, (j + 1) * chunk)
        shift = shift_ref[chosen, 0:1, cols]
        scale = 1.0 + shift_ref[chosen, 1:2, cols]
        normed[:, cols] = (emb[:, cols] * inverse * scale + shift).astype(BF16)

    seq_own = seq * ROWS
    seq_pair = (seq + 2 - 4 * yl) * ROWS

    def block(ref, z_, yl_, core_):
        return ref.at[rows_at((z_ * 4 + yl_ * 2 + core_) * ROWS, ROWS), :]

    def project(weight, loaded, stage, extra=None, scale=None):
        for copy in loaded:
            copy.wait()

        def step(n, carry):
            cols = lanes(n * 256, 256)
            part = dot(normed[...], weight[:, cols])
            if extra is not None:
                part = (part + dot(extra, upb[:, cols]) * out_scale) * scale
            stage[:, cols] = part.astype(BF16)
            return carry

        lax.fori_loop(0, 3, step, 0)

    store = (keys, values)

    def core_index(plane, pair, kv):
        return R_CORE + plane * 4 + pair * 2 + kv

    def to_core(plane, pair, kv):
        z_ = (z + plane) % 4
        yl_ = yl if pair == 0 else 1 - yl
        send(block(store[kv], z_, yl_, core), block(store[kv], z_, yl_, core), core_index(plane, pair, kv), other_core)

    def from_core(plane, pairs=(0, 1)):
        z_ = (z + plane) % 4
        for pair in pairs:
            yl_ = yl if pair == 0 else 1 - yl
            for kv in (0, 1):
                arrive(block(store[kv], z_, yl_, 1 - core), core_index(plane, pair, kv))

    def z_index(pair, kv, above):
        return R_Z + pair * 4 + kv * 2 + above

    def to_z(pair, kv):
        src = block(store[kv], z, yl if pair == 0 else 1 - yl, core)
        send(src, src, z_index(pair, kv, 0), z_up)
        send(src, src, z_index(pair, kv, 1), z_down)

    def from_z(pair, kv, above):
        z_ = (z + 1) % 4 if above else (z + 3) % 4
        src = block(store[kv], z_, yl if pair == 0 else 1 - yl, core)
        arrive(src, z_index(pair, kv, above))
        if kv == 0 and not above:
            send(src, src, R_FAR + pair * 2 + kv, z_up)
        if kv == 1 and above:
            send(src, src, R_FAR + pair * 2 + kv, z_down)
        to_core(1 if above else 3, pair, kv)

    def from_far(pair, kv):
        arrive(block(store[kv], (z + 2) % 4, yl if pair == 0 else 1 - yl, core), R_FAR + pair * 2 + kv)
        to_core(2, pair, kv)

    own_block = rows_at(seq_own, ROWS)
    for kv, (weight, stage) in enumerate(((wk, stage_k), (wv, stage_v))):
        project(weight, load_w[kv], stage)
        send(stage.at[:, OWN : 2 * OWN], block(store[kv], z, yl, core), R_PAIR + kv, partner)
        store[kv][own_block, :] = stage[:, 0:OWN]
        to_z(0, kv)
        to_core(0, 0, kv)
        if kv == 0:
            load_w.append(load_weight(wq_hbm, wk))
    own_rows = rows_at(yl * ROWS, ROWS)
    pair_rows = rows_at((1 - yl) * ROWS, ROWS)
    for copy in load_adapter:
        copy.wait()
    downb[...] = down_ref[...].astype(BF16)
    upb[:, 0:OWN] = up_ref[:, own_cols].astype(BF16)
    upb[:, OWN : 2 * OWN] = up_ref[:, other_cols].astype(BF16)
    low_own = (dot(normed[...], downb[...]) * input_scale).astype(BF16)
    low[own_rows, :] = low_own
    project(wk, load_w[2], stage_q, low_own, query_scale)
    send(stage_q.at[:, OWN : 2 * OWN], queries.at[own_rows, :], R_PAIR + 2, partner)
    queries[own_rows, :] = stage_q[:, 0:OWN]
    send(low.at[own_rows, :], low.at[own_rows, :], R_PAIR + 3, partner)
    for kv in (0, 1):
        arrive(block(store[kv], z, 1 - yl, core), R_PAIR + kv)
        to_z(1, kv)
        to_core(0, 1, kv)

    def key_bias(start, width):
        return jnp.where(start + iota((1, width), 1) < length, 0.0, masked_score)

    def forward_part(plane, slot, offset, width):
        start = ((z + plane) % 4) * PLANE + offset
        plane_rows = rows_at(start, width, width)
        bias = key_bias(start, width)
        first = plane == 0
        tiles = [(h, slice(h * HD, (h + 1) * HD), slice(b * ROWS, (b + 1) * ROWS)) for h in range(3) for b in (0, 1)]

        def score(tile):
            _, cols, rows = tile
            return dot_nt(queries[rows, cols], keys[plane_rows, cols]) + bias

        def softmax(tile, scores):
            head, cols, rows = tile
            peak = jnp.max(fold_lanes(jnp.maximum, scores), axis=1, keepdims=True)
            peak = jnp.broadcast_to(peak, (ROWS, 128))
            if not first:
                before = top[head, rows, :]
                peak = jnp.maximum(peak, before)
            exp_scores = jnp.exp2(scores - repeat(peak, width // 128))
            sums = fold_lanes(jnp.add, exp_scores)
            kept = exp_scores.astype(BF16)
            probs[plane, head, rows, lanes(offset, width)] = kept
            weighted = dot(kept, values[plane_rows, cols])
            if not first:
                decay = jnp.exp2(before - peak)
                sums += decay * total[head, rows, :]
                weighted += decay * acc[rows, cols]
            top[head, rows, :] = peak
            peaks[slot, head, rows, :] = peak
            total[head, rows, :] = sums
            acc[rows, cols] = weighted

        scores = score(tiles[0])
        for i, tile in enumerate(tiles):
            ahead = score(tiles[i + 1]) if i + 1 < len(tiles) else None
            softmax(tile, scores)
            scores = ahead

    for kv in (0, 1):
        for above in (0, 1):
            from_z(0, kv, above)
    arrive(queries.at[pair_rows, :], R_PAIR + 2)
    from_core(0)
    forward_part(0, 0, 0, PLANE)
    for kv in (0, 1):
        for above in (0, 1):
            from_z(1, kv, above)
    from_core(1)
    forward_part(1, 1, 0, PLANE)
    from_far(0, 0)
    from_far(0, 1)
    from_core(3)
    forward_part(3, 3, 0, PLANE)
    from_core(2, (0,))
    forward_part(2, 2, yl * 512, 512)
    from_far(1, 0)
    from_far(1, 1)
    from_core(2, (1,))
    forward_part(2, 4, (1 - yl) * 512, 512)

    for head in range(3):
        cols = slice(head * HD, (head + 1) * HD)
        sums = jnp.broadcast_to(jnp.sum(total[head], axis=1, keepdims=True), (2 * ROWS, 128))
        attn[:, cols] = (acc[:, cols] / sums).astype(BF16)
        top[head] = top[head] + jnp.log(sums) * math.log2(math.e)

    blank = jnp.zeros((PATCH, OWN), BF16)
    wide = [jnp.concatenate([wout_ref[...], blank], axis=0), jnp.concatenate([blank, wout_ref[...]], axis=0)]
    partial = dot_nt(attn[0:ROWS, :], wide[0]) + dot_nt(attn[ROWS : 2 * ROWS, :], wide[1])
    vel[y] = partial.astype(BF16)
    for d in (2, 1, 3):
        send(vel.at[y], vel.at[y], R_VEL + d - 1, y_peer(d)[1])
    arrive(latents.at[1 - yl], R_PAIR + 4)
    arrive(low.at[pair_rows, :], R_PAIR + 3)
    moved = jnp.zeros((ROWS, 128), F32)
    for b in (0, 1):
        moved += dot(token_rows(latents[b, 1]), fold(PATCH * b, 128))
        moved -= dot(token_rows(latents[b, 0]), fold(PATCH * b, 128))
    lane_block = iota((ROWS, 128), 1) >> 6
    position = (z * 4 + lane_block * 2 + core) * ROWS + iota((ROWS, 128), 0)
    live = position < length
    for d in (1, 2, 3):
        arrive(vel.at[(y + 4 - d) % 4], R_VEL + d - 1)
    velocity = jnp.zeros((ROWS, 128), F32)
    for b in range(4):
        velocity += vel[b].astype(F32)
    zscore = (moved + step_size * velocity) / spread
    own_squares = jnp.where(live, zscore * zscore, 0.0)
    squares[z] = jnp.sum(own_squares.reshape(ROWS // 8, 8, 128), axis=0)
    for d in (1, 2, 3):
        send(squares.at[z], squares.at[z], R_SQ + d - 1, at(sec, x, (z + d) % 4, yl, core))

    grad_vel = jnp.where(live, -zscore * step_size / (spread * count), 0.0).astype(BF16)
    for b in (0, 1):
        gout[b * ROWS : (b + 1) * ROWS, :] = dot(grad_vel, wide[b]).astype(BF16)

    for head in range(3):
        cols = slice(head * HD, (head + 1) * HD)
        delta = jnp.sum(gout[:, cols].astype(F32) * attn[:, cols].astype(F32), axis=1, keepdims=True)
        total[head] = jnp.broadcast_to(delta, (2 * ROWS, 128))
    acc[...] = jnp.zeros_like(acc)

    def backward_plane(plane, carry):
        plane_rows = rows_at(((z + plane) % 4) * PLANE, PLANE, PLANE)
        slots = [jnp.where((plane == 2) & (yl == 1 - b), 4, plane) for b in (0, 1)]

        def product(head):
            cols = slice(head * HD, (head + 1) * HD)
            return dot_nt(gout[:, cols], values[plane_rows, cols])

        def gradient(head, grad_probs):
            cols = slice(head * HD, (head + 1) * HD)
            scale = jnp.concatenate(
                [repeat(jnp.exp2(peaks[slot, head] - top[head]), 4) for slot in slots], axis=1
            )
            grad_scores = (grad_probs - repeat(total[head], PLANE // 128)) * scale
            grad_scores = (probs[plane, head].astype(F32) * grad_scores).astype(BF16)
            acc[:, cols] += dot(grad_scores, keys[plane_rows, cols])

        made = product(0)
        for head in range(3):
            ahead = product(head + 1) if head < 2 else None
            gradient(head, made)
            made = ahead
        return carry

    lax.fori_loop(0, 2, backward_plane, 0)
    for d in (1, 2, 3):
        arrive(squares.at[(z + 4 - d) % 4], R_SQ + d - 1)
    plane_squares = jnp.zeros((8, 128), F32)
    for b in range(4):
        plane_squares += squares[b]
    both[core] = plane_squares
    send(both.at[core], both.at[core], R_SQ + 3, other_core)
    lax.fori_loop(2, 4, backward_plane, 0)

    batch = rewards_ref.shape[1]
    reward = rewards_ref[...].astype(F32)
    group = groups_ref[...].astype(F32)
    mine = iota((1, batch), 1) == x
    own_group = jnp.sum(jnp.where(mine, group, 0.0), axis=1, keepdims=True)
    own_reward = jnp.sum(jnp.where(mine, reward, 0.0), axis=1, keepdims=True)
    member = jnp.where(group == own_group, 1.0, 0.0)
    mean = jnp.sum(member * reward, axis=1, keepdims=True) / GROUP
    centered = reward - mean
    variance = jnp.sum(member * centered * centered, axis=1, keepdims=True) / GROUP
    advantage = (own_reward - mean) / (jnp.sqrt(variance) + 1.0)

    arrive(both.at[1 - core], R_SQ + 3)
    clip_squares = both[0] + both[1]
    clip_squares = jnp.sum(jnp.sum(clip_squares, axis=1, keepdims=True), axis=0, keepdims=True)
    ratio = jnp.exp(-0.5 * clip_squares / count - one * rollout_ref[x])
    out_ratio[0] = jnp.sum(ratio)
    low_edge, high_edge = 1.0 - clip_range, 1.0 + clip_range
    inside = (ratio >= low_edge) & (ratio <= high_edge)
    active = inside | ((advantage > 0) & (ratio < low_edge)) | ((advantage < 0) & (ratio > high_edge))
    weight = jnp.where(active, -advantage * ratio / float(CLIPS), 0.0)

    gq[...] = (acc[...] * (head_scale * weight)).astype(BF16)

    for b in (0, 1):
        part = dot_nt(gq[b * ROWS : (b + 1) * ROWS, :], upb[:, 0:OWN]) * out_scale
        glow_send[b] = part.astype(BF16)
    for d in (2, 1, 3):
        other, device = y_peer(d)
        send(glow_send.at[other % 2], glow.at[y], R_LOW + d - 1, device)
    glow[y] = glow_send[yl]
    up_part = dot(jnp.transpose(low[...].astype(F32)).astype(BF16), gq[...])
    du[0, :, 768:1024] = up_part[:, 0:256]
    du[1, :, 768:896] = up_part[:, 256:384]
    du[1, :, 896:1024] = jnp.zeros((128, 128), F32)
    for d in (1, 2, 3):
        arrive(glow.at[(y + 4 - d) % 4], R_LOW + d - 1)
    low_sum = jnp.zeros((ROWS, 128), F32)
    for b in range(4):
        low_sum += glow[b].astype(F32)
    low_turned = jnp.transpose(low_sum).astype(BF16)

    for half in (1, 0):
        where = (core + half) % 2
        for j in range(3):
            cols = lanes(sec * HALF + where * 768 + j * 256, 256)
            du[where, :, j * 256 : (j + 1) * 256] = dot(low_turned, normed[:, cols])
        if half == 1:
            core_send[...] = du[where].astype(BF16)
            send(core_send, core_recv, R_RC, other_core)
    arrive(core_recv, R_RC)
    summed = du[core] + core_recv[...].astype(F32)
    du[core] = summed
    xs[...] = summed.astype(BF16)

    spots = (x, z)

    def along(half, step):
        if half == 0:
            other = (x + step) % 4
            return other, at(sec, other, z, yl, core)
        other = (z + step) % 4
        return other, at(sec, x, other, yl, core)

    def slab(index):
        return rows_at(index * 32, 32, 32)

    def piece_cols(index):
        return lanes(index * 128, 128)

    for d in (2, 1, 3):
        for half in (0, 1):
            other, device = along(half, d)
            send(xs.at[slab(other), half * 512 : (half + 1) * 512], xr.at[half, d - 1], R_S1 + half * 3 + d - 1, device)
    for half in (0, 1):
        part = du[core, slab(spots[half]), half * 512 : (half + 1) * 512]
        for d in (1, 2, 3):
            arrive(xr.at[half, d - 1], R_S1 + half * 3 + d - 1)
            part += xr[half, d - 1].astype(F32)
        slabs[half] = part
        slabs_send[half] = part.astype(BF16)
        for d in (2, 1, 3):
            other, device = along(1 - half, d)
            send(slabs_send.at[half, :, piece_cols(other)], zr.at[half, d - 1], R_S2 + half * 3 + d - 1, device)
    for half in (0, 1):
        part = slabs[half, :, piece_cols(spots[1 - half])]
        for d in (1, 2, 3):
            arrive(zr.at[half, d - 1], R_S2 + half * 3 + d - 1)
            part += zr[half, d - 1].astype(F32)
        yr[y, half] = part.astype(BF16)
    for d in (2, 1, 3):
        send(yr.at[y], yr.at[y], R_RY + d - 1, y_peer(d)[1])
    for d in (1, 2, 3):
        arrive(yr.at[(y + 4 - d) % 4], R_RY + d - 1)
    for b in (0, 1):
        sums = yr[2 * b].astype(F32) + yr[2 * b + 1].astype(F32)
        full[core, 0, b, slab(x), piece_cols(z)] = sums[0].astype(BF16)
        full[core, 1, b, slab(z), piece_cols(x)] = jnp.where(x < 2, sums[1], yr[sec * 2 + b, 1].astype(F32)).astype(BF16)

    for d in (2, 1, 3):
        for half in (0, 1):
            mine_ = full.at[core, half, :, slab(spots[half]), piece_cols(spots[1 - half])]
            send(mine_, mine_, R_G1 + half * 3 + d - 1, along(1 - half, d)[1])
    for half in (0, 1):
        for d in (1, 2, 3):
            source = along(1 - half, 4 - d)[0]
            arrive(full.at[core, half, :, slab(spots[half]), piece_cols(source)], R_G1 + half * 3 + d - 1)
        mine_ = full.at[core, half, :, slab(spots[half]), :]
        for d in (2, 1, 3):
            send(mine_, mine_, R_G2 + half * 3 + d - 1, along(half, d)[1])
        send(mine_, mine_, R_GC + half * 4, other_core)
    for d in (1, 3, 2):
        for half in (0, 1):
            source = slab(along(half, 4 - d)[0])
            theirs = full.at[core, half, :, source, :]
            arrive(theirs, R_G2 + half * 3 + d - 1)
            send(theirs, theirs, R_GC + half * 4 + d, other_core)
    handed = [load(full.at[core], out_grad.at[core])]
    for d in (0, 1, 2, 3):
        for half in (0, 1):
            arrive(full.at[1 - core, half, :, slab(along(half, 4 - d)[0]), :], R_GC + half * 4 + d)
    handed.append(load(full.at[1 - core], out_grad.at[1 - core]))

    for copy in handed:
        copy.wait()
    for copy in pending:
        copy.wait_send()


def update(grad_ref, down_ref, up_ref, ratio_ref, out_hbm, out_up, out_ratio, out_down, out_sem):
    norm_sum = jnp.zeros((128, 256), F32)
    for core in (0, 1):
        for half, width in ((0, 512), (1, 256)):
            for sec in (0, 1):
                for j in range(width // 256):
                    part = grad_ref[core, half, sec, :, j * 256 : (j + 1) * 256].astype(F32)
                    norm_sum += part * part
    norm_sum = jnp.sum(jnp.sum(norm_sum, axis=1, keepdims=True), axis=0, keepdims=True)
    factor = step_length / jnp.sqrt(norm_sum * (input_scale * input_scale) + norm_eps)
    down_factor, up_factor = factor * input_scale, factor * out_scale
    written = []
    for t in range(MODEL_WIDTH // 128):
        sec, core, j = t // 12, (t % 12) // 6, t % 6
        half, start = j // 4, (j % 4) * 128
        part = grad_ref[core, half, sec, :, start : start + 128].astype(F32)
        rows = slice(t * 128, (t + 1) * 128)
        out_down[rows, :] = down_ref[rows, :] - down_factor * jnp.transpose(part)
        if t % 6 == 5:
            rows = slice((t - 5) * 128, (t + 1) * 128)
            written.append(pltpu.make_async_copy(out_down.at[rows, :], out_hbm.at[rows, :], out_sem.at[t // 6]))
            written[-1].start()
    for b in (0, 1):
        for core, width in ((0, 256), (1, 128)):
            cols = slice(b * OWN + core * 256, b * OWN + core * 256 + width)
            part = grad_ref[core, 1, b, :, 256 : 256 + width].astype(F32)
            out_up[:, cols] = up_ref[:, cols] - up_factor * part
    out_ratio[0] = ratio_ref[0]
    for copy in written:
        copy.wait()


def shards(
    trajectory, block_input, chosen, lengths, rewards, prompt_group_index, rollout_log_probability,
    timestep_norm_shift, patch_input_weight, frozen_query_matrix, frozen_key_matrix, frozen_value_matrix,
    velocity_output_weight, adapter_down_factor, adapter_up_factor,
):
    vmem = pl.BlockSpec(memory_space=pltpu.VMEM)
    smem = pl.BlockSpec(memory_space=pltpu.SMEM)
    hbm = pl.BlockSpec(memory_space=pl.ANY)
    V = pltpu.VMEM
    scratch = [
        V((STEPS, 2, MODEL_WIDTH), F32),
        V((PATCH, MODEL_WIDTH), BF16),
        V((PATCH, OWN), BF16),
        V((MODEL_WIDTH, ADAPTER_RANK), F32),
        V((ADAPTER_RANK, 2 * OWN), F32),
        V((ROWS, MODEL_WIDTH), BF16),
        V((MODEL_WIDTH, 2 * OWN), BF16),
        V((MODEL_WIDTH, 2 * OWN), BF16),
        V((MODEL_WIDTH, ADAPTER_RANK), BF16),
        V((ADAPTER_RANK, 2 * OWN), BF16),
        V((ROWS, MODEL_WIDTH), F32),
        V((ROWS, MODEL_WIDTH), BF16),
        V((CLIPS, 2, PAIRS, 128), BF16),
        V((2, 2, 128, 128), BF16),
        V((ROWS, 2 * OWN), BF16),
        V((ROWS, 2 * OWN), BF16),
        V((ROWS, 2 * OWN), BF16),
        V((4 * PLANE, OWN), BF16),
        V((4 * PLANE, OWN), BF16),
        V((2 * ROWS, OWN), BF16),
        V((2 * ROWS, ADAPTER_RANK), BF16),
        V((3, 2 * ROWS, 128), F32),
        V((5, 3, 2 * ROWS, 128), F32),
        V((4, 3, 2 * ROWS, PLANE), BF16),
        V((3, 2 * ROWS, 128), F32),
        V((2 * ROWS, OWN), F32),
        V((2 * ROWS, OWN), BF16),
        V((4, ROWS, 128), BF16),
        V((4, 8, 128), F32),
        V((2, 8, 128), F32),
        V((2 * ROWS, OWN), BF16),
        V((2 * ROWS, OWN), BF16),
        V((2, ROWS, 128), BF16),
        V((4, ROWS, 128), BF16),
        V((2, 128, 1024), F32),
        V((128, 1024), BF16),
        V((128, 1024), BF16),
        V((128, 1024), BF16),
        V((2, 3, 32, 512), BF16),
        V((2, 32, 512), F32),
        V((2, 32, 512), BF16),
        V((2, 3, 32, 128), BF16),
        V((4, 2, 32, 128), BF16),
        V((2, 2, 2, 128, 512), BF16),
        pltpu.SemaphoreType.DMA((N_SEND,)),
        pltpu.SemaphoreType.DMA((N_RECV,)),
        pltpu.SemaphoreType.DMA((16,)),
    ]
    gradients, ratio = pl.pallas_call(
        body,
        out_shape=(
            jax.ShapeDtypeStruct((2, 2, 2, ADAPTER_RANK, 512), BF16),
            jax.ShapeDtypeStruct((1,), F32),
        ),
        in_specs=[smem] * 3 + [vmem] * 3 + [hbm] * 9,
        out_specs=(hbm, smem),
        scratch_shapes=scratch,
        compiler_params=pltpu.CompilerParams(
            collective_id=0, has_side_effects=True, vmem_limit_bytes=60 * 1024 * 1024
        ),
        cost_estimate=pl.CostEstimate(flops=12_000_000_000, bytes_accessed=24_000_000, transcendentals=13_000_000),
        name="policy_step",
    )(
        chosen, lengths, rollout_log_probability,
        trajectory.reshape(STEPS + 1, CLIPS, PAIRS, 128),
        rewards.reshape(1, -1), prompt_group_index.reshape(1, -1), timestep_norm_shift, patch_input_weight,
        velocity_output_weight.T, adapter_down_factor, adapter_up_factor,
        block_input.reshape(ROWS, MODEL_WIDTH), frozen_query_matrix, frozen_key_matrix, frozen_value_matrix,
    )
    return pl.pallas_call(
        update,
        out_shape=(
            jax.ShapeDtypeStruct((MODEL_WIDTH, ADAPTER_RANK), F32),
            jax.ShapeDtypeStruct((ADAPTER_RANK, 2 * OWN), F32),
            jax.ShapeDtypeStruct((1,), F32),
        ),
        in_specs=[vmem] * 3 + [smem],
        out_specs=(hbm, vmem, smem),
        scratch_shapes=[
            V((MODEL_WIDTH, ADAPTER_RANK), F32),
            pltpu.SemaphoreType.DMA((4,)),
        ],
        compiler_params=pltpu.CompilerParams(vmem_limit_bytes=32 * 1024 * 1024),
        name="update",
    )(gradients, adapter_down_factor, adapter_up_factor, ratio)


def solution(mesh):
    return jax.shard_map(
        shards,
        mesh=mesh,
        in_specs=(
            P(None, None, "seq", "dp", None),
            P("dp", "seq", None),
            P(), P(), P(), P(), P(), P(), P(),
            P(None, "section"),
            P(None, "section"),
            P(None, "section"),
            P("section", None),
            P(),
            P(None, "section"),
        ),
        out_specs=(P(), P(None, "section"), P("dp")),
        check_vma=False,
    )
```

```python
import functools
import math

import jax
import jax.numpy as jnp
from jax import lax
from jax.experimental import pallas as pl
from jax.experimental.pallas import tpu as pltpu
from jax.sharding import PartitionSpec as P

MESH = pl.DeviceIdType.MESH
F32 = jnp.float32
BF16 = jnp.bfloat16

MODEL_WIDTH = 3072
HD = 128
ADAPTER_RANK = 128
STEPS = 4
GROUP = 16
PATCH = 64
CLIPS = 4
ROWS = 256
PAIRS = 32
OWN = 384
PLANE = 1024
HALF = 1536

noise_level = 0.8
clip_range = 0.2
step_length = 256.0
norm_eps = 1e-06
masked_score = -1e30
step_size = 1.0 / (STEPS + 1)
input_scale = 1.0 / math.sqrt(MODEL_WIDTH)
out_scale = 1.0 / math.sqrt(ADAPTER_RANK)
head_scale = 1.0 / math.sqrt(HD)
query_scale = head_scale * math.log2(math.e)

NT = (((1,), (1,)), ((), ()))

R_X = 0
R_PAIR = 3
R_Z = 8
R_FAR = 16
R_CORE = 20
R_VEL = 36
R_SQ = 39
R_LOW = 43
R_RC = 46
R_S1 = 47
R_S2 = 53
R_RY = 59
R_G1 = 62
R_G2 = 68
R_GC = 74
N_RECV = 82
N_SEND = 96


def dot(a, b):
    return jnp.dot(a, b, preferred_element_type=F32)


def dot_nt(a, b):
    return lax.dot_general(a, b, NT, preferred_element_type=F32)


def iota(shape, dim):
    return lax.broadcasted_iota(jnp.int32, shape, dim)


def lanes(start, size):
    return pl.ds(pl.multiple_of(start, 128), size)


def rows_at(start, size, unit=256):
    return pl.ds(pl.multiple_of(start, unit), size)


def body(
    chosen_ref, lengths_ref, rollout_ref,
    traj_ref, rewards_ref, groups_ref,
    shift_hbm, patch_hbm, wout_hbm, down_hbm, up_hbm, x_hbm, wq_hbm, wk_hbm, wv_hbm,
    out_grad, out_ratio,
    shift_ref, patch_ref, wout_ref, down_ref, up_ref, xin, wk, wv, downb, upb, emb, normed,
    sel, latents, stage_k, stage_v, stage_q, keys, values, queries, low,
    top, peaks, probs, total, acc, attn, vel, squares, both, gout, gq, glow_send, glow,
    du, core_send, core_recv, xs, xr, slabs, slabs_send, zr, yr, full,
    send_sem, recv_sem, local_sem,
):
    sec = lax.axis_index("section")
    x = lax.axis_index("dp")
    seq = lax.axis_index("seq")
    z = seq // 4
    yl = (seq // 2) % 2
    core = seq % 2
    y = sec * 2 + yl

    def at(sec_, x_, z_, yl_, core_):
        return (sec_, x_, z_ * 4 + yl_ * 2 + core_)

    def y_peer(step):
        other = (y + step) % 4
        return other, at(other // 2, x, z, other % 2, core)

    other_core = at(sec, x, z, yl, 1 - core)
    partner = at(sec, x, z, 1 - yl, core)
    z_up = at(sec, x, (z + 1) % 4, yl, core)
    z_down = at(sec, x, (z + 3) % 4, yl, core)

    pending = []

    def descriptor(src, dst, send_index, recv_index, device):
        return pltpu.make_async_remote_copy(
            src_ref=src, dst_ref=dst, send_sem=send_sem.at[send_index], recv_sem=recv_sem.at[recv_index],
            device_id=device, device_id_type=MESH,
        )

    def send(src, dst, recv_index, device):
        copy = descriptor(src, dst, len(pending), recv_index, device)
        copy.start()
        pending.append(copy)

    def arrive(dst, recv_index):
        descriptor(dst, dst, 0, recv_index, other_core).wait_recv()

    loads = []

    def load(src, dst):
        copy = pltpu.make_async_copy(src, dst, local_sem.at[len(loads)])
        copy.start()
        loads.append(copy)
        return copy


    peers = [at(sec, (x + d) % 4, z, yl, core) for d in (1, 2, 3)]
    peers += [at(sec, x, (z + d) % 4, yl, core) for d in (1, 2, 3)]
    peers += [y_peer(d)[1] for d in (1, 2, 3)]
    peers += [other_core]
    barrier = pltpu.get_barrier_semaphore()
    for peer in peers:
        pl.semaphore_signal(barrier, inc=1, device_id=peer, device_id_type=MESH)

    load_x = [load(x_hbm, xin), load(patch_hbm, patch_ref), load(shift_hbm, shift_ref)]
    own_cols, other_cols = lanes(yl * OWN, OWN), lanes((1 - yl) * OWN, OWN)

    def load_weight(src, dst):
        return load(src.at[:, own_cols], dst.at[:, 0:OWN]), load(src.at[:, other_cols], dst.at[:, OWN : 2 * OWN])

    load_w = [load_weight(wk_hbm, wk), load_weight(wv_hbm, wv)]
    load_adapter = [load(down_hbm, down_ref), load(up_hbm, up_ref), load(wout_hbm.at[:, own_cols], wout_ref)]

    for c in range(CLIPS):
        sel[c, 0] = traj_ref[chosen_ref[c], c]
        sel[c, 1] = traj_ref[chosen_ref[c] + 1, c]
    pl.semaphore_wait(barrier, len(peers))
    x_rows = rows_at(x * PAIRS, PAIRS, PAIRS)
    for d in (1, 2, 3):
        to = (x + d) % 4
        send(sel.at[to], latents.at[yl, :, x_rows, :], R_X + d - 1, at(sec, to, z, yl, core))
    latents[yl, :, x_rows, :] = sel[x]

    chosen = chosen_ref[x]
    length = lengths_ref[x]
    one = jnp.ones((1, 1), F32)
    spread = noise_level * jnp.sqrt(step_size * (1.0 - one * chosen.astype(F32) * step_size))
    count = one * (length * PATCH).astype(F32)

    def repeat(stat, count):
        return jnp.concatenate([stat] * count, axis=1)

    def fold_lanes(op, tile):
        out = tile[:, 0:128]
        for j in range(1, tile.shape[1] // 128):
            out = op(out, tile[:, j * 128 : (j + 1) * 128])
        return out

    expand = jnp.where((iota((ROWS, 128), 0) >> 1) == iota((ROWS, 128), 1), 1.0, 0.0).astype(BF16)
    own_half = (iota((ROWS, 128), 1) >> 6) == (iota((ROWS, 128), 0) & 1)

    def token_rows(pairs):
        return jnp.where(own_half, dot(expand, pairs), 0.0).astype(BF16)

    def fold(offset, width):
        source = (iota((128, width), 0) & 63) + offset
        return jnp.where(source == iota((128, width), 1), 1.0, 0.0).astype(BF16)

    for d in (1, 2, 3):
        src_rows = rows_at(((x + 4 - d) % 4) * PAIRS, PAIRS, PAIRS)
        arrive(latents.at[yl, :, src_rows, :], R_X + d - 1)
    send(latents.at[yl], latents.at[yl], R_PAIR + 4, partner)

    now_tokens = dot(token_rows(latents[yl, 0]), fold(0, 64)).astype(BF16)
    for copy in load_x:
        copy.wait()
    squares_sum = jnp.zeros((ROWS, 128), F32)
    chunk = 512
    for j in range(MODEL_WIDTH // chunk):
        cols = slice(j * chunk, (j + 1) * chunk)
        part = xin[:, cols].astype(F32) + dot(now_tokens, patch_ref[:, cols])
        emb[:, cols] = part
        squares_sum += fold_lanes(jnp.add, part * part)
    mean_square = jnp.sum(squares_sum, axis=1, keepdims=True) * (1.0 / MODEL_WIDTH)
    inverse = repeat(jnp.broadcast_to(lax.rsqrt(mean_square + norm_eps), (ROWS, 128)), chunk // 128)
    for j in range(MODEL_WIDTH // chunk):
        cols = slice(j * chunk, (j + 1) * chunk)
        shift = shift_ref[chosen, 0:1, cols]
        scale = 1.0 + shift_ref[chosen, 1:2, cols]
        normed[:, cols] = (emb[:, cols] * inverse * scale + shift).astype(BF16)

    seq_own = seq * ROWS
    seq_pair = (seq + 2 - 4 * yl) * ROWS

    def block(ref, z_, yl_, core_):
        return ref.at[rows_at((z_ * 4 + yl_ * 2 + core_) * ROWS, ROWS), :]

    def project(weight, loaded, stage, extra=None, scale=None):
        for copy in loaded:
            copy.wait()

        def step(n, carry):
            cols = lanes(n * 256, 256)
            part = dot(normed[...], weight[:, cols])
            if extra is not None:
                part = (part + dot(extra, upb[:, cols]) * out_scale) * scale
            stage[:, cols] = part.astype(BF16)
            return carry

        lax.fori_loop(0, 3, step, 0)

    store = (keys, values)

    def core_index(plane, pair, kv):
        return R_CORE + plane * 4 + pair * 2 + kv

    def to_core(plane, pair, kv):
        z_ = (z + plane) % 4
        yl_ = yl if pair == 0 else 1 - yl
        send(block(store[kv], z_, yl_, core), block(store[kv], z_, yl_, core), core_index(plane, pair, kv), other_core)

    def from_core(plane, pairs=(0, 1)):
        z_ = (z + plane) % 4
        for pair in pairs:
            yl_ = yl if pair == 0 else 1 - yl
            for kv in (0, 1):
                arrive(block(store[kv], z_, yl_, 1 - core), core_index(plane, pair, kv))

    def z_index(pair, kv, above):
        return R_Z + pair * 4 + kv * 2 + above

    def to_z(pair, kv):
        src = block(store[kv], z, yl if pair == 0 else 1 - yl, core)
        send(src, src, z_index(pair, kv, 0), z_up)
        send(src, src, z_index(pair, kv, 1), z_down)

    def from_z(pair, kv, above):
        z_ = (z + 1) % 4 if above else (z + 3) % 4
        src = block(store[kv], z_, yl if pair == 0 else 1 - yl, core)
        arrive(src, z_index(pair, kv, above))
        if kv == 0 and not above:
            send(src, src, R_FAR + pair * 2 + kv, z_up)
        if kv == 1 and above:
            send(src, src, R_FAR + pair * 2 + kv, z_down)
        to_core(1 if above else 3, pair, kv)

    def from_far(pair, kv):
        arrive(block(store[kv], (z + 2) % 4, yl if pair == 0 else 1 - yl, core), R_FAR + pair * 2 + kv)
        to_core(2, pair, kv)

    own_block = rows_at(seq_own, ROWS)
    for kv, (weight, stage) in enumerate(((wk, stage_k), (wv, stage_v))):
        project(weight, load_w[kv], stage)
        send(stage.at[:, OWN : 2 * OWN], block(store[kv], z, yl, core), R_PAIR + kv, partner)
        store[kv][own_block, :] = stage[:, 0:OWN]
        to_z(0, kv)
        to_core(0, 0, kv)
        if kv == 0:
            load_w.append(load_weight(wq_hbm, wk))
    own_rows = rows_at(yl * ROWS, ROWS)
    pair_rows = rows_at((1 - yl) * ROWS, ROWS)
    for copy in load_adapter:
        copy.wait()
    downb[...] = down_ref[...].astype(BF16)
    upb[:, 0:OWN] = up_ref[:, own_cols].astype(BF16)
    upb[:, OWN : 2 * OWN] = up_ref[:, other_cols].astype(BF16)
    low_own = (dot(normed[...], downb[...]) * input_scale).astype(BF16)
    low[own_rows, :] = low_own
    project(wk, load_w[2], stage_q, low_own, query_scale)
    send(stage_q.at[:, OWN : 2 * OWN], queries.at[own_rows, :], R_PAIR + 2, partner)
    queries[own_rows, :] = stage_q[:, 0:OWN]
    send(low.at[own_rows, :], low.at[own_rows, :], R_PAIR + 3, partner)
    for kv in (0, 1):
        arrive(block(store[kv], z, 1 - yl, core), R_PAIR + kv)
        to_z(1, kv)
        to_core(0, 1, kv)

    def key_bias(start, width):
        return jnp.where(start + iota((1, width), 1) < length, 0.0, masked_score)

    def forward_part(plane, slot, offset, width):
        start = ((z + plane) % 4) * PLANE + offset
        plane_rows = rows_at(start, width, width)
        bias = key_bias(start, width)
        first = plane == 0
        tiles = [(h, slice(h * HD, (h + 1) * HD), slice(b * ROWS, (b + 1) * ROWS)) for h in range(3) for b in (0, 1)]

        def score(tile):
            _, cols, rows = tile
            return dot_nt(queries[rows, cols], keys[plane_rows, cols]) + bias

        def softmax(tile, scores):
            head, cols, rows = tile
            peak = jnp.max(fold_lanes(jnp.maximum, scores), axis=1, keepdims=True)
            peak = jnp.broadcast_to(peak, (ROWS, 128))
            if not first:
                before = top[head, rows, :]
                peak = jnp.maximum(peak, before)
            exp_scores = jnp.exp2(scores - repeat(peak, width // 128))
            sums = fold_lanes(jnp.add, exp_scores)
            kept = exp_scores.astype(BF16)
            probs[plane, head, rows, lanes(offset, width)] = kept
            weighted = dot(kept, values[plane_rows, cols])
            if not first:
                decay = jnp.exp2(before - peak)
                sums += decay * total[head, rows, :]
                weighted += decay * acc[rows, cols]
            top[head, rows, :] = peak
            peaks[slot, head, rows, :] = peak
            total[head, rows, :] = sums
            acc[rows, cols] = weighted

        scores = score(tiles[0])
        for i, tile in enumerate(tiles):
            ahead = score(tiles[i + 1]) if i + 1 < len(tiles) else None
            softmax(tile, scores)
            scores = ahead

    for kv in (0, 1):
        for above in (0, 1):
            from_z(0, kv, above)
    arrive(queries.at[pair_rows, :], R_PAIR + 2)
    from_core(0)
    forward_part(0, 0, 0, PLANE)
    for kv in (0, 1):
        for above in (0, 1):
            from_z(1, kv, above)
    from_core(1)
    forward_part(1, 1, 0, PLANE)
    from_far(0, 0)
    from_far(0, 1)
    from_core(3)
    forward_part(3, 3, 0, PLANE)
    from_core(2, (0,))
    forward_part(2, 2, yl * 512, 512)
    from_far(1, 0)
    from_far(1, 1)
    from_core(2, (1,))
    forward_part(2, 4, (1 - yl) * 512, 512)

    for head in range(3):
        cols = slice(head * HD, (head + 1) * HD)
        sums = jnp.broadcast_to(jnp.sum(total[head], axis=1, keepdims=True), (2 * ROWS, 128))
        attn[:, cols] = (acc[:, cols] / sums).astype(BF16)
        top[head] = top[head] + jnp.log(sums) * math.log2(math.e)

    blank = jnp.zeros((PATCH, OWN), BF16)
    wide = [jnp.concatenate([wout_ref[...], blank], axis=0), jnp.concatenate([blank, wout_ref[...]], axis=0)]
    partial = dot_nt(attn[0:ROWS, :], wide[0]) + dot_nt(attn[ROWS : 2 * ROWS, :], wide[1])
    vel[y] = partial.astype(BF16)
    for d in (2, 1, 3):
        send(vel.at[y], vel.at[y], R_VEL + d - 1, y_peer(d)[1])
    arrive(latents.at[1 - yl], R_PAIR + 4)
    arrive(low.at[pair_rows, :], R_PAIR + 3)
    moved = jnp.zeros((ROWS, 128), F32)
    for b in (0, 1):
        moved += dot(token_rows(latents[b, 1]), fold(PATCH * b, 128))
        moved -= dot(token_rows(latents[b, 0]), fold(PATCH * b, 128))
    lane_block = iota((ROWS, 128), 1) >> 6
    position = (z * 4 + lane_block * 2 + core) * ROWS + iota((ROWS, 128), 0)
    live = position < length
    for d in (1, 2, 3):
        arrive(vel.at[(y + 4 - d) % 4], R_VEL + d - 1)
    velocity = jnp.zeros((ROWS, 128), F32)
    for b in range(4):
        velocity += vel[b].astype(F32)
    zscore = (moved + step_size * velocity) / spread
    own_squares = jnp.where(live, zscore * zscore, 0.0)
    squares[z] = jnp.sum(own_squares.reshape(ROWS // 8, 8, 128), axis=0)
    for d in (1, 2, 3):
        send(squares.at[z], squares.at[z], R_SQ + d - 1, at(sec, x, (z + d) % 4, yl, core))

    grad_vel = jnp.where(live, -zscore * step_size / (spread * count), 0.0).astype(BF16)
    for b in (0, 1):
        gout[b * ROWS : (b + 1) * ROWS, :] = dot(grad_vel, wide[b]).astype(BF16)

    for head in range(3):
        cols = slice(head * HD, (head + 1) * HD)
        delta = jnp.sum(gout[:, cols].astype(F32) * attn[:, cols].astype(F32), axis=1, keepdims=True)
        total[head] = jnp.broadcast_to(delta, (2 * ROWS, 128))
    acc[...] = jnp.zeros_like(acc)

    def backward_plane(plane, carry):
        plane_rows = rows_at(((z + plane) % 4) * PLANE, PLANE, PLANE)
        slots = [jnp.where((plane == 2) & (yl == 1 - b), 4, plane) for b in (0, 1)]

        def product(head):
            cols = slice(head * HD, (head + 1) * HD)
            return dot_nt(gout[:, cols], values[plane_rows, cols])

        def gradient(head, grad_probs):
            cols = slice(head * HD, (head + 1) * HD)
            scale = jnp.concatenate(
                [repeat(jnp.exp2(peaks[slot, head] - top[head]), 4) for slot in slots], axis=1
            )
            grad_scores = (grad_probs - repeat(total[head], PLANE // 128)) * scale
            grad_scores = (probs[plane, head].astype(F32) * grad_scores).astype(BF16)
            acc[:, cols] += dot(grad_scores, keys[plane_rows, cols])

        made = product(0)
        for head in range(3):
            ahead = product(head + 1) if head < 2 else None
            gradient(head, made)
            made = ahead
        return carry

    lax.fori_loop(0, 2, backward_plane, 0)
    for d in (1, 2, 3):
        arrive(squares.at[(z + 4 - d) % 4], R_SQ + d - 1)
    plane_squares = jnp.zeros((8, 128), F32)
    for b in range(4):
        plane_squares += squares[b]
    both[core] = plane_squares
    send(both.at[core], both.at[core], R_SQ + 3, other_core)
    lax.fori_loop(2, 4, backward_plane, 0)

    batch = rewards_ref.shape[1]
    reward = rewards_ref[...].astype(F32)
    group = groups_ref[...].astype(F32)
    mine = iota((1, batch), 1) == x
    own_group = jnp.sum(jnp.where(mine, group, 0.0), axis=1, keepdims=True)
    own_reward = jnp.sum(jnp.where(mine, reward, 0.0), axis=1, keepdims=True)
    member = jnp.where(group == own_group, 1.0, 0.0)
    mean = jnp.sum(member * reward, axis=1, keepdims=True) / GROUP
    centered = reward - mean
    variance = jnp.sum(member * centered * centered, axis=1, keepdims=True) / GROUP
    advantage = (own_reward - mean) / (jnp.sqrt(variance) + 1.0)

    arrive(both.at[1 - core], R_SQ + 3)
    clip_squares = both[0] + both[1]
    clip_squares = jnp.sum(jnp.sum(clip_squares, axis=1, keepdims=True), axis=0, keepdims=True)
    ratio = jnp.exp(-0.5 * clip_squares / count - one * rollout_ref[x])
    out_ratio[0] = jnp.sum(ratio)
    low_edge, high_edge = 1.0 - clip_range, 1.0 + clip_range
    inside = (ratio >= low_edge) & (ratio <= high_edge)
    active = inside | ((advantage > 0) & (ratio < low_edge)) | ((advantage < 0) & (ratio > high_edge))
    weight = jnp.where(active, -advantage * ratio / float(CLIPS), 0.0)

    gq[...] = (acc[...] * (head_scale * weight)).astype(BF16)

    for near, steps in ((0, (2,)), (1, (1, 3))):
        b = (yl + near) % 2
        part = dot_nt(gq[rows_at(b * ROWS, ROWS), :], upb[:, 0:OWN]) * out_scale
        glow_send[b] = part.astype(BF16)
        for d in steps:
            send(glow_send.at[b], glow.at[y], R_LOW + d - 1, y_peer(d)[1])
    glow[y] = glow_send[yl]
    up_part = dot(jnp.transpose(low[...].astype(F32)).astype(BF16), gq[...])
    du[0, :, 768:1024] = up_part[:, 0:256]
    du[1, :, 768:896] = up_part[:, 256:384]
    du[1, :, 896:1024] = jnp.zeros((128, 128), F32)
    for d in (1, 2, 3):
        arrive(glow.at[(y + 4 - d) % 4], R_LOW + d - 1)
    low_sum = jnp.zeros((ROWS, 128), F32)
    for b in range(4):
        low_sum += glow[b].astype(F32)
    low_turned = jnp.transpose(low_sum).astype(BF16)

    for half in (1, 0):
        where = (core + half) % 2
        for j in range(3):
            cols = lanes(sec * HALF + where * 768 + j * 256, 256)
            du[where, :, j * 256 : (j + 1) * 256] = dot(low_turned, normed[:, cols])
        if half == 1:
            core_send[...] = du[where].astype(BF16)
            send(core_send, core_recv, R_RC, other_core)
    arrive(core_recv, R_RC)
    summed = du[core] + core_recv[...].astype(F32)
    du[core] = summed
    xs[...] = summed.astype(BF16)

    spots = (x, z)

    def along(half, step):
        if half == 0:
            other = (x + step) % 4
            return other, at(sec, other, z, yl, core)
        other = (z + step) % 4
        return other, at(sec, x, other, yl, core)

    def slab(index):
        return rows_at(index * 32, 32, 32)

    def piece_cols(index):
        return lanes(index * 128, 128)

    for d in (2, 1, 3):
        for half in (0, 1):
            other, device = along(half, d)
            send(xs.at[slab(other), half * 512 : (half + 1) * 512], xr.at[half, d - 1], R_S1 + half * 3 + d - 1, device)
    for half in (0, 1):
        part = du[core, slab(spots[half]), half * 512 : (half + 1) * 512]
        for d in (1, 2, 3):
            arrive(xr.at[half, d - 1], R_S1 + half * 3 + d - 1)
            part += xr[half, d - 1].astype(F32)
        slabs[half] = part
        slabs_send[half] = part.astype(BF16)
        for d in (2, 1, 3):
            other, device = along(1 - half, d)
            send(slabs_send.at[half, :, piece_cols(other)], zr.at[half, d - 1], R_S2 + half * 3 + d - 1, device)
    for half in (0, 1):
        part = slabs[half, :, piece_cols(spots[1 - half])]
        for d in (1, 2, 3):
            arrive(zr.at[half, d - 1], R_S2 + half * 3 + d - 1)
            part += zr[half, d - 1].astype(F32)
        yr[y, half] = part.astype(BF16)
    for d in (2, 1, 3):
        send(yr.at[y], yr.at[y], R_RY + d - 1, y_peer(d)[1])
    for d in (1, 2, 3):
        arrive(yr.at[(y + 4 - d) % 4], R_RY + d - 1)
    for b in (0, 1):
        sums = yr[2 * b].astype(F32) + yr[2 * b + 1].astype(F32)
        full[core, 0, b, slab(x), piece_cols(z)] = sums[0].astype(BF16)
        full[core, 1, b, slab(z), piece_cols(x)] = jnp.where(x < 2, sums[1], yr[sec * 2 + b, 1].astype(F32)).astype(BF16)

    for d in (2, 1, 3):
        for half in (0, 1):
            mine_ = full.at[core, half, :, slab(spots[half]), piece_cols(spots[1 - half])]
            send(mine_, mine_, R_G1 + half * 3 + d - 1, along(1 - half, d)[1])
    for half in (0, 1):
        for d in (1, 2, 3):
            source = along(1 - half, 4 - d)[0]
            arrive(full.at[core, half, :, slab(spots[half]), piece_cols(source)], R_G1 + half * 3 + d - 1)
        mine_ = full.at[core, half, :, slab(spots[half]), :]
        for d in (2, 1, 3):
            send(mine_, mine_, R_G2 + half * 3 + d - 1, along(half, d)[1])
        send(mine_, mine_, R_GC + half * 4, other_core)
    for d in (1, 3, 2):
        for half in (0, 1):
            source = slab(along(half, 4 - d)[0])
            theirs = full.at[core, half, :, source, :]
            arrive(theirs, R_G2 + half * 3 + d - 1)
            send(theirs, theirs, R_GC + half * 4 + d, other_core)
    handed = [load(full.at[core], out_grad.at[core])]
    for d in (0, 1, 2, 3):
        for half in (0, 1):
            arrive(full.at[1 - core, half, :, slab(along(half, 4 - d)[0]), :], R_GC + half * 4 + d)
    handed.append(load(full.at[1 - core], out_grad.at[1 - core]))

    for copy in handed:
        copy.wait()
    for copy in pending:
        copy.wait_send()


def update(grad_ref, down_ref, up_ref, ratio_ref, out_hbm, out_up, out_ratio, out_down, out_sem):
    norm_sum = jnp.zeros((128, 256), F32)
    for core in (0, 1):
        for half, width in ((0, 512), (1, 256)):
            for sec in (0, 1):
                for j in range(width // 256):
                    part = grad_ref[core, half, sec, :, j * 256 : (j + 1) * 256].astype(F32)
                    norm_sum += part * part
    norm_sum = jnp.sum(jnp.sum(norm_sum, axis=1, keepdims=True), axis=0, keepdims=True)
    factor = step_length / jnp.sqrt(norm_sum * (input_scale * input_scale) + norm_eps)
    down_factor, up_factor = factor * input_scale, factor * out_scale
    written = []
    for t in range(MODEL_WIDTH // 128):
        sec, core, j = t // 12, (t % 12) // 6, t % 6
        half, start = j // 4, (j % 4) * 128
        part = grad_ref[core, half, sec, :, start : start + 128].astype(F32)
        rows = slice(t * 128, (t + 1) * 128)
        out_down[rows, :] = down_ref[rows, :] - down_factor * jnp.transpose(part)
        if t % 6 == 5:
            rows = slice((t - 5) * 128, (t + 1) * 128)
            written.append(pltpu.make_async_copy(out_down.at[rows, :], out_hbm.at[rows, :], out_sem.at[t // 6]))
            written[-1].start()
    for b in (0, 1):
        for core, width in ((0, 256), (1, 128)):
            cols = slice(b * OWN + core * 256, b * OWN + core * 256 + width)
            part = grad_ref[core, 1, b, :, 256 : 256 + width].astype(F32)
            out_up[:, cols] = up_ref[:, cols] - up_factor * part
    out_ratio[0] = ratio_ref[0]
    for copy in written:
        copy.wait()


def shards(
    trajectory, block_input, chosen, lengths, rewards, prompt_group_index, rollout_log_probability,
    timestep_norm_shift, patch_input_weight, frozen_query_matrix, frozen_key_matrix, frozen_value_matrix,
    velocity_output_weight, adapter_down_factor, adapter_up_factor,
):
    vmem = pl.BlockSpec(memory_space=pltpu.VMEM)
    smem = pl.BlockSpec(memory_space=pltpu.SMEM)
    hbm = pl.BlockSpec(memory_space=pl.ANY)
    V = pltpu.VMEM
    scratch = [
        V((STEPS, 2, MODEL_WIDTH), F32),
        V((PATCH, MODEL_WIDTH), BF16),
        V((PATCH, OWN), BF16),
        V((MODEL_WIDTH, ADAPTER_RANK), F32),
        V((ADAPTER_RANK, 2 * OWN), F32),
        V((ROWS, MODEL_WIDTH), BF16),
        V((MODEL_WIDTH, 2 * OWN), BF16),
        V((MODEL_WIDTH, 2 * OWN), BF16),
        V((MODEL_WIDTH, ADAPTER_RANK), BF16),
        V((ADAPTER_RANK, 2 * OWN), BF16),
        V((ROWS, MODEL_WIDTH), F32),
        V((ROWS, MODEL_WIDTH), BF16),
        V((CLIPS, 2, PAIRS, 128), BF16),
        V((2, 2, 128, 128), BF16),
        V((ROWS, 2 * OWN), BF16),
        V((ROWS, 2 * OWN), BF16),
        V((ROWS, 2 * OWN), BF16),
        V((4 * PLANE, OWN), BF16),
        V((4 * PLANE, OWN), BF16),
        V((2 * ROWS, OWN), BF16),
        V((2 * ROWS, ADAPTER_RANK), BF16),
        V((3, 2 * ROWS, 128), F32),
        V((5, 3, 2 * ROWS, 128), F32),
        V((4, 3, 2 * ROWS, PLANE), BF16),
        V((3, 2 * ROWS, 128), F32),
        V((2 * ROWS, OWN), F32),
        V((2 * ROWS, OWN), BF16),
        V((4, ROWS, 128), BF16),
        V((4, 8, 128), F32),
        V((2, 8, 128), F32),
        V((2 * ROWS, OWN), BF16),
        V((2 * ROWS, OWN), BF16),
        V((2, ROWS, 128), BF16),
        V((4, ROWS, 128), BF16),
        V((2, 128, 1024), F32),
        V((128, 1024), BF16),
        V((128, 1024), BF16),
        V((128, 1024), BF16),
        V((2, 3, 32, 512), BF16),
        V((2, 32, 512), F32),
        V((2, 32, 512), BF16),
        V((2, 3, 32, 128), BF16),
        V((4, 2, 32, 128), BF16),
        V((2, 2, 2, 128, 512), BF16),
        pltpu.SemaphoreType.DMA((N_SEND,)),
        pltpu.SemaphoreType.DMA((N_RECV,)),
        pltpu.SemaphoreType.DMA((16,)),
    ]
    gradients, ratio = pl.pallas_call(
        body,
        out_shape=(
            jax.ShapeDtypeStruct((2, 2, 2, ADAPTER_RANK, 512), BF16),
            jax.ShapeDtypeStruct((1,), F32),
        ),
        in_specs=[smem] * 3 + [vmem] * 3 + [hbm] * 9,
        out_specs=(hbm, smem),
        scratch_shapes=scratch,
        compiler_params=pltpu.CompilerParams(
            collective_id=0, has_side_effects=True, vmem_limit_bytes=60 * 1024 * 1024
        ),
        cost_estimate=pl.CostEstimate(flops=12_000_000_000, bytes_accessed=24_000_000, transcendentals=13_000_000),
        name="policy_step",
    )(
        chosen, lengths, rollout_log_probability,
        trajectory.reshape(STEPS + 1, CLIPS, PAIRS, 128),
        rewards.reshape(1, -1), prompt_group_index.reshape(1, -1), timestep_norm_shift, patch_input_weight,
        velocity_output_weight.T, adapter_down_factor, adapter_up_factor,
        block_input.reshape(ROWS, MODEL_WIDTH), frozen_query_matrix, frozen_key_matrix, frozen_value_matrix,
    )
    return pl.pallas_call(
        update,
        out_shape=(
            jax.ShapeDtypeStruct((MODEL_WIDTH, ADAPTER_RANK), F32),
            jax.ShapeDtypeStruct((ADAPTER_RANK, 2 * OWN), F32),
            jax.ShapeDtypeStruct((1,), F32),
        ),
        in_specs=[vmem] * 3 + [smem],
        out_specs=(hbm, vmem, smem),
        scratch_shapes=[
            V((MODEL_WIDTH, ADAPTER_RANK), F32),
            pltpu.SemaphoreType.DMA((4,)),
        ],
        compiler_params=pltpu.CompilerParams(vmem_limit_bytes=32 * 1024 * 1024),
        name="update",
    )(gradients, adapter_down_factor, adapter_up_factor, ratio)


def solution(mesh):
    return jax.shard_map(
        shards,
        mesh=mesh,
        in_specs=(
            P(None, None, "seq", "dp", None),
            P("dp", "seq", None),
            P(), P(), P(), P(), P(), P(), P(),
            P(None, "section"),
            P(None, "section"),
            P(None, "section"),
            P("section", None),
            P(),
            P(None, "section"),
        ),
        out_specs=(P(), P(None, "section"), P("dp")),
        check_vma=False,
    )
```
